32 devices in a mesh: dp: 4 (over y, core), seq: 8 (over z, x).
Axes of the slice: x: 2, y: 2, z: 4, core: 2. Of those that a mesh axis runs over, the one named last changes fastest.
Arguments:
- activations: bfloat16 [8, 512, 1536], P('dp', 'seq'), may hold values from -6 to 6
- cotangent: bfloat16 [8, 512, 1536], P('dp', 'seq'), may hold values from -6 to 6
- carried_state: float32 [8, 16, 3072], P('dp'), may hold values from -6 to 6
- carried_kv: bfloat16 [8, 2048, 3072], P('dp', 'seq'), may hold values from -6 to 6
- row_lengths: int32 [8], P('dp'), may hold values from 32 to 512, as said below
- mamba_gain: bfloat16 [1536], P(('dp', 'seq')), may hold values from 0.25 to 1.75
- mamba_in: bfloat16 [1536, 6144], P(('dp', 'seq')), may hold values from -0.15625 to 0.15625
- conv_weight: bfloat16 [4, 3072], P(None, ('dp', 'seq')), may hold values from -3 to 3
- conv_bias: bfloat16 [3072], P(('dp', 'seq')), may hold values from -3 to 3
- selection: bfloat16 [3072, 128], P(('dp', 'seq')), may hold values from -0.109375 to 0.109375
- step_proj: bfloat16 [96, 3072], P(None, ('dp', 'seq')), may hold values from -0.625 to 0.625
- step_bias: float32 [3072], P(('dp', 'seq')), may hold values from -11 to -3
- decay_log: float32 [16, 3072], P(None, ('dp', 'seq')), may hold values from 0 to 2.7
- skip_gain: float32 [3072], P(('dp', 'seq')), may hold values from 0.5 to 1.5
- mamba_out: bfloat16 [3072, 1536], P(('dp', 'seq')), may hold values from -0.109375 to 0.109375
- first_gain: bfloat16 [1536], P(('dp', 'seq')), may hold values from 0.25 to 1.75
- first_gate_up: bfloat16 [1536, 8192], P(('dp', 'seq')), may hold values from -0.15625 to 0.15625
- first_down: bfloat16 [4096, 1536], P(('dp', 'seq')), may hold values from -0.09375 to 0.09375
- attention_gain: bfloat16 [1536], P(('dp', 'seq')), may hold values from 0.25 to 1.75
- attention_qkv: bfloat16 [1536, 4608], P(('dp', 'seq')), may hold values from -0.15625 to 0.15625
- attention_out: bfloat16 [1536, 1536], P(('dp', 'seq')), may hold values from -0.625 to 0.625
- second_gain: bfloat16 [1536], P(('dp', 'seq')), may hold values from 0.25 to 1.75
- second_gate_up: bfloat16 [1536, 8192], P(('dp', 'seq')), may hold values from -0.15625 to 0.15625
- second_down: bfloat16 [4096, 1536], P(('dp', 'seq')), may hold values from -0.09375 to 0.09375
Outputs:
- output: bfloat16 [8, 512, 1536], P('dp', 'seq')
- new_state: float32 [8, 16, 3072], P('dp', None, 'seq')
- segment_kv: bfloat16 [8, 512, 3072], P('dp', 'seq')
- grad_input: float32 [8, 512, 1536], P('dp', 'seq')
- grad_state: float32 [8, 16, 3072], P('dp', None, 'seq')
- grad_cache: float32 [8, 2048, 3072], P('dp', 'seq')
- mamba_gain_grad: float32 [1536], P(('dp', 'seq'))
- mamba_in_grad: float32 [1536, 6144], P(('dp', 'seq'))
- conv_weight_grad: float32 [4, 3072], P(None, ('dp', 'seq'))
- conv_bias_grad: float32 [3072], P(('dp', 'seq'))
- selection_grad: float32 [3072, 128], P(('dp', 'seq'))
- step_proj_grad: float32 [96, 3072], P(None, ('dp', 'seq'))
- step_bias_grad: float32 [3072], P(('dp', 'seq'))
- decay_log_grad: float32 [16, 3072], P(None, ('dp', 'seq'))
- skip_gain_grad: float32 [3072], P(('dp', 'seq'))
- mamba_out_grad: float32 [3072, 1536], P(('dp', 'seq'))
- first_gain_grad: float32 [1536], P(('dp', 'seq'))
- first_gate_up_grad: float32 [1536, 8192], P(('dp', 'seq'))
- first_down_grad: float32 [4096, 1536], P(('dp', 'seq'))
- attention_gain_grad: float32 [1536], P(('dp', 'seq'))
- attention_qkv_grad: float32 [1536, 4608], P(('dp', 'seq'))
- attention_out_grad: float32 [1536, 1536], P(('dp', 'seq'))
- second_gain_grad: float32 [1536], P(('dp', 'seq'))
- second_gate_up_grad: float32 [1536, 8192], P(('dp', 'seq'))
- second_down_grad: float32 [4096, 1536], P(('dp', 'seq'))
The draws below stay inside these ranges and needn't reach their ends.
Inputs may be any that keep to these rules, and one draw needn't show every extreme that they name: `row_lengths`: in each aligned block of 2 rows (the rows of one index of dp), one row drawn from the seed holds 512 real tokens.
All inputs are finite; a program needn't handle non-finite values.
Results may differ from the reference program's by a relative error of at most 0.04.
Values may be sent and summed in bfloat16 or wider, within the bound.
No kernel may reach another device: no remote copies, remote signals or barrier semaphores. Data moves between devices by JAX's collectives and lax.ppermute only.
A program may use at most 640 MiB of HBM per device.

```python
import jax
import jax.numpy as jnp
from jax import lax

D = 1536
HEADS = 12
HEAD_DIM = 128
INNER = 3072
STATE = 16
CONV = 4
DT_RANK = 96
FF = 4096
WINDOW = 2048
ROWS_DEV = 2
GROUP = 64
SEQ_LEN = 512
ROWS = 8
N_SEQ = 8


def draw_row_lengths(key, part):
    key_shift, key_value, key_pick = jax.random.split(key, 3)
    shift = jax.random.randint(key_shift, (ROWS,), 0, 4)
    upper = jnp.right_shift(jnp.full((ROWS,), SEQ_LEN, jnp.int32), shift)
    lower = upper // 2
    value = lower + jax.random.randint(key_value, (ROWS,), 0, SEQ_LEN) % (upper - lower + 1)
    pick = jax.random.randint(key_pick, (ROWS // ROWS_DEV,), 0, ROWS_DEV)
    full = jnp.arange(ROWS) % ROWS_DEV == jnp.repeat(pick, ROWS_DEV, total_repeat_length=ROWS)
    return jnp.where(full, SEQ_LEN, value).astype(jnp.int32)


def draw_step_bias(key, part):
    key_pick, key_slow, key_fast = jax.random.split(key, 3)
    share = 0.5
    pick = jax.random.uniform(key_pick, (INNER,), jnp.float32)
    slow_value = jax.random.uniform(key_slow, (INNER,), jnp.float32, -11.0, -9.5)
    fast_value = jax.random.uniform(key_fast, (INNER,), jnp.float32, -4.5, -3.0)
    return jnp.where(pick < share, slow_value, fast_value)


def steps_of(stream_key, dims, shards, least, high):
    def one(dim, blocks):
        heights = jax.random.uniform(jax.random.fold_in(jax.random.fold_in(stream_key, 6), dim), (blocks,), jnp.float32, least / len(shards), high / len(shards))
        return jnp.repeat(jnp.exp(heights), dims[dim] // blocks).reshape((-1,) + (1,) * (len(dims) - dim - 1))

    factor_of = one(*shards[0])
    for cut in shards[1:]:
        factor_of = factor_of * one(*cut)
    return factor_of


def centred(stream_key, extent, spread, limit, cuts=(), kind=jnp.bfloat16):
    level = steps_of(stream_key, extent, cuts, -0.22, 0.18) if cuts else 1.0
    values = jax.random.normal(stream_key, extent, jnp.float32) * spread * level
    return jnp.minimum(jnp.maximum(values, -limit), limit).astype(kind)


def setup_inputs(seed: int = 0) -> dict:
    arg_keys = jax.random.split(jax.random.key(seed), 25)
    return {
        "activations": centred(arg_keys[0], (ROWS, SEQ_LEN, D), 1.0, 6.0, ((0, 4), (1, 8))),
        "cotangent": centred(arg_keys[1], (ROWS, SEQ_LEN, D), 1.0, 6.0, ((0, 4), (1, 8))),
        "carried_state": centred(arg_keys[2], (ROWS, STATE, INNER), 1.0, 6.0, ((0, 4),), jnp.float32),
        "carried_kv": centred(arg_keys[3], (ROWS, WINDOW, 2 * D), 1.0, 6.0, ((0, 4), (1, 8))),
        "row_lengths": draw_row_lengths(jax.random.fold_in(arg_keys[24], 71), 0),
        "mamba_gain": jnp.clip(1.0 + 0.15 * jax.random.normal(arg_keys[5], (D,), jnp.float32), 0.25, 1.75).astype(jnp.bfloat16),
        "mamba_in": centred(arg_keys[6], (D, 2 * INNER), D ** -0.5, 0.15625, ((0, 32),)),
        "conv_weight": centred(arg_keys[7], (CONV, INNER), CONV ** -0.5, 3.0, ((1, 32),)),
        "conv_bias": centred(arg_keys[8], (INNER,), 0.5, 3.0, ((0, 32),)),
        "selection": centred(arg_keys[9], (INNER, DT_RANK + 2 * STATE), INNER ** -0.5, 0.109375, ((0, 32),)),
        "step_proj": centred(arg_keys[10], (DT_RANK, INNER), DT_RANK ** -0.5, 0.625, ((1, 32),)),
        "step_bias": draw_step_bias(jax.random.fold_in(arg_keys[24], 71), 0),
        "decay_log": jnp.clip(2.7 * jax.random.uniform(arg_keys[12], (STATE, INNER), jnp.float32) ** steps_of(arg_keys[12], (STATE, INNER), ((1, 32),), -0.2, 0.2), 0.0, 2.7),
        "skip_gain": jnp.clip(0.5 + 1.0 * jax.random.uniform(arg_keys[13], (INNER,), jnp.float32) ** steps_of(arg_keys[13], (INNER,), ((0, 32),), -0.2, 0.2), 0.5, 1.5),
        "mamba_out": centred(arg_keys[14], (INNER, D), INNER ** -0.5, 0.109375, ((0, 32),)),
        "first_gain": jnp.clip(1.0 + 0.15 * jax.random.normal(arg_keys[15], (D,), jnp.float32), 0.25, 1.75).astype(jnp.bfloat16),
        "first_gate_up": centred(arg_keys[16], (D, 2 * FF), D ** -0.5, 0.15625, ((0, 32),)),
        "first_down": centred(arg_keys[17], (FF, D), FF ** -0.5, 0.09375, ((0, 32),)),
        "attention_gain": jnp.clip(1.0 + 0.15 * jax.random.normal(arg_keys[18], (D,), jnp.float32), 0.25, 1.75).astype(jnp.bfloat16),
        "attention_qkv": centred(arg_keys[19], (D, 3 * D), D ** -0.5, 0.15625, ((0, 32),)),
        "attention_out": centred(arg_keys[20], (D, D), (max(D // 16, 1)) ** -0.5, 0.625, ((0, 32),)),
        "second_gain": jnp.clip(1.0 + 0.15 * jax.random.normal(arg_keys[21], (D,), jnp.float32), 0.25, 1.75).astype(jnp.bfloat16),
        "second_gate_up": centred(arg_keys[22], (D, 2 * FF), D ** -0.5, 0.15625, ((0, 32),)),
        "second_down": centred(arg_keys[23], (FF, D), FF ** -0.5, 0.09375, ((0, 32),)),
    }


@jax.custom_vjp
def low(v):
    return lax.optimization_barrier(v.astype(jnp.bfloat16)).astype(jnp.float32)

@jax.custom_vjp
def low_back(v):
    return v

def low_keep(v):
    return (low(v), None)

def low_pass(kept, grad):
    return (grad,)

def back_keep(v):
    return (v, None)

def back_low(kept, grad):
    return (low(grad),)
low.defvjp(low_keep, low_pass)
low_back.defvjp(back_keep, back_low)
EPSILON = 1e-05
NEGATIVE = -1e+30
HIGHEST = lax.Precision.HIGHEST

def matmul(left, right):
    return jnp.dot(left, right, precision=HIGHEST, preferred_element_type=jnp.float32)

def rms_gain(values, gain):
    return values * lax.rsqrt(lax.optimization_barrier(jnp.mean(values * values, axis=-1, keepdims=True)) + EPSILON) * gain

def feed_forward(values, gain, gate_up, down):
    normed = low(rms_gain(values, gain))
    both = low_back(matmul(normed, gate_up))
    hidden = low(jax.nn.silu(both[..., :FF]) * both[..., FF:])
    return values + low_back(matmul(hidden, down))

def recurrence(decay):

    def advance(carry, slot):
        mixed_now, step_now, input_now, output_now = slot
        carry = jnp.exp(step_now[:, None, :] * decay) * carry + (step_now * mixed_now)[:, None, :] * input_now[:, :, None]
        return (carry, lax.optimization_barrier(jnp.sum(output_now[:, :, None] * carry, axis=1)))
    return advance

def selective(mixed, step, inputs_b, outputs_c, decay, state):
    rows = mixed.shape[0]

    def block(carry, slots):
        current, rate = carry
        current, core = lax.scan(recurrence(rate), current, slots)
        return ((current, rate), core)

    def blocks(values):
        return jnp.transpose(values.reshape(rows, N_SEQ, GROUP, values.shape[-1]), (1, 2, 0, 3))
    (state_end, rate_end), core = lax.scan(jax.checkpoint(block), (state, decay), tuple((blocks(item) for item in (mixed, step, inputs_b, outputs_c))))
    return (jnp.transpose(core, (2, 0, 1, 3)).reshape(rows, SEQ_LEN, INNER), state_end)

def mamba(values, valid, state, gain, mamba_in, conv_weight, conv_bias, selection, step_proj, step_bias, decay_log, skip_gain, mamba_out):
    normed = low(rms_gain(values, gain))
    projected = low_back(matmul(normed, mamba_in))
    inner = projected[..., :INNER]
    gate = projected[..., INNER:]
    padded = jnp.pad(inner, ((0, 0), (CONV - 1, 0), (0, 0)))
    total = conv_bias
    for index in range(CONV):
        total = total + conv_weight[index] * padded[:, index:index + SEQ_LEN]
    mixed = jax.nn.silu(total)
    select = low_back(matmul(low(mixed), selection))
    step_low = low(select[..., :DT_RANK])
    inputs_b = select[..., DT_RANK:DT_RANK + STATE]
    outputs_c = select[..., DT_RANK + STATE:]
    step = jax.nn.softplus(low_back(matmul(step_low, step_proj)) + step_bias) * valid[..., None]
    decay = -jnp.exp(decay_log)
    core, state_end = selective(mixed, step, inputs_b, outputs_c, decay, state)
    gated = low((core + skip_gain * mixed) * jax.nn.silu(gate))
    return (values + low_back(matmul(gated, mamba_out)), state_end)

def attend_row(pieces):
    queries, keys, contents, length = pieces
    key_pos = jnp.arange(WINDOW + SEQ_LEN) - WINDOW
    size = min(512, SEQ_LEN)
    scale = HEAD_DIM ** (-0.5)

    def block(args):
        query_block, first = args
        query_pos = first + jnp.arange(size)
        near = (key_pos[None, :] > query_pos[:, None] - WINDOW) & (key_pos[None, :] <= query_pos[:, None])
        real = (key_pos[None, :] < length) | (key_pos[None, :] == query_pos[:, None])
        inside = (near & real)[:, None, :]
        scores = low_back(jnp.einsum('qhd,khd->qhk', query_block, keys, precision=HIGHEST) * scale)
        top = lax.optimization_barrier(jnp.max(jnp.where(inside, scores, NEGATIVE), axis=-1, keepdims=True))
        weights = jnp.exp(jnp.where(inside, scores - top, NEGATIVE))
        weights = weights / lax.optimization_barrier(jnp.sum(weights, axis=-1, keepdims=True))
        return low_back(jnp.einsum('qhk,khd->qhd', low(weights), contents, precision=HIGHEST))
    query_blocks = queries.reshape(SEQ_LEN // size, size, HEADS, HEAD_DIM)
    starts = jnp.arange(SEQ_LEN // size) * size
    result = lax.map(jax.checkpoint(block), (query_blocks, starts))
    return result.reshape(SEQ_LEN, HEADS * HEAD_DIM)

def attention(values, lengths, carried, gain, qkv_proj, out_proj):
    rows = values.shape[0]
    normed = low(rms_gain(values, gain))
    qkv = low(low_back(matmul(normed, qkv_proj)))
    queries = qkv[..., :D].reshape(rows, SEQ_LEN, HEADS, HEAD_DIM)
    keys = jnp.concatenate([carried[..., :D], qkv[..., D:2 * D]], axis=1).reshape(rows, WINDOW + SEQ_LEN, HEADS, HEAD_DIM)
    contents = jnp.concatenate([carried[..., D:], qkv[..., 2 * D:]], axis=1).reshape(rows, WINDOW + SEQ_LEN, HEADS, HEAD_DIM)
    attended = low(lax.map(jax.checkpoint(attend_row), (queries, keys, contents, lengths)))
    return (values + low_back(matmul(attended, out_proj)), qkv[..., D:])

def reference(activations, cotangent, carried_state, carried_kv, row_lengths, mamba_gain, mamba_in, conv_weight, conv_bias, selection, step_proj, step_bias, decay_log, skip_gain, mamba_out, first_gain, first_gate_up, first_down, attention_gain, attention_qkv, attention_out, second_gain, second_gate_up, second_down):
    valid = (jnp.arange(SEQ_LEN)[None, :] < row_lengths[:, None]).astype(jnp.float32)
    weights = tuple((item.astype(jnp.float32) for item in (mamba_gain, mamba_in, conv_weight, conv_bias, selection, step_proj, step_bias, decay_log, skip_gain, mamba_out, first_gain, first_gate_up, first_down, attention_gain, attention_qkv, attention_out, second_gain, second_gate_up, second_down)))

    def forward(stream, state, carried, params):
        first, state_end = mamba(stream, valid, state, *params[:10])
        second = feed_forward(first, *params[10:13])
        third, segment = attention(second, row_lengths, carried, *params[13:16])
        fourth = feed_forward(third, *params[16:19])
        return (fourth, (state_end, segment))
    fourth, backward, aux = jax.vjp(forward, activations.astype(jnp.float32), carried_state, carried_kv.astype(jnp.float32), weights, has_aux=True)
    grad_input, grad_state, grad_cache, grads = backward(cotangent.astype(jnp.float32))
    return (fourth.astype(jnp.bfloat16), aux[0], aux[1].astype(jnp.bfloat16), grad_input, grad_state, grad_cache, grads[0], grads[1], grads[2], grads[3], grads[4], grads[5], grads[6], grads[7], grads[8], grads[9], grads[10], grads[11], grads[12], grads[13], grads[14], grads[15], grads[16], grads[17], grads[18])
```

```python
import jax
import jax.numpy as jnp
from jax import lax
from jax.experimental import pallas as pl
from jax.experimental.pallas import tpu as pltpu
from jax.sharding import Mesh
from jax.sharding import PartitionSpec as P

HEAD_DIM = 128
CONV = 4
WINDOW = 2048


EPSILON = 1e-05
NEGATIVE = -1e30


def shifted(block, axis, distance):
    devices = range(lax.axis_size(axis))
    route = [(i - distance, i) for i in devices if i - distance in devices]
    return lax.ppermute(block, axis, route)


def carried_in(part, axis, combine, identity, reverse):
    count = lax.axis_size(axis)
    place = lax.axis_index(axis)
    ahead = count - 1 - place if reverse else place
    gathered = jax.tree.map(lambda a: lax.all_gather(a, axis), part)
    state = jax.tree.map(lambda a, e: jnp.zeros_like(a) + jnp.asarray(e, a.dtype), part, identity)

    def one(lap, state):
        source = count - 1 - lap if reverse else lap
        return combine(
            state, jax.tree.map(lambda a: lax.dynamic_index_in_dim(a, source, 0, False), gathered)
        )

    return lax.fori_loop(0, ahead, one, state)


def rms_gain(values, gain):
    return values * lax.rsqrt(jnp.mean(values * values, axis=-1, keepdims=True) + EPSILON) * gain


def product(left, right):
    return lax.dot_general(
        left, right, (((left.ndim - 1,), (0,)), ((), ())), preferred_element_type=jnp.float32
    )


def product_back(left, right):
    return lax.dot_general(
        left, right, (((left.ndim - 1,), (1,)), ((), ())), preferred_element_type=jnp.float32
    )


def outer(left, right):
    flat_left = left.reshape(-1, left.shape[-1])
    flat_right = right.reshape(-1, right.shape[-1])
    return lax.dot_general(
        flat_left, flat_right, (((0,), (0,)), ((), ())), preferred_element_type=jnp.float32
    )


def fetch_front(shards):
    return (
        lax.all_gather(shards[0], ("dp", "seq"), axis=0, tiled=True),
        lax.all_gather(shards[1], ("dp", "seq"), axis=0, tiled=True),
        lax.all_gather(shards[2], ("dp", "seq"), axis=1, tiled=True),
        lax.all_gather(shards[3], ("dp", "seq"), axis=0, tiled=True),
        lax.all_gather(shards[4], ("dp", "seq"), axis=0, tiled=True),
        lax.all_gather(shards[5], ("dp", "seq"), axis=1, tiled=True),
        lax.all_gather(shards[6].astype(jnp.bfloat16), ("dp", "seq"), axis=0, tiled=True).astype(
            jnp.float32
        ),
        lax.all_gather(shards[7].astype(jnp.bfloat16), ("dp", "seq"), axis=1, tiled=True).astype(
            jnp.float32
        ),
        lax.all_gather(shards[8].astype(jnp.bfloat16), ("dp", "seq"), axis=0, tiled=True).astype(
            jnp.float32
        ),
        lax.all_gather(shards[9], ("dp", "seq"), axis=0, tiled=True),
        lax.all_gather(shards[10], ("dp", "seq"), axis=0, tiled=True),
        lax.all_gather(shards[11], ("dp", "seq"), axis=0, tiled=True),
        lax.all_gather(shards[12], ("dp", "seq"), axis=0, tiled=True),
    )


def settle_front(grads):
    return (
        lax.psum_scatter(grads[0], ("dp", "seq"), scatter_dimension=0, tiled=True),
        lax.psum_scatter(grads[1], ("dp", "seq"), scatter_dimension=0, tiled=True),
        lax.psum_scatter(grads[2], ("dp", "seq"), scatter_dimension=1, tiled=True),
        lax.psum_scatter(grads[3], ("dp", "seq"), scatter_dimension=0, tiled=True),
        lax.psum_scatter(grads[4], ("dp", "seq"), scatter_dimension=0, tiled=True),
        lax.psum_scatter(grads[5], ("dp", "seq"), scatter_dimension=1, tiled=True),
        lax.psum_scatter(grads[6], ("dp", "seq"), scatter_dimension=0, tiled=True),
        lax.psum_scatter(grads[7], ("dp", "seq"), scatter_dimension=1, tiled=True),
        lax.psum_scatter(grads[8], ("dp", "seq"), scatter_dimension=0, tiled=True),
        lax.psum_scatter(grads[9], ("dp", "seq"), scatter_dimension=0, tiled=True),
        lax.psum_scatter(grads[10], ("dp", "seq"), scatter_dimension=0, tiled=True),
        lax.psum_scatter(grads[11], ("dp", "seq"), scatter_dimension=0, tiled=True),
        lax.psum_scatter(grads[12], ("dp", "seq"), scatter_dimension=0, tiled=True),
    )


def fetch_rear(shards):
    return (
        lax.all_gather(shards[0], ("dp", "seq"), axis=0, tiled=True),
        lax.all_gather(shards[1], ("dp", "seq"), axis=0, tiled=True),
        lax.all_gather(shards[2], ("dp", "seq"), axis=0, tiled=True),
        lax.all_gather(shards[3], ("dp", "seq"), axis=0, tiled=True),
        lax.all_gather(shards[4], ("dp", "seq"), axis=0, tiled=True),
        lax.all_gather(shards[5], ("dp", "seq"), axis=0, tiled=True),
    )


def settle_rear(grads):
    return (
        lax.psum_scatter(grads[0], ("dp", "seq"), scatter_dimension=0, tiled=True),
        lax.psum_scatter(grads[1], ("dp", "seq"), scatter_dimension=0, tiled=True),
        lax.psum_scatter(grads[2], ("dp", "seq"), scatter_dimension=0, tiled=True),
        lax.psum_scatter(grads[3], ("dp", "seq"), scatter_dimension=0, tiled=True),
        lax.psum_scatter(grads[4], ("dp", "seq"), scatter_dimension=0, tiled=True),
        lax.psum_scatter(grads[5], ("dp", "seq"), scatter_dimension=0, tiled=True),
    )


def ffn_forward(values, weights):
    gain, gate_up, down = weights
    width = down.shape[0]
    normed = rms_gain(values, gain.astype(jnp.float32)).astype(jnp.bfloat16)
    both = product(normed, gate_up)
    hidden = (jax.nn.silu(both[..., :width]) * both[..., width:]).astype(jnp.bfloat16)
    return (values + product(hidden, down), (normed, both, hidden))


def ffn_backward(values, grad, weights, kept):
    gain, gate_up, down = weights
    normed, both, hidden = kept
    width = down.shape[0]
    grad_low = grad.astype(jnp.bfloat16)
    grad_down = outer(hidden, grad_low)
    grad_hidden = product_back(grad_low, down)

    def ffn_gating(pair):
        return jax.nn.silu(pair[..., :width]) * pair[..., width:]

    unused, gating_back = jax.vjp(ffn_gating, both)
    grad_both = gating_back(grad_hidden)[0].astype(jnp.bfloat16)
    grad_gate_up = outer(normed, grad_both)
    grad_normed = product_back(grad_both, gate_up)
    unused, norm_back = jax.vjp(rms_gain, values, gain.astype(jnp.float32))
    grad_values, grad_gain = norm_back(grad_normed)
    return (grad + grad_values, (grad_gain, grad_gate_up, grad_down))


def convolve(before, inner, conv_weight, conv_bias):
    group = inner.shape[1]
    padded = jnp.concatenate([before, inner], axis=1)
    total = conv_bias
    for index in range(CONV):
        total = total + conv_weight[index] * padded[:, index : index + group]
    return jax.nn.silu(total)


def recurrence(decay):

    def advance(carry, slot):
        mixed_now, step_now, input_now, output_now = slot
        carry = (
            jnp.exp(step_now[:, None, :] * decay) * carry
            + (step_now * mixed_now)[:, None, :] * input_now[:, :, None]
        )
        return (carry, jnp.sum(output_now[:, :, None] * carry, axis=1))

    return advance


def selective(mixed, step, inputs_b, outputs_c, decay, state):
    slots = tuple((jnp.moveaxis(item, 1, 0) for item in (mixed, step, inputs_b, outputs_c)))
    state_end, core = lax.scan(recurrence(decay), state, slots, unroll=8)
    return (jnp.moveaxis(core, 0, 1), state_end)


def chain(earlier, later):
    return (earlier[0] * later[0], later[0] * earlier[1] + later[1])


def chain_both(earlier, later):
    return (
        earlier[0] * later[0],
        later[0] * earlier[1] + later[1],
        earlier[2] * later[2],
        earlier[2] * later[3] + earlier[3],
    )


def stepping(pre, step_bias, valid):
    return jax.nn.softplus(pre + step_bias) * valid[..., None]


def mamba_forward(values, lengths, carried_state, weights):
    (
        gain,
        mamba_in,
        conv_weight,
        conv_bias,
        selection,
        step_proj,
        step_bias,
        decay_log,
        skip_gain,
        mamba_out,
    ) = weights
    rows, group, width = values.shape
    inner_width = mamba_out.shape[0]
    rank = step_proj.shape[0]
    states = decay_log.shape[0]
    shard = lax.axis_index("seq")
    positions = shard * group + jnp.arange(group)
    valid = (positions[None, :] < lengths[:, None]).astype(jnp.float32)
    normed = rms_gain(values, gain.astype(jnp.float32)).astype(jnp.bfloat16)
    projected = product(normed, mamba_in)
    inner = projected[..., :inner_width]
    gate = projected[..., inner_width:]
    before = shifted(inner[:, group - CONV + 1 :], "seq", 1)
    mixed = convolve(before, inner, conv_weight.astype(jnp.float32), conv_bias.astype(jnp.float32))
    mixed_low = mixed.astype(jnp.bfloat16)
    select = product(mixed_low, selection)
    step_low = select[..., :rank].astype(jnp.bfloat16)
    inputs_b = select[..., rank : rank + states]
    outputs_c = select[..., rank + states :]
    pre = product(step_low, step_proj)
    step = stepping(pre, step_bias.astype(jnp.float32), valid)
    decay = -jnp.exp(decay_log.astype(jnp.float32))
    empty = jnp.zeros((rows, states, inner_width), jnp.float32)
    local_end = selective(mixed, step, inputs_b, outputs_c, decay, empty)[1]
    through = jnp.exp(decay * jnp.sum(step, axis=1)[:, None, :])
    prefix_decay, prefix_state = carried_in(
        (through, local_end), "seq", chain, (jnp.ones_like(through), empty), False
    )
    state = prefix_decay * carried_state + prefix_state
    core, state_end = selective(mixed, step, inputs_b, outputs_c, decay, state)
    mixed_out = core + skip_gain.astype(jnp.float32) * mixed
    gated = (mixed_out * jax.nn.silu(gate)).astype(jnp.bfloat16)
    kept = (
        valid,
        normed,
        projected,
        before,
        mixed,
        mixed_low,
        step_low,
        pre,
        step,
        inputs_b,
        outputs_c,
        decay,
        state,
        through,
        prefix_decay,
        mixed_out,
        gated,
        local_end,
        state_end,
    )
    return (values + product(gated, mamba_out), kept)


def mamba_backward(values, grad, weights, kept):
    (
        gain,
        mamba_in,
        conv_weight,
        conv_bias,
        selection,
        step_proj,
        step_bias,
        decay_log,
        skip_gain,
        mamba_out,
    ) = weights
    (
        valid,
        normed,
        projected,
        before,
        mixed,
        mixed_low,
        step_low,
        pre,
        step,
        inputs_b,
        outputs_c,
        decay,
        state,
        through,
        prefix_decay,
        mixed_out,
        gated,
        local_end,
        state_end,
    ) = kept
    group = values.shape[1]
    inner_width = mamba_out.shape[0]
    grad_low = grad.astype(jnp.bfloat16)
    grad_out = outer(gated, grad_low)
    grad_gated = product_back(grad_low, mamba_out)
    gate = projected[..., inner_width:]

    def mamba_gating(mixed_part, gate_part):
        return mixed_part * jax.nn.silu(gate_part)

    unused, gating_back = jax.vjp(mamba_gating, mixed_out, gate)
    grad_mixed_out, grad_gate = gating_back(grad_gated)
    skip = skip_gain.astype(jnp.float32)
    grad_skip = jnp.sum(grad_mixed_out * mixed, axis=(0, 1))
    unused, scan_back = jax.vjp(selective, mixed, step, inputs_b, outputs_c, decay, state)
    zero = jnp.zeros_like(state)
    ones = jnp.ones_like(state)
    own = scan_back((grad_mixed_out, zero))[5]
    suffix = carried_in(
        (through, own, through, local_end), "seq", chain_both, (ones, zero, ones, zero), True
    )
    final = suffix[2] * state_end + suffix[3]
    piece_width = inner_width // lax.axis_size("seq")
    new_state = lax.dynamic_slice_in_dim(final, lax.axis_index("seq") * piece_width, piece_width, 2)
    grad_state = lax.psum_scatter(prefix_decay * own, "seq", scatter_dimension=2, tiled=True)
    grad_mixed, grad_step, grad_inputs, grad_outputs, grad_decay, unused_state = scan_back(
        (grad_mixed_out, suffix[1])
    )
    grad_mixed = grad_mixed + grad_mixed_out * skip
    unused, step_back = jax.vjp(
        lambda pre_part, bias_part: stepping(pre_part, bias_part, valid),
        pre,
        step_bias.astype(jnp.float32),
    )
    grad_pre, grad_step_bias = step_back(grad_step)
    grad_pre_low = grad_pre.astype(jnp.bfloat16)
    grad_step_proj = outer(step_low, grad_pre_low)
    grad_step_low = product_back(grad_pre_low, step_proj)
    grad_select = jnp.concatenate([grad_step_low, grad_inputs, grad_outputs], axis=-1).astype(
        jnp.bfloat16
    )
    grad_selection = outer(mixed_low, grad_select)
    grad_mixed = grad_mixed + product_back(grad_select, selection)
    inner = projected[..., :inner_width]
    unused, conv_back = jax.vjp(
        convolve, before, inner, conv_weight.astype(jnp.float32), conv_bias.astype(jnp.float32)
    )
    grad_before, grad_inner, grad_conv_weight, grad_conv_bias = conv_back(grad_mixed)
    returned = shifted(grad_before, "seq", -1)
    grad_inner = jnp.concatenate(
        [grad_inner[:, : group - CONV + 1], grad_inner[:, group - CONV + 1 :] + returned], axis=1
    )
    grad_projected = jnp.concatenate([grad_inner, grad_gate], axis=-1).astype(jnp.bfloat16)
    grad_in = outer(normed, grad_projected)
    grad_normed = product_back(grad_projected, mamba_in)
    unused, norm_back = jax.vjp(rms_gain, values, gain.astype(jnp.float32))
    grad_values, grad_gain = norm_back(grad_normed)
    grads = (
        grad_gain,
        grad_in,
        grad_conv_weight,
        grad_conv_bias,
        grad_selection,
        grad_step_proj,
        grad_step_bias,
        grad_decay * decay,
        grad_skip,
        grad_out,
    )
    return (grad + grad_values, grads, grad_state, new_state)


def key_positions(start, count, cache_rows, group):
    index = start + jnp.arange(count)
    owner = index // (cache_rows + group)
    offset = index % (cache_rows + group)
    return jnp.where(
        offset < cache_rows,
        owner * cache_rows + offset - WINDOW,
        owner * group + offset - cache_rows,
    )


def visible(query_pos, key_pos, lengths):
    near = (key_pos[None, :] > query_pos[:, None] - WINDOW) & (
        key_pos[None, :] <= query_pos[:, None]
    )
    real = (key_pos[None, None, :] < lengths[:, None, None]) | (
        key_pos[None, None, :] == query_pos[None, :, None]
    )
    return (near[None] & real)[:, :, None, :]


def blockwise(step_fn, carry, piece, size):
    count = jax.tree.leaves(piece)[0].shape[1]
    blocks = count // size

    def split(item):
        return jnp.moveaxis(item.reshape((item.shape[0], blocks, size) + item.shape[2:]), 1, 0)

    def turn(inner, pair):
        return (step_fn(inner, pair[1], pair[0] * size), None)

    carry, unused = lax.scan(turn, carry, (jnp.arange(blocks), jax.tree.map(split, piece)))
    return carry


def over_keys(local_kv, fold, init):
    return fold(init, lax.all_gather(local_kv, "seq", axis=1, tiled=True), jnp.int32(0))


def attention_forward(values, lengths, carried_kv, weights):
    gain, qkv_proj, out_proj = weights
    rows, group, width = values.shape
    heads = width // HEAD_DIM
    cache_rows = carried_kv.shape[1]
    size = cache_rows + group
    scale = HEAD_DIM ** (-0.5)
    query_pos = lax.axis_index("seq") * group + jnp.arange(group)
    normed = rms_gain(values, gain.astype(jnp.float32)).astype(jnp.bfloat16)
    qkv = product(normed, qkv_proj).astype(jnp.bfloat16)
    queries = qkv[..., :width].reshape(rows, group, heads, HEAD_DIM)
    segment_kv = qkv[..., width:]
    local_kv = jnp.concatenate([carried_kv, segment_kv], axis=1)

    def one_block(carry, piece, start):
        count = piece.shape[1]
        inside = visible(query_pos, key_positions(start, count, cache_rows, group), lengths)

        def one_work(state):
            top, total, accum = state
            keys = piece[..., :width].reshape(rows, count, heads, HEAD_DIM)
            contents = piece[..., width:].reshape(rows, count, heads, HEAD_DIM)
            scores = (
                jnp.einsum("rqhd,rkhd->rqhk", queries, keys, preferred_element_type=jnp.float32)
                * scale
            )
            new_top = jnp.maximum(top, jnp.max(jnp.where(inside, scores, NEGATIVE), axis=-1))
            weights_now = jnp.exp(jnp.where(inside, scores - new_top[..., None], NEGATIVE))
            factor = jnp.exp(top - new_top)
            total = total * factor + jnp.sum(weights_now, axis=-1)
            accum = accum * factor[..., None] + jnp.einsum(
                "rqhk,rkhd->rqhd",
                weights_now.astype(jnp.bfloat16),
                contents,
                preferred_element_type=jnp.float32,
            )
            return (new_top, total, accum)

        return lax.cond(jnp.any(inside), one_work, lambda state: state, carry)

    init = (
        jnp.full((rows, group, heads), NEGATIVE, jnp.float32),
        jnp.zeros((rows, group, heads), jnp.float32),
        jnp.zeros((rows, group, heads, HEAD_DIM), jnp.float32),
    )
    top, total, accum = over_keys(
        local_kv, lambda carry, piece, start: blockwise(one_block, carry, piece, size), init
    )
    attended = accum / total[..., None]
    logsum = top + jnp.log(total)
    attended_low = attended.astype(jnp.bfloat16).reshape(rows, group, width)
    kept = (normed, queries, local_kv, attended, attended_low, logsum, query_pos)
    return (values + product(attended_low, out_proj), segment_kv, kept)


def attention_backward(values, grad, lengths, weights, kept):
    gain, qkv_proj, out_proj = weights
    normed, queries, local_kv, attended, attended_low, logsum, query_pos = kept
    rows, group, width = values.shape
    heads = width // HEAD_DIM
    size = local_kv.shape[1]
    cache_rows = size - group
    scale = HEAD_DIM ** (-0.5)
    grad_low = grad.astype(jnp.bfloat16)
    grad_out = outer(attended_low, grad_low)
    grad_attended = (
        product_back(grad_low, out_proj).astype(jnp.bfloat16).reshape(rows, group, heads, HEAD_DIM)
    )
    delta = jnp.sum(grad_attended.astype(jnp.float32) * attended, axis=-1)

    def query_block(carry, piece, start):
        count = piece.shape[1]
        inside = visible(query_pos, key_positions(start, count, cache_rows, group), lengths)

        def query_work(grad_queries):
            keys = piece[..., :width].reshape(rows, count, heads, HEAD_DIM)
            contents = piece[..., width:].reshape(rows, count, heads, HEAD_DIM)
            scores = (
                jnp.einsum("rqhd,rkhd->rqhk", queries, keys, preferred_element_type=jnp.float32)
                * scale
            )
            weights_now = jnp.exp(jnp.where(inside, scores - logsum[..., None], NEGATIVE))
            grad_weights = jnp.einsum(
                "rqhd,rkhd->rqhk", grad_attended, contents, preferred_element_type=jnp.float32
            )
            grad_scores = (weights_now * (grad_weights - delta[..., None])).astype(jnp.bfloat16)
            return (
                grad_queries
                + jnp.einsum(
                    "rqhk,rkhd->rqhd", grad_scores, keys, preferred_element_type=jnp.float32
                )
                * scale
            )

        return lax.cond(jnp.any(inside), query_work, lambda state: state, carry)

    grad_queries = over_keys(
        local_kv,
        lambda carry, piece, start: blockwise(query_block, carry, piece, size),
        jnp.zeros((rows, group, heads, HEAD_DIM), jnp.float32),
    )
    whole_logsum, whole_delta = (
        lax.all_gather(logsum, "seq", axis=1, tiled=True),
        lax.all_gather(delta, "seq", axis=1, tiled=True),
    )
    own_pos = key_positions(lax.axis_index("seq") * size, size, cache_rows, group)
    own_keys = local_kv[..., :width].reshape(rows, size, heads, HEAD_DIM)
    own_contents = local_kv[..., width:].reshape(rows, size, heads, HEAD_DIM)

    def key_block(carry, piece, start):
        part_queries, part_grads = piece
        count = part_queries.shape[1]
        inside = visible(start + jnp.arange(count), own_pos, lengths)

        def key_work(state):
            grad_keys, grad_contents = state
            part_logsum = lax.dynamic_slice_in_dim(whole_logsum, start, count, 1)
            part_delta = lax.dynamic_slice_in_dim(whole_delta, start, count, 1)
            scores = (
                jnp.einsum(
                    "rqhd,rkhd->rqhk", part_queries, own_keys, preferred_element_type=jnp.float32
                )
                * scale
            )
            weights_now = jnp.exp(jnp.where(inside, scores - part_logsum[..., None], NEGATIVE))
            grad_contents = grad_contents + jnp.einsum(
                "rqhk,rqhd->rkhd",
                weights_now.astype(jnp.bfloat16),
                part_grads,
                preferred_element_type=jnp.float32,
            )
            grad_weights = jnp.einsum(
                "rqhd,rkhd->rqhk", part_grads, own_contents, preferred_element_type=jnp.float32
            )
            grad_scores = (weights_now * (grad_weights - part_delta[..., None])).astype(
                jnp.bfloat16
            )
            grad_keys = (
                grad_keys
                + jnp.einsum(
                    "rqhk,rqhd->rkhd", grad_scores, part_queries, preferred_element_type=jnp.float32
                )
                * scale
            )
            return (grad_keys, grad_contents)

        return lax.cond(jnp.any(inside), key_work, lambda state: state, carry)

    empty = jnp.zeros((rows, size, heads, HEAD_DIM), jnp.float32)
    grad_keys, grad_contents = blockwise(
        key_block,
        (empty, empty),
        (
            lax.all_gather(queries, "seq", axis=1, tiled=True),
            lax.all_gather(grad_attended, "seq", axis=1, tiled=True),
        ),
        group,
    )
    grad_local = jnp.concatenate(
        [grad_keys.reshape(rows, size, width), grad_contents.reshape(rows, size, width)], axis=-1
    )
    grad_cache = grad_local[:, :cache_rows]
    grad_qkv = jnp.concatenate(
        [grad_queries.reshape(rows, group, width), grad_local[:, cache_rows:]], axis=-1
    ).astype(jnp.bfloat16)
    grad_qkv_proj = outer(normed, grad_qkv)
    grad_normed = product_back(grad_qkv, qkv_proj)
    unused, norm_back = jax.vjp(rms_gain, values, gain.astype(jnp.float32))
    grad_values, grad_gain = norm_back(grad_normed)
    return (grad + grad_values, (grad_gain, grad_qkv_proj, grad_out), grad_cache)


def local(
    activations,
    cotangent,
    carried_state,
    carried_kv,
    row_lengths,
    mamba_gain,
    mamba_in,
    conv_weight,
    conv_bias,
    selection,
    step_proj,
    step_bias,
    decay_log,
    skip_gain,
    mamba_out,
    first_gain,
    first_gate_up,
    first_down,
    attention_gain,
    attention_qkv,
    attention_out,
    second_gain,
    second_gate_up,
    second_down,
):
    front_shards = (
        mamba_gain,
        mamba_in,
        conv_weight,
        conv_bias,
        selection,
        step_proj,
        step_bias,
        decay_log,
        skip_gain,
        mamba_out,
        first_gain,
        first_gate_up,
        first_down,
    )
    rear_shards = (
        attention_gain,
        attention_qkv,
        attention_out,
        second_gain,
        second_gate_up,
        second_down,
    )
    stream = activations.astype(jnp.float32)
    front_whole = fetch_front(front_shards)
    first_stream, mamba_kept = mamba_forward(stream, row_lengths, carried_state, front_whole[:10])
    second_stream, first_kept = ffn_forward(first_stream, front_whole[10:])
    rear_whole = fetch_rear(rear_shards)
    third_stream, segment_kv, attention_kept = attention_forward(
        second_stream, row_lengths, carried_kv, rear_whole[:3]
    )
    fourth_stream, second_kept = ffn_forward(third_stream, rear_whole[3:])
    grad = cotangent.astype(jnp.float32)
    rear_back = fetch_rear(rear_shards)
    grad, second_grads = ffn_backward(third_stream, grad, rear_back[3:], second_kept)
    grad, attention_grads, grad_cache = attention_backward(
        second_stream, grad, row_lengths, rear_back[:3], attention_kept
    )
    rear_grads = settle_rear(attention_grads + second_grads)
    front_back = fetch_front(front_shards)
    grad, first_grads = ffn_backward(first_stream, grad, front_back[10:], first_kept)
    grad, mamba_grads, grad_state, new_state = mamba_backward(
        stream, grad, front_back[:10], mamba_kept
    )
    front_grads = settle_front(mamba_grads + first_grads)
    return (
        fourth_stream.astype(jnp.bfloat16),
        new_state,
        segment_kv,
        grad,
        grad_state,
        grad_cache,
        front_grads[0],
        front_grads[1],
        front_grads[2],
        front_grads[3],
        front_grads[4],
        front_grads[5],
        front_grads[6],
        front_grads[7],
        front_grads[8],
        front_grads[9],
        front_grads[10],
        front_grads[11],
        front_grads[12],
        rear_grads[0],
        rear_grads[1],
        rear_grads[2],
        rear_grads[3],
        rear_grads[4],
        rear_grads[5],
    )


EVERY = ("y", "c", "z", "x")
PLANE = ("y", "c", "x")
BF = jnp.bfloat16
F32 = jnp.float32


def params(**more):
    return pltpu.CompilerParams(vmem_limit_bytes=60 * 2**20, **more)


def swap_planes(block):
    planes = lax.axis_size("z")
    inner = lax.axis_size("x")
    route = []
    for d in range(planes):
        for z in range(planes):
            for x in range(inner):
                route.append(((d * planes + z) * inner + x, (z * planes + d) * inner + x))
    return lax.ppermute(block, EVERY, route)


def other(block, axis):
    return lax.ppermute(block, axis, [(0, 1), (1, 0)])


def gather_plane(block):
    from_y = other(block, "y")
    from_x = other(block, "x")
    corner = jnp.concatenate([other(from_y[:1], "x"), other(from_x[1:], "y")], axis=0)
    own = jnp.stack([block, from_x, from_y, corner])
    return jnp.concatenate([own, other(own, "c")], axis=0)


def scatter_plane(parts):
    kind = parts.dtype
    half = parts.shape[0] // 2
    mine = parts[:half].astype(F32) + other(parts[half:], "c").astype(F32)
    sent = mine[1:].astype(kind)
    to_x, to_y, corner = sent[0], sent[1], sent[2]
    via_y = other(corner[:1], "y").astype(F32)
    via_x = other(corner[1:], "x").astype(F32)
    to_x = jnp.concatenate([(mine[1][:1] + via_y).astype(kind), to_x[1:]], axis=0)
    to_y = jnp.concatenate([to_y[:1], (mine[2][1:] + via_x).astype(kind)], axis=0)
    return mine[0] + other(to_x, "x").astype(F32) + other(to_y, "y").astype(F32)


def sum_plane(parts):
    return gather_plane(scatter_plane(parts))


def trade(block, axes):
    return lax.all_to_all(block, axes, 0, 0, tiled=True)


def turned(block, distance):
    planes = lax.axis_size("z")
    return lax.ppermute(block, "z", [(z, (z + distance) % planes) for z in range(planes)])


def gather_z(block):
    planes = lax.axis_size("z")
    ring = [block] + [turned(block, planes - k) for k in range(1, planes)]
    ring = jnp.stack(ring + ring[:-1])
    first = (planes - lax.axis_index("z")) % planes
    return lax.dynamic_slice_in_dim(ring, first, planes, 0)


def gather_small(block):
    for axis in ("x", "c", "y"):
        pair = (block, other(block, axis))
        here = lax.axis_index(axis) == 0
        block = jnp.stack([jnp.where(here, pair[0], pair[1]), jnp.where(here, pair[1], pair[0])])
    return gather_z(block)


def total_small(block):
    for axis in ("x", "y", "c"):
        block = block + other(block, axis)
    return block + sum(turned(block, k) for k in range(1, lax.axis_size("z")))


def reduce_z(parts):
    return lax.psum_scatter(parts, "z", scatter_dimension=0)


def deal(pieces, back):
    planes, inner = lax.axis_size("z"), lax.axis_size("x")
    result = []
    for k, piece in enumerate(pieces):
        turn, flip = k // inner, k % inner
        route = []
        for d in range(planes):
            for z in range(planes):
                for x in range(inner):
                    goal = (z, d ^ turn, x ^ flip) if back else (z ^ turn, d, x ^ flip)
                    place = (d * planes + z) * inner + x
                    route.append((place, (goal[0] * planes + goal[1]) * inner + goal[2]))
        result.append(lax.ppermute(piece, EVERY, route))
    return result


def rows_gather(block):
    x = lax.axis_index("x")
    mine = lax.dynamic_index_in_dim(block, x, 0, False)
    theirs = lax.dynamic_index_in_dim(block, 1 - x, 0, False)
    pair = jnp.stack([mine, other(theirs, "x")])
    four = jnp.concatenate([pair, other(pair, "y")], axis=0)
    return jnp.concatenate([four, other(four, "c")], axis=0)


def rows_scatter(parts):
    kind = parts.dtype
    for axis in ("c", "y"):
        half = parts.shape[0] // 2
        parts = (
            parts[:half].astype(F32) + other(parts[half:].astype(kind), axis).astype(F32)
        )
    mine, theirs = parts[0], other(parts[1].astype(kind), "x").astype(F32)
    first = lax.axis_index("x") == 0
    return jnp.stack([jnp.where(first, mine, theirs), jnp.where(first, theirs, mine)])


def rows_of(gathered):
    planes, members, rows, width = gathered.shape
    inner = lax.axis_size("x")
    split = gathered.reshape(planes, members // inner, inner, rows, width)
    return split.transpose(1, 0, 2, 3, 4).reshape(planes * members * rows, width)


def by_plane(grad):
    planes, inner = lax.axis_size("z"), lax.axis_size("x")
    total, width = grad.shape
    rows = total // (planes * planes * inner)
    split = grad.reshape(planes, planes, inner, rows, width).transpose(1, 0, 2, 3, 4)
    return split.reshape(planes, planes * inner, rows, width)


def columns_in(payload):
    return rows_of(lax.all_gather(trade(payload, PLANE), "z", axis=0))


def columns_out(grad):
    return trade(reduce_z(by_plane(grad.astype(BF))), PLANE)


def relocate(block, back):
    planes, inner = lax.axis_size("z"), lax.axis_size("x")
    route = []
    for place in range(planes * inner):
        goal = (place % planes) * inner + place // planes
        route.append((goal, place) if back else (place, goal))
    return lax.ppermute(block, ("z", "x"), route)


def dot(left, right, left_dim, right_dim):
    return lax.dot_general(
        left, right, (((left_dim,), (right_dim,)), ((), ())), preferred_element_type=F32
    )


def conv_body(order, inner_ref, taps_ref, bias_ref, total_ref, mixed_ref, low_ref, held):
    step = pl.program_id(0)
    rows, group = inner_ref.shape[1], inner_ref.shape[2]

    @pl.when(step == 0)
    def clear():
        held[:, :8] = jnp.zeros_like(held[:, :8])

    @pl.when(step > 0)
    def keep():
        held[:, :8] = held[:, group:]

    for row in range(rows):
        held[row, 8:] = inner_ref[0, row]
        total = bias_ref[...] + taps_ref[0:1] * held[row, 5 : 5 + group]
        for tap in range(1, CONV):
            total = total + taps_ref[tap : tap + 1] * held[row, 5 + tap : 5 + tap + group]
        mixed = total / (1.0 + jnp.exp(-total))
        total_ref[0, row] = total
        mixed_ref[0, row] = mixed
        low_ref[0, row] = mixed.astype(BF)


def conv_forward(order, projected, taps, bias):
    blocks, rows, group, both = projected.shape
    width = both // 2
    spec = pl.BlockSpec((1, rows, group, width), lambda i, order: (order[i], 0, 0, 0))
    shape = (blocks, rows, group, width)
    return pl.pallas_call(
        conv_body,
        grid_spec=pltpu.PrefetchScalarGridSpec(
            num_scalar_prefetch=1,
            grid=(blocks,),
            in_specs=[
                spec,
                pl.BlockSpec((CONV, width), lambda i, order: (0, 0)),
                pl.BlockSpec((1, width), lambda i, order: (0, 0)),
            ],
            out_specs=[spec, spec, spec],
            scratch_shapes=[pltpu.VMEM((rows, group + 8, width), F32)],
        ),
        out_shape=[
            jax.ShapeDtypeStruct(shape, F32),
            jax.ShapeDtypeStruct(shape, F32),
            jax.ShapeDtypeStruct(shape, BF),
        ],
        compiler_params=params(),
        name="conv_forward",
    )(order, projected, taps, bias)


def conv_back_body(order, grad_ref, total_ref, inner_ref, taps_ref, out_ref, sums_ref, held):
    step = pl.program_id(0)
    rows, group = inner_ref.shape[1], inner_ref.shape[2]

    @pl.when(step == 0)
    def clear():
        held[:, group:] = jnp.zeros_like(held[:, group:])
        sums_ref[...] = jnp.zeros_like(sums_ref)

    @pl.when(step > 0)
    def keep():
        held[:, group:] = held[:, :8]

    for row in range(rows):
        total = total_ref[0, row]
        sig = 1.0 / (1.0 + jnp.exp(-total))
        grad = grad_ref[0, row] * (sig * (1.0 + total * (1.0 - sig)))
        held[row, :group] = grad
        inner = inner_ref[0, row]
        back = None
        for tap in range(CONV):
            later = held[row, CONV - 1 - tap : CONV - 1 - tap + group]
            part = taps_ref[tap : tap + 1] * later
            back = part if back is None else back + part
            sums_ref[tap : tap + 1] += jnp.sum(inner * later, axis=0, keepdims=True)
        sums_ref[CONV : CONV + 1] += jnp.sum(grad, axis=0, keepdims=True)
        out_ref[0, row] = back.astype(BF)


def conv_back(order, grad, total, projected, taps):
    blocks, rows, group, width = grad.shape
    spec = pl.BlockSpec(
        (1, rows, group, width), lambda i, order: (order[blocks - 1 - i], 0, 0, 0)
    )
    return pl.pallas_call(
        conv_back_body,
        grid_spec=pltpu.PrefetchScalarGridSpec(
            num_scalar_prefetch=1,
            grid=(blocks,),
            in_specs=[spec, spec, spec, pl.BlockSpec((CONV, width), lambda i, order: (0, 0))],
            out_specs=[spec, pl.BlockSpec((8, width), lambda i, order: (0, 0))],
            scratch_shapes=[pltpu.VMEM((rows, group + 8, width), F32)],
        ),
        out_shape=[
            jax.ShapeDtypeStruct(grad.shape, BF),
            jax.ShapeDtypeStruct((8, width), F32),
        ],
        compiler_params=params(),
        name="conv_back",
    )(order, grad, total, projected, taps)


def widen(tile, width):
    return jnp.concatenate([tile] * (width // 128), axis=1)


def narrow(tile):
    total = tile[:, :128]
    for start in range(128, tile.shape[1], 128):
        total = total + tile[:, start : start + 128]
    return total


def scan_body(
    order, mixed_ref, step_ref, b_ref, c_ref, decay_ref, start_ref, core_ref, past_ref, end_ref, held
):
    @pl.when(pl.program_id(0) == 0)
    def begin():
        held[...] = start_ref[...]

    decay = decay_ref[...]
    rows, group, width = mixed_ref.shape[1:]

    def eight(turn, states):
        base = pl.multiple_of(turn * 8, 8)
        states = list(states)
        steps = [step_ref[0, row, pl.ds(base, 8), :] for row in range(rows)]
        drives = [steps[row] * mixed_ref[0, row, pl.ds(base, 8), :] for row in range(rows)]
        cores = [[] for row in range(rows)]
        for k in range(8):
            for row in range(rows):
                past_ref[0, row, base + k] = states[row]
                fade = jnp.exp(steps[row][k : k + 1] * decay)
                state = fade * states[row] + drives[row][k : k + 1] * widen(
                    b_ref[0, row, base + k], width
                )
                states[row] = state
                seen = widen(c_ref[0, row, base + k], width) * state
                cores[row].append(jnp.sum(seen, axis=0, keepdims=True))
        for row in range(rows):
            core_ref[0, row, pl.ds(base, 8), :] = jnp.concatenate(cores[row], axis=0)
        return tuple(states)

    states = lax.fori_loop(0, group // 8, eight, tuple(held[row] for row in range(rows)))
    for row in range(rows):
        held[row] = states[row]
        end_ref[row] = states[row]


def scan_forward(order, mixed, step, wide_b, wide_c, decay, start):
    blocks, rows, group, width = mixed.shape
    states = decay.shape[0]
    spec = pl.BlockSpec((1, rows, group, width), lambda i, order: (order[i], 0, 0, 0))
    maps = pl.BlockSpec((1, rows, group, states, 128), lambda i, order: (order[i], 0, 0, 0, 0))
    whole = pl.BlockSpec((rows, states, width), lambda i, order: (0, 0, 0))
    return pl.pallas_call(
        scan_body,
        grid_spec=pltpu.PrefetchScalarGridSpec(
            num_scalar_prefetch=1,
            grid=(blocks,),
            in_specs=[
                spec,
                spec,
                maps,
                maps,
                pl.BlockSpec((states, width), lambda i, order: (0, 0)),
                whole,
            ],
            out_specs=[
                spec,
                pl.BlockSpec(
                    (1, rows, group, states, width), lambda i, order: (order[i], 0, 0, 0, 0)
                ),
                whole,
            ],
            scratch_shapes=[pltpu.VMEM((rows, states, width), F32)],
        ),
        out_shape=[
            jax.ShapeDtypeStruct(mixed.shape, F32),
            jax.ShapeDtypeStruct((blocks, rows, group, states, width), F32),
            jax.ShapeDtypeStruct(start.shape, F32),
        ],
        compiler_params=params(),
        name="scan_forward",
    )(order, mixed, step, wide_b, wide_c, decay, start)


def scan_back_body(
    order,
    mixed_ref,
    step_ref,
    b_ref,
    c_ref,
    grad_ref,
    past_ref,
    decay_ref,
    end_ref,
    dmixed_ref,
    dstep_ref,
    db_ref,
    dc_ref,
    ddecay_ref,
    dstart_ref,
    held,
    after,
):
    @pl.when(pl.program_id(0) == 0)
    def begin():
        held[...] = jnp.zeros_like(held)
        after[...] = end_ref[...]
        ddecay_ref[...] = jnp.zeros_like(ddecay_ref)

    decay = decay_ref[...]
    rows, group, width = mixed_ref.shape[1:]
    turns = group // 8

    def eight(turn, carry):
        base = pl.multiple_of((turns - 1 - turn) * 8, 8)
        backs, states, sums = list(carry[0]), list(carry[1]), carry[2]
        steps = [step_ref[0, row, pl.ds(base, 8), :] for row in range(rows)]
        inputs = [mixed_ref[0, row, pl.ds(base, 8), :] for row in range(rows)]
        grads = [grad_ref[0, row, pl.ds(base, 8), :] for row in range(rows)]
        drives = [steps[row] * inputs[row] for row in range(rows)]
        firsts = [[None] * 8 for row in range(rows)]
        seconds = [[None] * 8 for row in range(rows)]
        for k in reversed(range(8)):
            for row in range(rows):
                now = steps[row][k : k + 1]
                grad = grads[row][k : k + 1]
                past = past_ref[0, row, base + k]
                fade = jnp.exp(now * decay)
                back = widen(c_ref[0, row, base + k], width) * grad + backs[row]
                dc_ref[0, row, base + k] = narrow(states[row] * grad)
                firsts[row][k] = jnp.sum(
                    widen(b_ref[0, row, base + k], width) * back, axis=0, keepdims=True
                )
                db_ref[0, row, base + k] = narrow(back * drives[row][k : k + 1])
                faded = fade * back
                flow = faded * past
                seconds[row][k] = jnp.sum(flow * decay, axis=0, keepdims=True)
                sums = sums + flow * now
                backs[row] = faded
                states[row] = past
        for row in range(rows):
            first = jnp.concatenate(firsts[row], axis=0)
            second = jnp.concatenate(seconds[row], axis=0)
            dmixed_ref[0, row, pl.ds(base, 8), :] = steps[row] * first
            dstep_ref[0, row, pl.ds(base, 8), :] = inputs[row] * first + second
        return (tuple(backs), tuple(states), sums)

    backs, states, sums = lax.fori_loop(
        0,
        turns,
        eight,
        (
            tuple(held[row] for row in range(rows)),
            tuple(after[row] for row in range(rows)),
            ddecay_ref[...],
        ),
    )
    ddecay_ref[...] = sums
    for row in range(rows):
        held[row] = backs[row]
        after[row] = states[row]
        dstart_ref[row] = backs[row]


def scan_back(order, mixed, step, wide_b, wide_c, grad, past, decay, end):
    blocks, rows, group, width = mixed.shape
    states = decay.shape[0]
    last = blocks - 1
    spec = pl.BlockSpec((1, rows, group, width), lambda i, order: (order[last - i], 0, 0, 0))
    maps = pl.BlockSpec(
        (1, rows, group, states, 128), lambda i, order: (order[last - i], 0, 0, 0, 0)
    )
    kept = pl.BlockSpec(
        (1, rows, group, states, width), lambda i, order: (order[last - i], 0, 0, 0, 0)
    )
    whole = pl.BlockSpec((rows, states, width), lambda i, order: (0, 0, 0))
    rates = pl.BlockSpec((states, width), lambda i, order: (0, 0))
    return pl.pallas_call(
        scan_back_body,
        grid_spec=pltpu.PrefetchScalarGridSpec(
            num_scalar_prefetch=1,
            grid=(blocks,),
            in_specs=[spec, spec, maps, maps, spec, kept, rates, whole],
            out_specs=[spec, spec, maps, maps, rates, whole],
            scratch_shapes=[
                pltpu.VMEM((rows, states, width), F32),
                pltpu.VMEM((rows, states, width), F32),
            ],
        ),
        out_shape=[
            jax.ShapeDtypeStruct(mixed.shape, F32),
            jax.ShapeDtypeStruct(mixed.shape, F32),
            jax.ShapeDtypeStruct((blocks, rows, group, states, 128), F32),
            jax.ShapeDtypeStruct((blocks, rows, group, states, 128), F32),
            jax.ShapeDtypeStruct(decay.shape, F32),
            jax.ShapeDtypeStruct(end.shape, F32),
        ],
        compiler_params=params(),
        name="scan_back",
    )(order, mixed, step, wide_b, wide_c, grad, past, decay, end)


def own_positions(shape, axis, first, member, group):
    index = first + lax.broadcasted_iota(jnp.int32, shape, axis)
    slot = index // group
    block = (((slot & 2) << 1) | ((slot & 4) >> 1) | (slot & 1)) ^ member
    return block * group + index % group


def seen_cache(query, place, shape, group):
    index = lax.broadcasted_iota(jnp.int32, shape, 1)
    return (index + place * group) > query


def seen_own(query, key, length):
    return (key <= query) & ((key < length) | (key == query))


def attend_body(meta_ref, q_ref, ck_ref, cv_ref, k_ref, v_ref, out_ref, log_ref):
    count = q_ref.shape[0]
    first = pl.program_id(1) * count
    scale = HEAD_DIM ** (-0.5)
    queries = q_ref[...]
    pieces = ck_ref.shape[0]
    size = ck_ref.shape[2]
    tokens = k_ref.shape[0]
    member = meta_ref[1]
    group = tokens // pieces
    query = own_positions((count, 1), 0, first, member, group)
    scores = []
    for piece in range(pieces):
        score = dot(queries, ck_ref[piece, 0], 1, 1) * scale
        inside = seen_cache(query, member ^ piece, (1, size), size)
        scores.append(jnp.where(inside, score, NEGATIVE))
    score = dot(queries, k_ref[...], 1, 1) * scale
    key = own_positions((1, tokens), 1, 0, member, group)
    scores.append(jnp.where(seen_own(query, key, meta_ref[0]), score, NEGATIVE))
    top = jnp.max(scores[0], axis=1, keepdims=True)
    for score in scores[1:]:
        top = jnp.maximum(top, jnp.max(score, axis=1, keepdims=True))
    total = jnp.zeros_like(top)
    result = jnp.zeros((count, HEAD_DIM), F32)
    for piece, score in enumerate(scores):
        part = jnp.exp(score - top)
        total = total + jnp.sum(part, axis=1, keepdims=True)
        contents = cv_ref[piece, 0] if piece < pieces else v_ref[...]
        result = result + dot(part.astype(BF), contents, 1, 0)
    out_ref[...] = result / total
    log_ref[0] = jnp.broadcast_to(top + jnp.log(total), (count, 128))


def attend(meta, qkv, cache):
    tokens, width = qkv.shape
    width = width // 3
    heads = width // HEAD_DIM
    count = 256
    shards, two, group, unused = cache.shape
    own = lambda base: pl.BlockSpec((tokens, HEAD_DIM), lambda h, i, meta: (0, base + h))
    held = lambda which: pl.BlockSpec(
        (shards, 1, group, HEAD_DIM), lambda h, i, meta: (0, which, 0, h)
    )
    block = pl.BlockSpec((count, HEAD_DIM), lambda h, i, meta: (i, h))
    return pl.pallas_call(
        attend_body,
        grid_spec=pltpu.PrefetchScalarGridSpec(
            num_scalar_prefetch=1,
            grid=(heads, tokens // count),
            in_specs=[block, held(0), held(1), own(heads), own(2 * heads)],
            out_specs=[block, pl.BlockSpec((1, count, 128), lambda h, i, meta: (h, i, 0))],
        ),
        out_shape=[
            jax.ShapeDtypeStruct((tokens, width), F32),
            jax.ShapeDtypeStruct((heads, tokens, 128), F32),
        ],
        compiler_params=params(),
        name="attend",
    )(meta, qkv, cache, cache, qkv, qkv)


def attend_back_body(
    meta_ref,
    q_ref,
    grad_ref,
    out_ref,
    log_ref,
    ck_ref,
    cv_ref,
    k_ref,
    v_ref,
    dcache_ref,
    dq_ref,
    dk_ref,
    dv_ref,
    total,
    delta,
):
    piece = pl.program_id(1)
    pieces = pl.num_programs(1) - 1
    scale = HEAD_DIM ** (-0.5)
    queries = q_ref[...]
    grad = grad_ref[...]
    count = queries.shape[0]
    size = ck_ref.shape[2]
    member = meta_ref[1]
    group = count // (2 * pieces)
    query = own_positions((count, 1), 0, 0, member, group)

    @pl.when(piece == 0)
    def begin():
        total[...] = jnp.zeros_like(total)
        mine = jnp.sum(grad.astype(F32) * out_ref[...], axis=1, keepdims=True)
        delta[...] = jnp.broadcast_to(mine, delta.shape)

    def work(keys, contents, inside):
        score = dot(queries, keys, 1, 1) * scale
        part = jnp.where(inside, jnp.exp(score - log_ref[0][:, :1]), 0.0)
        dcontents = dot(part.astype(BF), grad, 0, 0)
        slope = dot(grad, contents, 1, 1)
        dscore = (part * (slope - delta[:, :1])).astype(BF)
        total[...] += dot(dscore, keys, 1, 0) * scale
        return dot(dscore, queries, 0, 0) * scale, dcontents

    @pl.when(piece < pieces)
    def cached():
        for half in range(2):
            inside = seen_cache(query, member ^ (2 * piece + half), (1, size), size)
            dkeys, dcontents = work(ck_ref[half, 0], cv_ref[half, 0], inside)
            dcache_ref[half, 0] = dkeys.astype(BF)
            dcache_ref[half, 1] = dcontents.astype(BF)

    @pl.when(piece == pieces)
    def own():
        key = own_positions((1, count), 1, 0, member, group)
        dkeys, dcontents = work(k_ref[...], v_ref[...], seen_own(query, key, meta_ref[0]))
        dk_ref[...] = dkeys.astype(BF)
        dv_ref[...] = dcontents.astype(BF)
        dq_ref[...] = total[...].astype(BF)


def attend_back(meta, qkv, grad, out, log, cache):
    tokens, width = grad.shape
    heads = width // HEAD_DIM
    shards, two, group, unused = cache.shape
    pieces = shards // 2
    own = lambda base: pl.BlockSpec((tokens, HEAD_DIM), lambda h, i, meta: (0, base + h))
    place = lambda i: jnp.minimum(i, pieces - 1)
    held = lambda which: pl.BlockSpec(
        (2, 1, group, HEAD_DIM), lambda h, i, meta: (place(i), which, 0, h)
    )
    result = jax.ShapeDtypeStruct((tokens, width), BF)
    return pl.pallas_call(
        attend_back_body,
        grid_spec=pltpu.PrefetchScalarGridSpec(
            num_scalar_prefetch=1,
            grid=(heads, pieces + 1),
            in_specs=[
                own(0),
                own(0),
                own(0),
                pl.BlockSpec((1, tokens, 128), lambda h, i, meta: (h, 0, 0)),
                held(0),
                held(1),
                own(heads),
                own(2 * heads),
            ],
            out_specs=[
                pl.BlockSpec((2, 2, group, HEAD_DIM), lambda h, i, meta: (place(i), 0, 0, h)),
                own(0),
                own(0),
                own(0),
            ],
            scratch_shapes=[
                pltpu.VMEM((tokens, HEAD_DIM), F32),
                pltpu.VMEM((tokens, 128), F32),
            ],
        ),
        out_shape=[jax.ShapeDtypeStruct(cache.shape, BF), result, result, result],
        compiler_params=params(),
        name="attend_back",
    )(meta, qkv, grad, out, log, cache, cache, qkv, qkv)


def silu_slope(values):
    sig = jax.nn.sigmoid(values)
    return sig * (1.0 + values * (1.0 - sig))


def norm_back(values, gain, grad):
    back = jax.vjp(rms_gain, values, gain)[1](grad)
    return back


def plane_forward_ffn(stream, gain, gate_up, down):
    rows, group, wide = stream.shape
    normed = gather_plane(rms_gain(stream, gain).astype(BF)).reshape(-1, wide)
    both = dot(normed, gate_up, 1, 0)
    hidden_width = down.shape[0]
    hidden = (jax.nn.silu(both[:, :hidden_width]) * both[:, hidden_width:]).astype(BF)
    parts = dot(hidden, down, 1, 0).astype(BF).reshape(-1, rows, group, wide)
    return stream + scatter_plane(parts), (normed, both, hidden)


def plane_backward_ffn(stream, grad, grad_whole, gain, gate_up, down, kept):
    normed, both, hidden = kept
    rows, group, wide = stream.shape
    hidden_width = down.shape[0]
    grad_hidden = dot(grad_whole, down, 1, 1)
    gate, up = both[:, :hidden_width], both[:, hidden_width:]
    grad_both = jnp.concatenate(
        [grad_hidden * up * silu_slope(gate), grad_hidden * jax.nn.silu(gate)], axis=1
    ).astype(BF)
    parts = dot(grad_both, gate_up, 1, 1).astype(BF).reshape(-1, rows, group, wide)
    grad_normed = scatter_plane(parts)
    grad_stream, grad_gain = norm_back(stream, gain, grad_normed)
    grad_down = dot(hidden, grad_whole, 0, 0)
    grad_gate_up = dot(normed, grad_both, 0, 0)
    return grad + grad_stream, grad_gain, grad_gate_up, grad_down


def plane_local(
    activations,
    cotangent,
    carried_state,
    carried_kv,
    row_lengths,
    mamba_gain,
    mamba_in,
    conv_weight,
    conv_bias,
    selection,
    step_proj,
    step_bias,
    decay_log,
    skip_gain,
    mamba_out,
    first_gain,
    first_gate_up,
    first_down,
    attention_gain,
    attention_qkv,
    attention_out,
    second_gain,
    second_gate_up,
    second_down,
):
    rows, group, wide = activations.shape
    planes, inner = lax.axis_size("z"), lax.axis_size("x")
    members = planes * inner
    y, c, z, x = (lax.axis_index(name) for name in EVERY)
    member = (y * 2 + c) * inner + x
    place = z * inner + x
    slots = jnp.arange(members) ^ member
    order = (((slots & 2) << 1) | ((slots & 4) >> 1) | (slots & 1)).astype(jnp.int32)
    tokens = swap_planes(activations)
    stream = tokens.astype(F32)
    lengths = swap_planes(row_lengths)

    shard = mamba_gain.shape[0]
    gains = jnp.stack([mamba_gain, first_gain, attention_gain, second_gain])
    gains = gather_small(gains).reshape(planes, planes, inner, 4, shard).transpose(3, 1, 0, 2, 4)
    gains = gains.reshape(4, wide).astype(F32)
    channels = skip_gain.shape[0]
    width = channels * planes
    rank = step_proj.shape[0]
    states = decay_log.shape[0]
    cuts = (selection.shape[1], rank, CONV, 1, 1, states, 1)
    packed = jnp.concatenate(
        [
            selection.astype(F32),
            step_proj.astype(F32).T,
            conv_weight.astype(F32).T,
            conv_bias.astype(F32)[:, None],
            step_bias[:, None],
            decay_log.T,
            skip_gain[:, None],
        ],
        axis=1,
    )
    packed = jnp.pad(packed, ((0, 0), (0, -packed.shape[1] % 128)))
    packed = gather_z(relocate(packed, False)).reshape(width, -1)
    starts = [sum(cuts[:index]) for index in range(len(cuts) + 1)]
    pieces = [packed[:, starts[index] : starts[index + 1]] for index in range(len(cuts))]
    own_selection = pieces[0].astype(BF)
    own_step_proj = pieces[1].astype(BF)
    taps = pieces[2].T
    tap_bias = pieces[3].T
    own_step_bias = pieces[4].T
    decay = -jnp.exp(pieces[5].T)
    skip = pieces[6].T
    own_in = columns_in(
        mamba_in.reshape(shard, 2, members, width).transpose(2, 0, 1, 3).reshape(members, shard, -1)
    )
    own_out = lax.all_gather(relocate(mamba_out, False), "z", axis=0, tiled=True)

    def hidden_columns(gate_up, units):
        split = gate_up.reshape(shard, 2, planes, planes, inner, units)
        return split.transpose(2, 4, 0, 1, 3, 5).reshape(members, shard, -1)

    units = first_down.shape[0]
    head_width = wide // planes
    split = attention_qkv.reshape(shard, 3, planes, head_width).transpose(2, 0, 1, 3)
    split = jnp.broadcast_to(
        split.reshape(planes, 1, shard, 3 * head_width), (planes, inner, shard, 3 * head_width)
    )
    dealt = trade(
        jnp.concatenate(
            [
                hidden_columns(first_gate_up, units),
                split.reshape(members, shard, 3 * head_width),
                hidden_columns(second_gate_up, units),
            ],
            axis=2,
        ),
        PLANE,
    )
    edges = (0, 2 * planes * units, 2 * planes * units + 3 * head_width, dealt.shape[2])
    own_first, own_qkv, own_second = (
        rows_of(lax.all_gather(dealt[:, :, edges[k] : edges[k + 1]], "z", axis=0)) for k in range(3)
    )
    own_first_down = lax.all_gather(first_down, "z", axis=0, tiled=True)
    own_attention_out = lax.all_gather(attention_out, ("z", "x"), axis=0, tiled=True)
    own_second_down = lax.all_gather(second_down, "z", axis=0, tiled=True)
    cache_rows = carried_kv.shape[1]
    chunks = []
    for k in range(members):
        group_of, row_of = z ^ (k // inner), x ^ (k % inner)
        row = lax.dynamic_index_in_dim(carried_kv, row_of, 0, False)
        chunks.append(
            jnp.stack(
                [
                    lax.dynamic_slice_in_dim(row, which * wide + group_of * head_width, head_width, 1)
                    for which in range(2)
                ]
            )
        )
    cache = jnp.stack(deal(chunks, False))
    start = swap_planes(lax.dynamic_slice_in_dim(carried_state, place * width, width, 2))
    grad = swap_planes(cotangent)
    grad_whole = gather_plane(grad).reshape(-1, wide)
    grad = grad.astype(F32)

    normed = gather_plane(tokens).reshape(-1, wide).astype(F32)
    normed = rms_gain(normed, gains[0]).astype(BF)
    projected = dot(normed, own_in, 1, 0).reshape(members, rows, group, 2 * width)
    gate = projected[..., width:]
    total, mixed, mixed_low = conv_forward(order, projected, taps, tap_bias)
    flat_low = mixed_low.reshape(-1, width)
    select = sum_plane(dot(flat_low, own_selection, 1, 0).reshape(members, rows, group, -1))
    step_low = select[..., :rank].astype(BF).reshape(-1, rank)
    pre = dot(step_low, own_step_proj, 1, 1).reshape(members, rows, group, width) + own_step_bias
    blocks = jnp.zeros((members,), jnp.int32).at[order].set(jnp.arange(members, dtype=jnp.int32))
    positions = blocks[:, None] * group + jnp.arange(group)[None, :]
    valid = (positions[:, None, :] < lengths[None, :, None]).astype(F32)[..., None]
    step = jax.nn.softplus(pre) * valid
    wide_shape = (members, rows, group, states, 128)
    wide_b = jnp.broadcast_to(select[..., rank : rank + states, None], wide_shape)
    wide_c = jnp.broadcast_to(select[..., rank + states :, None], wide_shape)
    core, past, end = scan_forward(order, mixed, step, wide_b, wide_c, decay, start)
    mixed_out = core + skip * mixed
    gated = (mixed_out * jax.nn.silu(gate)).astype(BF).reshape(-1, width)
    parts = dot(gated, own_out, 1, 0).astype(BF).reshape(members, rows, group, wide)
    first_stream = stream + scatter_plane(parts)
    new_state = swap_planes(end)

    second_stream, first_kept = plane_forward_ffn(first_stream, gains[1], own_first, own_first_down)

    def kv_back(pieces, kind):
        count = pieces[0].shape[1]
        whole = jnp.zeros((rows, count, 2 * wide), kind)
        for k, piece in enumerate(deal(pieces, True)):
            group_of, row_of = z ^ (k // inner), x ^ (k % inner)
            for which in range(2):
                whole = lax.dynamic_update_slice(
                    whole,
                    piece[which : which + 1].astype(kind),
                    (row_of, 0, which * wide + group_of * head_width),
                )
        return whole

    length = jnp.concatenate([lax.dynamic_slice_in_dim(lengths, x, 1), member[None]])
    normed_rows = rows_gather(rms_gain(second_stream, gains[2]).astype(BF)).reshape(-1, wide)
    qkv = dot(normed_rows, own_qkv, 1, 0).astype(BF)
    attended, log = attend(length, qkv, cache)
    attended_low = attended.astype(BF)
    parts = dot(attended_low, own_attention_out, 1, 0).astype(BF)
    third_stream = second_stream + rows_scatter(parts.reshape(members, group, wide))
    slot_of = [((k & 2) << 1) | ((k & 4) >> 1) | (k & 1) for k in range(members)]
    own_kv = qkv[:, head_width:].reshape(members, group, 2, head_width).transpose(0, 2, 1, 3)
    segment_kv = kv_back([own_kv[slot_of[k]] for k in range(members)], BF)

    fourth_stream, second_kept = plane_forward_ffn(
        third_stream, gains[3], own_second, own_second_down
    )
    output = swap_planes(fourth_stream.astype(BF))

    def hidden_back(grad_columns):
        got = columns_out(grad_columns).astype(F32)
        got = got.reshape(planes, inner, shard, 2, planes, units)
        return got.transpose(2, 3, 0, 4, 1, 5).reshape(shard, -1)

    def down_back(grad_down):
        return reduce_z(grad_down.astype(BF).reshape(planes, units, wide)).astype(F32)

    grad, second_gain_grad, grad_columns, grad_down = plane_backward_ffn(
        third_stream, grad, grad_whole, gains[3], own_second, own_second_down, second_kept
    )
    second_gate_up_grad = hidden_back(grad_columns)
    second_down_grad = down_back(grad_down)

    grad_rows = rows_gather(grad.astype(BF)).reshape(-1, wide)
    grad_attended = dot(grad_rows, own_attention_out, 1, 1).astype(BF)
    grad_cache, dq, dk, dv = attend_back(length, qkv, grad_attended, attended, log, cache)
    grad_qkv = jnp.concatenate([dq, dk, dv], axis=1)
    parts = dot(grad_qkv, own_qkv, 1, 1).astype(BF)
    grad_normed = rows_scatter(parts.reshape(members, group, wide))
    grad_stream, attention_gain_grad = norm_back(second_stream, gains[2], grad_normed)
    grad = grad + grad_stream
    grad_cache = kv_back([grad_cache[k] for k in range(members)], F32)
    grad_out = dot(attended_low, grad_rows, 0, 0).astype(BF)
    grad_out = reduce_z(grad_out.reshape(planes, inner, shard, wide))
    theirs = other(lax.dynamic_index_in_dim(grad_out, 1 - x, 0, False), "x").astype(F32)
    attention_out_grad = lax.dynamic_index_in_dim(grad_out, x, 0, False).astype(F32) + theirs
    got = columns_out(dot(normed_rows, grad_qkv, 0, 0)).astype(F32)
    got = jnp.sum(got.reshape(planes, inner, shard, 3, head_width), axis=1)
    attention_qkv_grad = got.transpose(1, 2, 0, 3).reshape(shard, 3 * wide)

    grad_whole = gather_plane(grad.astype(BF)).reshape(-1, wide)
    grad, first_gain_grad, grad_columns, grad_down = plane_backward_ffn(
        first_stream, grad, grad_whole, gains[1], own_first, own_first_down, first_kept
    )
    first_gate_up_grad = hidden_back(grad_columns)
    first_down_grad = down_back(grad_down)

    grad_whole = gather_plane(grad.astype(BF)).reshape(-1, wide)
    grad_gated = dot(grad_whole, own_out, 1, 1).reshape(mixed.shape)
    grad_core = grad_gated * jax.nn.silu(gate)
    grad_gate = (grad_gated * mixed_out * silu_slope(gate)).astype(BF)
    skip_grad = jnp.sum(grad_core * mixed, axis=(0, 1, 2))
    grad_mixed, grad_step, grad_b, grad_c, grad_decay, grad_start = scan_back(
        order, mixed, step, wide_b, wide_c, grad_core, past, decay, end
    )
    grad_state = swap_planes(grad_start)
    grad_pre = grad_step * valid * jax.nn.sigmoid(pre)
    step_bias_grad = jnp.sum(grad_pre, axis=(0, 1, 2))
    grad_pre = grad_pre.astype(BF).reshape(-1, width)
    step_proj_grad = dot(grad_pre, step_low, 0, 0)
    grad_low = dot(grad_pre, own_step_proj, 1, 0).reshape(members, rows, group, rank)
    grad_select = sum_plane(
        jnp.concatenate([grad_low, jnp.sum(grad_b, axis=-1), jnp.sum(grad_c, axis=-1)], axis=-1)
    )
    grad_select = grad_select.astype(BF).reshape(-1, rank + 2 * states)
    selection_grad = dot(flat_low, grad_select, 0, 0)
    grad_mixed = (
        grad_mixed
        + grad_core * skip
        + dot(grad_select, own_selection, 1, 1).reshape(mixed.shape)
    )
    grad_inner, tap_sums = conv_back(order, grad_mixed, total, projected, taps)
    grad_projected = jnp.concatenate([grad_inner, grad_gate], axis=-1).reshape(-1, 2 * width)
    parts = dot(grad_projected, own_in, 1, 1).astype(BF).reshape(members, rows, group, wide)
    grad_normed = scatter_plane(parts)
    grad_stream, mamba_gain_grad = norm_back(stream, gains[0], grad_normed)
    grad_input = swap_planes(grad + grad_stream)

    got = columns_out(dot(normed, grad_projected, 0, 0)).astype(F32)
    got = got.reshape(members, shard, 2, width)
    mamba_in_grad = got.transpose(1, 2, 0, 3).reshape(shard, -1)
    grad_out = dot(gated, grad_whole, 0, 0).astype(BF).reshape(planes, channels, wide)
    mamba_out_grad = relocate(reduce_z(grad_out), True).astype(F32)
    packed = jnp.concatenate(
        [
            selection_grad,
            step_proj_grad,
            tap_sums[: CONV + 1].T,
            step_bias_grad[:, None],
            (grad_decay * decay).T,
            skip_grad[:, None],
        ],
        axis=1,
    )
    packed = jnp.pad(packed, ((0, 0), (0, -packed.shape[1] % 128)))
    packed = packed.reshape(planes, channels, -1)
    summed = lax.dynamic_index_in_dim(packed, z, 0, False)
    for distance in range(1, planes):
        goal = (z + distance) % planes
        summed = summed + turned(lax.dynamic_index_in_dim(packed, goal, 0, False), distance)
    packed = relocate(summed, True)
    pieces = [packed[:, starts[index] : starts[index + 1]] for index in range(len(cuts))]

    gain_grads = total_small(jnp.stack([first_gain_grad, attention_gain_grad, second_gain_grad]))
    mamba_gain_grad = total_small(mamba_gain_grad[None])
    gain_grads = jnp.concatenate([mamba_gain_grad, gain_grads], axis=0)
    index = ((y * 2 + c) * planes + z) * inner + x
    gain_grads = lax.dynamic_slice_in_dim(gain_grads, index * shard, shard, 1)
    return (
        output,
        new_state,
        segment_kv,
        grad_input,
        grad_state,
        grad_cache,
        gain_grads[0],
        mamba_in_grad,
        pieces[2].T,
        pieces[3][:, 0],
        pieces[0],
        pieces[1].T,
        pieces[4][:, 0],
        pieces[5].T,
        pieces[6][:, 0],
        mamba_out_grad,
        gain_grads[1],
        first_gate_up_grad,
        first_down_grad,
        gain_grads[2],
        attention_qkv_grad,
        attention_out_grad,
        gain_grads[3],
        second_gate_up_grad,
        second_down_grad,
    )


def placements(dp, seq):
    every = dp + seq
    places = (
        P(dp, seq, None),
        P(dp, seq, None),
        P(dp, None, None),
        P(dp, seq, None),
        P(dp),
        P(every),
        P(every, None),
        P(None, every),
        P(every),
        P(every, None),
        P(None, every),
        P(every),
        P(None, every),
        P(every),
        P(every, None),
        P(every),
        P(every, None),
        P(every, None),
        P(every),
        P(every, None),
        P(every, None),
        P(every),
        P(every, None),
        P(every, None),

    )
    results = (
        P(dp, seq, None),
        P(dp, None, seq),
        P(dp, seq, None),
        P(dp, seq, None),
        P(dp, None, seq),
        P(dp, seq, None),
        P(every),
        P(every, None),
        P(None, every),
        P(every),
        P(every, None),
        P(None, every),
        P(every),
        P(None, every),
        P(every),
        P(every, None),
        P(every),
        P(every, None),
        P(every, None),
        P(every),
        P(every, None),
        P(every, None),
        P(every),
        P(every, None),
        P(every, None),

    )
    return places, results


def plane_fits(mesh):
    dp, seq = mesh.shape["dp"], mesh.shape["seq"]
    return dp == 4 and seq == 2 * dp


def solution(mesh):
    if not plane_fits(mesh):
        places, results = placements(("dp",), ("seq",))
        return jax.shard_map(
            local, mesh=mesh, in_specs=places, out_specs=results, check_vma=False
        )
    dp, seq = mesh.shape["dp"], mesh.shape["seq"]
    devices = mesh.devices.reshape(dp // 2, 2, dp, seq // dp)
    places, results = placements(("y", "c"), ("z", "x"))
    return jax.shard_map(
        plane_local,
        mesh=Mesh(devices, EVERY),
        in_specs=places,
        out_specs=results,
        check_vma=False,
    )
```

```python
import jax
import jax.numpy as jnp
from jax import lax
from jax.experimental import pallas as pl
from jax.experimental.pallas import tpu as pltpu
from jax.sharding import Mesh
from jax.sharding import PartitionSpec as P

HEAD_DIM = 128
CONV = 4
WINDOW = 2048


EPSILON = 1e-05
NEGATIVE = -1e30


def shifted(block, axis, distance):
    devices = range(lax.axis_size(axis))
    route = [(i - distance, i) for i in devices if i - distance in devices]
    return lax.ppermute(block, axis, route)


def carried_in(part, axis, combine, identity, reverse):
    count = lax.axis_size(axis)
    place = lax.axis_index(axis)
    ahead = count - 1 - place if reverse else place
    gathered = jax.tree.map(lambda a: lax.all_gather(a, axis), part)
    state = jax.tree.map(lambda a, e: jnp.zeros_like(a) + jnp.asarray(e, a.dtype), part, identity)

    def one(lap, state):
        source = count - 1 - lap if reverse else lap
        return combine(
            state, jax.tree.map(lambda a: lax.dynamic_index_in_dim(a, source, 0, False), gathered)
        )

    return lax.fori_loop(0, ahead, one, state)


def rms_gain(values, gain):
    return values * lax.rsqrt(jnp.mean(values * values, axis=-1, keepdims=True) + EPSILON) * gain


def product(left, right):
    return lax.dot_general(
        left, right, (((left.ndim - 1,), (0,)), ((), ())), preferred_element_type=jnp.float32
    )


def product_back(left, right):
    return lax.dot_general(
        left, right, (((left.ndim - 1,), (1,)), ((), ())), preferred_element_type=jnp.float32
    )


def outer(left, right):
    flat_left = left.reshape(-1, left.shape[-1])
    flat_right = right.reshape(-1, right.shape[-1])
    return lax.dot_general(
        flat_left, flat_right, (((0,), (0,)), ((), ())), preferred_element_type=jnp.float32
    )


def fetch_front(shards):
    return (
        lax.all_gather(shards[0], ("dp", "seq"), axis=0, tiled=True),
        lax.all_gather(shards[1], ("dp", "seq"), axis=0, tiled=True),
        lax.all_gather(shards[2], ("dp", "seq"), axis=1, tiled=True),
        lax.all_gather(shards[3], ("dp", "seq"), axis=0, tiled=True),
        lax.all_gather(shards[4], ("dp", "seq"), axis=0, tiled=True),
        lax.all_gather(shards[5], ("dp", "seq"), axis=1, tiled=True),
        lax.all_gather(shards[6].astype(jnp.bfloat16), ("dp", "seq"), axis=0, tiled=True).astype(
            jnp.float32
        ),
        lax.all_gather(shards[7].astype(jnp.bfloat16), ("dp", "seq"), axis=1, tiled=True).astype(
            jnp.float32
        ),
        lax.all_gather(shards[8].astype(jnp.bfloat16), ("dp", "seq"), axis=0, tiled=True).astype(
            jnp.float32
        ),
        lax.all_gather(shards[9], ("dp", "seq"), axis=0, tiled=True),
        lax.all_gather(shards[10], ("dp", "seq"), axis=0, tiled=True),
        lax.all_gather(shards[11], ("dp", "seq"), axis=0, tiled=True),
        lax.all_gather(shards[12], ("dp", "seq"), axis=0, tiled=True),
    )


def settle_front(grads):
    return (
        lax.psum_scatter(grads[0], ("dp", "seq"), scatter_dimension=0, tiled=True),
        lax.psum_scatter(grads[1], ("dp", "seq"), scatter_dimension=0, tiled=True),
        lax.psum_scatter(grads[2], ("dp", "seq"), scatter_dimension=1, tiled=True),
        lax.psum_scatter(grads[3], ("dp", "seq"), scatter_dimension=0, tiled=True),
        lax.psum_scatter(grads[4], ("dp", "seq"), scatter_dimension=0, tiled=True),
        lax.psum_scatter(grads[5], ("dp", "seq"), scatter_dimension=1, tiled=True),
        lax.psum_scatter(grads[6], ("dp", "seq"), scatter_dimension=0, tiled=True),
        lax.psum_scatter(grads[7], ("dp", "seq"), scatter_dimension=1, tiled=True),
        lax.psum_scatter(grads[8], ("dp", "seq"), scatter_dimension=0, tiled=True),
        lax.psum_scatter(grads[9], ("dp", "seq"), scatter_dimension=0, tiled=True),
        lax.psum_scatter(grads[10], ("dp", "seq"), scatter_dimension=0, tiled=True),
        lax.psum_scatter(grads[11], ("dp", "seq"), scatter_dimension=0, tiled=True),
        lax.psum_scatter(grads[12], ("dp", "seq"), scatter_dimension=0, tiled=True),
    )


def fetch_rear(shards):
    return (
        lax.all_gather(shards[0], ("dp", "seq"), axis=0, tiled=True),
        lax.all_gather(shards[1], ("dp", "seq"), axis=0, tiled=True),
        lax.all_gather(shards[2], ("dp", "seq"), axis=0, tiled=True),
        lax.all_gather(shards[3], ("dp", "seq"), axis=0, tiled=True),
        lax.all_gather(shards[4], ("dp", "seq"), axis=0, tiled=True),
        lax.all_gather(shards[5], ("dp", "seq"), axis=0, tiled=True),
    )


def settle_rear(grads):
    return (
        lax.psum_scatter(grads[0], ("dp", "seq"), scatter_dimension=0, tiled=True),
        lax.psum_scatter(grads[1], ("dp", "seq"), scatter_dimension=0, tiled=True),
        lax.psum_scatter(grads[2], ("dp", "seq"), scatter_dimension=0, tiled=True),
        lax.psum_scatter(grads[3], ("dp", "seq"), scatter_dimension=0, tiled=True),
        lax.psum_scatter(grads[4], ("dp", "seq"), scatter_dimension=0, tiled=True),
        lax.psum_scatter(grads[5], ("dp", "seq"), scatter_dimension=0, tiled=True),
    )


def ffn_forward(values, weights):
    gain, gate_up, down = weights
    width = down.shape[0]
    normed = rms_gain(values, gain.astype(jnp.float32)).astype(jnp.bfloat16)
    both = product(normed, gate_up)
    hidden = (jax.nn.silu(both[..., :width]) * both[..., width:]).astype(jnp.bfloat16)
    return (values + product(hidden, down), (normed, both, hidden))


def ffn_backward(values, grad, weights, kept):
    gain, gate_up, down = weights
    normed, both, hidden = kept
    width = down.shape[0]
    grad_low = grad.astype(jnp.bfloat16)
    grad_down = outer(hidden, grad_low)
    grad_hidden = product_back(grad_low, down)

    def ffn_gating(pair):
        return jax.nn.silu(pair[..., :width]) * pair[..., width:]

    unused, gating_back = jax.vjp(ffn_gating, both)
    grad_both = gating_back(grad_hidden)[0].astype(jnp.bfloat16)
    grad_gate_up = outer(normed, grad_both)
    grad_normed = product_back(grad_both, gate_up)
    unused, norm_back = jax.vjp(rms_gain, values, gain.astype(jnp.float32))
    grad_values, grad_gain = norm_back(grad_normed)
    return (grad + grad_values, (grad_gain, grad_gate_up, grad_down))


def convolve(before, inner, conv_weight, conv_bias):
    group = inner.shape[1]
    padded = jnp.concatenate([before, inner], axis=1)
    total = conv_bias
    for index in range(CONV):
        total = total + conv_weight[index] * padded[:, index : index + group]
    return jax.nn.silu(total)


def recurrence(decay):

    def advance(carry, slot):
        mixed_now, step_now, input_now, output_now = slot
        carry = (
            jnp.exp(step_now[:, None, :] * decay) * carry
            + (step_now * mixed_now)[:, None, :] * input_now[:, :, None]
        )
        return (carry, jnp.sum(output_now[:, :, None] * carry, axis=1))

    return advance


def selective(mixed, step, inputs_b, outputs_c, decay, state):
    slots = tuple((jnp.moveaxis(item, 1, 0) for item in (mixed, step, inputs_b, outputs_c)))
    state_end, core = lax.scan(recurrence(decay), state, slots, unroll=8)
    return (jnp.moveaxis(core, 0, 1), state_end)


def chain(earlier, later):
    return (earlier[0] * later[0], later[0] * earlier[1] + later[1])


def chain_both(earlier, later):
    return (
        earlier[0] * later[0],
        later[0] * earlier[1] + later[1],
        earlier[2] * later[2],
        earlier[2] * later[3] + earlier[3],
    )


def stepping(pre, step_bias, valid):
    return jax.nn.softplus(pre + step_bias) * valid[..., None]


def mamba_forward(values, lengths, carried_state, weights):
    (
        gain,
        mamba_in,
        conv_weight,
        conv_bias,
        selection,
        step_proj,
        step_bias,
        decay_log,
        skip_gain,
        mamba_out,
    ) = weights
    rows, group, width = values.shape
    inner_width = mamba_out.shape[0]
    rank = step_proj.shape[0]
    states = decay_log.shape[0]
    shard = lax.axis_index("seq")
    positions = shard * group + jnp.arange(group)
    valid = (positions[None, :] < lengths[:, None]).astype(jnp.float32)
    normed = rms_gain(values, gain.astype(jnp.float32)).astype(jnp.bfloat16)
    projected = product(normed, mamba_in)
    inner = projected[..., :inner_width]
    gate = projected[..., inner_width:]
    before = shifted(inner[:, group - CONV + 1 :], "seq", 1)
    mixed = convolve(before, inner, conv_weight.astype(jnp.float32), conv_bias.astype(jnp.float32))
    mixed_low = mixed.astype(jnp.bfloat16)
    select = product(mixed_low, selection)
    step_low = select[..., :rank].astype(jnp.bfloat16)
    inputs_b = select[..., rank : rank + states]
    outputs_c = select[..., rank + states :]
    pre = product(step_low, step_proj)
    step = stepping(pre, step_bias.astype(jnp.float32), valid)
    decay = -jnp.exp(decay_log.astype(jnp.float32))
    empty = jnp.zeros((rows, states, inner_width), jnp.float32)
    local_end = selective(mixed, step, inputs_b, outputs_c, decay, empty)[1]
    through = jnp.exp(decay * jnp.sum(step, axis=1)[:, None, :])
    prefix_decay, prefix_state = carried_in(
        (through, local_end), "seq", chain, (jnp.ones_like(through), empty), False
    )
    state = prefix_decay * carried_state + prefix_state
    core, state_end = selective(mixed, step, inputs_b, outputs_c, decay, state)
    mixed_out = core + skip_gain.astype(jnp.float32) * mixed
    gated = (mixed_out * jax.nn.silu(gate)).astype(jnp.bfloat16)
    kept = (
        valid,
        normed,
        projected,
        before,
        mixed,
        mixed_low,
        step_low,
        pre,
        step,
        inputs_b,
        outputs_c,
        decay,
        state,
        through,
        prefix_decay,
        mixed_out,
        gated,
        local_end,
        state_end,
    )
    return (values + product(gated, mamba_out), kept)


def mamba_backward(values, grad, weights, kept):
    (
        gain,
        mamba_in,
        conv_weight,
        conv_bias,
        selection,
        step_proj,
        step_bias,
        decay_log,
        skip_gain,
        mamba_out,
    ) = weights
    (
        valid,
        normed,
        projected,
        before,
        mixed,
        mixed_low,
        step_low,
        pre,
        step,
        inputs_b,
        outputs_c,
        decay,
        state,
        through,
        prefix_decay,
        mixed_out,
        gated,
        local_end,
        state_end,
    ) = kept
    group = values.shape[1]
    inner_width = mamba_out.shape[0]
    grad_low = grad.astype(jnp.bfloat16)
    grad_out = outer(gated, grad_low)
    grad_gated = product_back(grad_low, mamba_out)
    gate = projected[..., inner_width:]

    def mamba_gating(mixed_part, gate_part):
        return mixed_part * jax.nn.silu(gate_part)

    unused, gating_back = jax.vjp(mamba_gating, mixed_out, gate)
    grad_mixed_out, grad_gate = gating_back(grad_gated)
    skip = skip_gain.astype(jnp.float32)
    grad_skip = jnp.sum(grad_mixed_out * mixed, axis=(0, 1))
    unused, scan_back = jax.vjp(selective, mixed, step, inputs_b, outputs_c, decay, state)
    zero = jnp.zeros_like(state)
    ones = jnp.ones_like(state)
    own = scan_back((grad_mixed_out, zero))[5]
    suffix = carried_in(
        (through, own, through, local_end), "seq", chain_both, (ones, zero, ones, zero), True
    )
    final = suffix[2] * state_end + suffix[3]
    piece_width = inner_width // lax.axis_size("seq")
    new_state = lax.dynamic_slice_in_dim(final, lax.axis_index("seq") * piece_width, piece_width, 2)
    grad_state = lax.psum_scatter(prefix_decay * own, "seq", scatter_dimension=2, tiled=True)
    grad_mixed, grad_step, grad_inputs, grad_outputs, grad_decay, unused_state = scan_back(
        (grad_mixed_out, suffix[1])
    )
    grad_mixed = grad_mixed + grad_mixed_out * skip
    unused, step_back = jax.vjp(
        lambda pre_part, bias_part: stepping(pre_part, bias_part, valid),
        pre,
        step_bias.astype(jnp.float32),
    )
    grad_pre, grad_step_bias = step_back(grad_step)
    grad_pre_low = grad_pre.astype(jnp.bfloat16)
    grad_step_proj = outer(step_low, grad_pre_low)
    grad_step_low = product_back(grad_pre_low, step_proj)
    grad_select = jnp.concatenate([grad_step_low, grad_inputs, grad_outputs], axis=-1).astype(
        jnp.bfloat16
    )
    grad_selection = outer(mixed_low, grad_select)
    grad_mixed = grad_mixed + product_back(grad_select, selection)
    inner = projected[..., :inner_width]
    unused, conv_back = jax.vjp(
        convolve, before, inner, conv_weight.astype(jnp.float32), conv_bias.astype(jnp.float32)
    )
    grad_before, grad_inner, grad_conv_weight, grad_conv_bias = conv_back(grad_mixed)
    returned = shifted(grad_before, "seq", -1)
    grad_inner = jnp.concatenate(
        [grad_inner[:, : group - CONV + 1], grad_inner[:, group - CONV + 1 :] + returned], axis=1
    )
    grad_projected = jnp.concatenate([grad_inner, grad_gate], axis=-1).astype(jnp.bfloat16)
    grad_in = outer(normed, grad_projected)
    grad_normed = product_back(grad_projected, mamba_in)
    unused, norm_back = jax.vjp(rms_gain, values, gain.astype(jnp.float32))
    grad_values, grad_gain = norm_back(grad_normed)
    grads = (
        grad_gain,
        grad_in,
        grad_conv_weight,
        grad_conv_bias,
        grad_selection,
        grad_step_proj,
        grad_step_bias,
        grad_decay * decay,
        grad_skip,
        grad_out,
    )
    return (grad + grad_values, grads, grad_state, new_state)


def key_positions(start, count, cache_rows, group):
    index = start + jnp.arange(count)
    owner = index // (cache_rows + group)
    offset = index % (cache_rows + group)
    return jnp.where(
        offset < cache_rows,
        owner * cache_rows + offset - WINDOW,
        owner * group + offset - cache_rows,
    )


def visible(query_pos, key_pos, lengths):
    near = (key_pos[None, :] > query_pos[:, None] - WINDOW) & (
        key_pos[None, :] <= query_pos[:, None]
    )
    real = (key_pos[None, None, :] < lengths[:, None, None]) | (
        key_pos[None, None, :] == query_pos[None, :, None]
    )
    return (near[None] & real)[:, :, None, :]


def blockwise(step_fn, carry, piece, size):
    count = jax.tree.leaves(piece)[0].shape[1]
    blocks = count // size

    def split(item):
        return jnp.moveaxis(item.reshape((item.shape[0], blocks, size) + item.shape[2:]), 1, 0)

    def turn(inner, pair):
        return (step_fn(inner, pair[1], pair[0] * size), None)

    carry, unused = lax.scan(turn, carry, (jnp.arange(blocks), jax.tree.map(split, piece)))
    return carry


def over_keys(local_kv, fold, init):
    return fold(init, lax.all_gather(local_kv, "seq", axis=1, tiled=True), jnp.int32(0))


def attention_forward(values, lengths, carried_kv, weights):
    gain, qkv_proj, out_proj = weights
    rows, group, width = values.shape
    heads = width // HEAD_DIM
    cache_rows = carried_kv.shape[1]
    size = cache_rows + group
    scale = HEAD_DIM ** (-0.5)
    query_pos = lax.axis_index("seq") * group + jnp.arange(group)
    normed = rms_gain(values, gain.astype(jnp.float32)).astype(jnp.bfloat16)
    qkv = product(normed, qkv_proj).astype(jnp.bfloat16)
    queries = qkv[..., :width].reshape(rows, group, heads, HEAD_DIM)
    segment_kv = qkv[..., width:]
    local_kv = jnp.concatenate([carried_kv, segment_kv], axis=1)

    def one_block(carry, piece, start):
        count = piece.shape[1]
        inside = visible(query_pos, key_positions(start, count, cache_rows, group), lengths)

        def one_work(state):
            top, total, accum = state
            keys = piece[..., :width].reshape(rows, count, heads, HEAD_DIM)
            contents = piece[..., width:].reshape(rows, count, heads, HEAD_DIM)
            scores = (
                jnp.einsum("rqhd,rkhd->rqhk", queries, keys, preferred_element_type=jnp.float32)
                * scale
            )
            new_top = jnp.maximum(top, jnp.max(jnp.where(inside, scores, NEGATIVE), axis=-1))
            weights_now = jnp.exp(jnp.where(inside, scores - new_top[..., None], NEGATIVE))
            factor = jnp.exp(top - new_top)
            total = total * factor + jnp.sum(weights_now, axis=-1)
            accum = accum * factor[..., None] + jnp.einsum(
                "rqhk,rkhd->rqhd",
                weights_now.astype(jnp.bfloat16),
                contents,
                preferred_element_type=jnp.float32,
            )
            return (new_top, total, accum)

        return lax.cond(jnp.any(inside), one_work, lambda state: state, carry)

    init = (
        jnp.full((rows, group, heads), NEGATIVE, jnp.float32),
        jnp.zeros((rows, group, heads), jnp.float32),
        jnp.zeros((rows, group, heads, HEAD_DIM), jnp.float32),
    )
    top, total, accum = over_keys(
        local_kv, lambda carry, piece, start: blockwise(one_block, carry, piece, size), init
    )
    attended = accum / total[..., None]
    logsum = top + jnp.log(total)
    attended_low = attended.astype(jnp.bfloat16).reshape(rows, group, width)
    kept = (normed, queries, local_kv, attended, attended_low, logsum, query_pos)
    return (values + product(attended_low, out_proj), segment_kv, kept)


def attention_backward(values, grad, lengths, weights, kept):
    gain, qkv_proj, out_proj = weights
    normed, queries, local_kv, attended, attended_low, logsum, query_pos = kept
    rows, group, width = values.shape
    heads = width // HEAD_DIM
    size = local_kv.shape[1]
    cache_rows = size - group
    scale = HEAD_DIM ** (-0.5)
    grad_low = grad.astype(jnp.bfloat16)
    grad_out = outer(attended_low, grad_low)
    grad_attended = (
        product_back(grad_low, out_proj).astype(jnp.bfloat16).reshape(rows, group, heads, HEAD_DIM)
    )
    delta = jnp.sum(grad_attended.astype(jnp.float32) * attended, axis=-1)

    def query_block(carry, piece, start):
        count = piece.shape[1]
        inside = visible(query_pos, key_positions(start, count, cache_rows, group), lengths)

        def query_work(grad_queries):
            keys = piece[..., :width].reshape(rows, count, heads, HEAD_DIM)
            contents = piece[..., width:].reshape(rows, count, heads, HEAD_DIM)
            scores = (
                jnp.einsum("rqhd,rkhd->rqhk", queries, keys, preferred_element_type=jnp.float32)
                * scale
            )
            weights_now = jnp.exp(jnp.where(inside, scores - logsum[..., None], NEGATIVE))
            grad_weights = jnp.einsum(
                "rqhd,rkhd->rqhk", grad_attended, contents, preferred_element_type=jnp.float32
            )
            grad_scores = (weights_now * (grad_weights - delta[..., None])).astype(jnp.bfloat16)
            return (
                grad_queries
                + jnp.einsum(
                    "rqhk,rkhd->rqhd", grad_scores, keys, preferred_element_type=jnp.float32
                )
                * scale
            )

        return lax.cond(jnp.any(inside), query_work, lambda state: state, carry)

    grad_queries = over_keys(
        local_kv,
        lambda carry, piece, start: blockwise(query_block, carry, piece, size),
        jnp.zeros((rows, group, heads, HEAD_DIM), jnp.float32),
    )
    whole_logsum, whole_delta = (
        lax.all_gather(logsum, "seq", axis=1, tiled=True),
        lax.all_gather(delta, "seq", axis=1, tiled=True),
    )
    own_pos = key_positions(lax.axis_index("seq") * size, size, cache_rows, group)
    own_keys = local_kv[..., :width].reshape(rows, size, heads, HEAD_DIM)
    own_contents = local_kv[..., width:].reshape(rows, size, heads, HEAD_DIM)

    def key_block(carry, piece, start):
        part_queries, part_grads = piece
        count = part_queries.shape[1]
        inside = visible(start + jnp.arange(count), own_pos, lengths)

        def key_work(state):
            grad_keys, grad_contents = state
            part_logsum = lax.dynamic_slice_in_dim(whole_logsum, start, count, 1)
            part_delta = lax.dynamic_slice_in_dim(whole_delta, start, count, 1)
            scores = (
                jnp.einsum(
                    "rqhd,rkhd->rqhk", part_queries, own_keys, preferred_element_type=jnp.float32
                )
                * scale
            )
            weights_now = jnp.exp(jnp.where(inside, scores - part_logsum[..., None], NEGATIVE))
            grad_contents = grad_contents + jnp.einsum(
                "rqhk,rqhd->rkhd",
                weights_now.astype(jnp.bfloat16),
                part_grads,
                preferred_element_type=jnp.float32,
            )
            grad_weights = jnp.einsum(
                "rqhd,rkhd->rqhk", part_grads, own_contents, preferred_element_type=jnp.float32
            )
            grad_scores = (weights_now * (grad_weights - part_delta[..., None])).astype(
                jnp.bfloat16
            )
            grad_keys = (
                grad_keys
                + jnp.einsum(
                    "rqhk,rqhd->rkhd", grad_scores, part_queries, preferred_element_type=jnp.float32
                )
                * scale
            )
            return (grad_keys, grad_contents)

        return lax.cond(jnp.any(inside), key_work, lambda state: state, carry)

    empty = jnp.zeros((rows, size, heads, HEAD_DIM), jnp.float32)
    grad_keys, grad_contents = blockwise(
        key_block,
        (empty, empty),
        (
            lax.all_gather(queries, "seq", axis=1, tiled=True),
            lax.all_gather(grad_attended, "seq", axis=1, tiled=True),
        ),
        group,
    )
    grad_local = jnp.concatenate(
        [grad_keys.reshape(rows, size, width), grad_contents.reshape(rows, size, width)], axis=-1
    )
    grad_cache = grad_local[:, :cache_rows]
    grad_qkv = jnp.concatenate(
        [grad_queries.reshape(rows, group, width), grad_local[:, cache_rows:]], axis=-1
    ).astype(jnp.bfloat16)
    grad_qkv_proj = outer(normed, grad_qkv)
    grad_normed = product_back(grad_qkv, qkv_proj)
    unused, norm_back = jax.vjp(rms_gain, values, gain.astype(jnp.float32))
    grad_values, grad_gain = norm_back(grad_normed)
    return (grad + grad_values, (grad_gain, grad_qkv_proj, grad_out), grad_cache)


def local(
    activations,
    cotangent,
    carried_state,
    carried_kv,
    row_lengths,
    mamba_gain,
    mamba_in,
    conv_weight,
    conv_bias,
    selection,
    step_proj,
    step_bias,
    decay_log,
    skip_gain,
    mamba_out,
    first_gain,
    first_gate_up,
    first_down,
    attention_gain,
    attention_qkv,
    attention_out,
    second_gain,
    second_gate_up,
    second_down,
):
    front_shards = (
        mamba_gain,
        mamba_in,
        conv_weight,
        conv_bias,
        selection,
        step_proj,
        step_bias,
        decay_log,
        skip_gain,
        mamba_out,
        first_gain,
        first_gate_up,
        first_down,
    )
    rear_shards = (
        attention_gain,
        attention_qkv,
        attention_out,
        second_gain,
        second_gate_up,
        second_down,
    )
    stream = activations.astype(jnp.float32)
    front_whole = fetch_front(front_shards)
    first_stream, mamba_kept = mamba_forward(stream, row_lengths, carried_state, front_whole[:10])
    second_stream, first_kept = ffn_forward(first_stream, front_whole[10:])
    rear_whole = fetch_rear(rear_shards)
    third_stream, segment_kv, attention_kept = attention_forward(
        second_stream, row_lengths, carried_kv, rear_whole[:3]
    )
    fourth_stream, second_kept = ffn_forward(third_stream, rear_whole[3:])
    grad = cotangent.astype(jnp.float32)
    rear_back = fetch_rear(rear_shards)
    grad, second_grads = ffn_backward(third_stream, grad, rear_back[3:], second_kept)
    grad, attention_grads, grad_cache = attention_backward(
        second_stream, grad, row_lengths, rear_back[:3], attention_kept
    )
    rear_grads = settle_rear(attention_grads + second_grads)
    front_back = fetch_front(front_shards)
    grad, first_grads = ffn_backward(first_stream, grad, front_back[10:], first_kept)
    grad, mamba_grads, grad_state, new_state = mamba_backward(
        stream, grad, front_back[:10], mamba_kept
    )
    front_grads = settle_front(mamba_grads + first_grads)
    return (
        fourth_stream.astype(jnp.bfloat16),
        new_state,
        segment_kv,
        grad,
        grad_state,
        grad_cache,
        front_grads[0],
        front_grads[1],
        front_grads[2],
        front_grads[3],
        front_grads[4],
        front_grads[5],
        front_grads[6],
        front_grads[7],
        front_grads[8],
        front_grads[9],
        front_grads[10],
        front_grads[11],
        front_grads[12],
        rear_grads[0],
        rear_grads[1],
        rear_grads[2],
        rear_grads[3],
        rear_grads[4],
        rear_grads[5],
    )


EVERY = ("u", "c", "y", "x", "v")
PLANE = ("y", "x", "c")
SQUARES = ("u", "v")
BF = jnp.bfloat16
F32 = jnp.float32


def params(**more):
    return pltpu.CompilerParams(vmem_limit_bytes=32 * 2**20, **more)


def bit_route(move):
    route = []
    for place in range(2 ** len(EVERY)):
        bits = [place >> (len(EVERY) - 1 - k) & 1 for k in range(len(EVERY))]
        goal = 0
        for bit in move(*bits):
            goal = 2 * goal + bit
        if goal != place:
            route.append((place, goal))
    return route


def swap_planes(block):
    away = lax.axis_index("c") != lax.axis_index("v")
    route = bit_route(lambda u, c, y, x, v: (u, v, y, x, c))
    return jnp.where(away, lax.ppermute(block, EVERY, route), block)


def other(block, axis):
    return lax.ppermute(block, axis, [(0, 1), (1, 0)])


def gather_line(block):
    from_y = other(block, "y")
    return jnp.stack([block, other(block, "x"), from_y, other(from_y, "x")])


def gather_plane(block):
    own = gather_line(block)
    return jnp.concatenate([own, other(own, "c")], axis=0)


def scatter_line(mine, kind):
    to_y = (mine[2] + other(mine[3].astype(kind), "x").astype(F32)).astype(kind)
    from_x = other(mine[1].astype(kind), "x").astype(F32)
    return mine[0] + from_x + other(to_y, "y").astype(F32)


def scatter_plane(parts):
    half = parts.shape[0] // 2
    mine = parts[:half].astype(F32) + other(parts[half:], "c").astype(F32)
    return scatter_line(mine, parts.dtype)


def sum_plane(parts):
    return gather_plane(scatter_plane(parts))


def trade(block, axes):
    return lax.all_to_all(block, axes, 0, 0, tiled=True)


def gather_small(block, axes):
    for axis in reversed(axes):
        block = in_order(block, other(block, axis), axis)
    return block


def total_small(block):
    for axis in EVERY:
        block = block + other(block, axis)
    return block


def pair_sum(parts, axis):
    here = lax.axis_index(axis)
    theirs = other(lax.dynamic_index_in_dim(parts, 1 - here, 0, False), axis)
    mine = lax.dynamic_index_in_dim(parts, here, 0, False)
    return mine.astype(F32) + theirs.astype(F32)


def reduce_squares(parts):
    return lax.psum_scatter(parts, SQUARES, scatter_dimension=0)


def gather_squares(block):
    return lax.all_gather(block, SQUARES, axis=0)


def settle(stage, *pieces):
    return lax.optimization_barrier((stage,) + pieces)


def tie(value, *stages):
    return lax.optimization_barrier((value,) + stages)[0]


def in_order(mine, theirs, axis):
    first = lax.axis_index(axis) == 0
    return jnp.stack([jnp.where(first, mine, theirs), jnp.where(first, theirs, mine)])


def kv_owners(parts):
    for axis in PLANE:
        lead = parts.ndim - {"y": 6, "x": 5, "c": 4}[axis]
        stay = lax.index_in_dim(parts, 0, lead, False)
        leave = lax.index_in_dim(parts, 1, lead, False)
        parts = in_order(stay, other(leave, axis), axis)
    side, y_size, c_size, two, count, width = parts.shape
    return parts.transpose(0, 4, 3, 2, 1, 5).reshape(side, count, two * y_size * c_size * width)


def rows_gather(block):
    here = lax.axis_index("c")
    mine = lax.dynamic_index_in_dim(block, here, 0, False)
    theirs = lax.dynamic_index_in_dim(block, 1 - here, 0, False)
    return gather_line(jnp.stack([mine, other(theirs, "c")]))


def rows_scatter(parts):
    parts = parts.reshape((4, 2) + parts.shape[1:])
    pair = scatter_line(parts.astype(F32), parts.dtype)
    return in_order(pair[0], other(pair[1].astype(parts.dtype), "c").astype(F32), "c")


def rows_of(gathered):
    squares, members, rows, width = gathered.shape
    split = gathered.reshape(2, 2, members // 2, 2, rows, width)
    return split.transpose(0, 3, 2, 1, 4, 5).reshape(squares * members * rows, width)


def by_square(grad):
    total, width = grad.shape
    split = grad.reshape(2, 2, 4, 2, total // 32, width).transpose(0, 3, 2, 1, 4, 5)
    return split.reshape(4, 8, total // 32, width)


def relocate(block, back):
    route = bit_route(lambda u, c, y, x, v: (x, y, u, c, v))
    moving = jnp.zeros((2 ** len(EVERY),), bool).at[jnp.array([place for place, goal in route])].set(True)
    here = lax.axis_index(EVERY)
    moved = lax.ppermute(block, EVERY, [(goal, place) for place, goal in route] if back else route)
    return jnp.where(moving[here], moved, block)


def dot(left, right, left_dim, right_dim):
    return lax.dot_general(
        left, right, (((left_dim,), (right_dim,)), ((), ())), preferred_element_type=F32
    )


def conv_body(order, inner_ref, taps_ref, bias_ref, total_ref, mixed_ref, low_ref, held):
    step = pl.program_id(0)
    rows, group = inner_ref.shape[1], inner_ref.shape[2]

    @pl.when(step == 0)
    def clear():
        held[:, :8] = jnp.zeros_like(held[:, :8])

    @pl.when(step > 0)
    def keep():
        held[:, :8] = held[:, group:]

    for row in range(rows):
        held[row, 8:] = inner_ref[0, row]
        total = bias_ref[...] + taps_ref[0:1] * held[row, 5 : 5 + group]
        for tap in range(1, CONV):
            total = total + taps_ref[tap : tap + 1] * held[row, 5 + tap : 5 + tap + group]
        mixed = total / (1.0 + jnp.exp(-total))
        total_ref[0, row] = total
        mixed_ref[0, row] = mixed
        low_ref[0, row] = mixed.astype(BF)


def conv_forward(order, projected, taps, bias):
    blocks, rows, group, width = projected.shape
    spec = pl.BlockSpec((1, rows, group, width), lambda i, order: (order[i], 0, 0, 0))
    shape = (blocks, rows, group, width)
    return pl.pallas_call(
        conv_body,
        grid_spec=pltpu.PrefetchScalarGridSpec(
            num_scalar_prefetch=1,
            grid=(blocks,),
            in_specs=[
                spec,
                pl.BlockSpec((CONV, width), lambda i, order: (0, 0)),
                pl.BlockSpec((1, width), lambda i, order: (0, 0)),
            ],
            out_specs=[spec, spec, spec],
            scratch_shapes=[pltpu.VMEM((rows, group + 8, width), F32)],
        ),
        out_shape=[
            jax.ShapeDtypeStruct(shape, F32),
            jax.ShapeDtypeStruct(shape, F32),
            jax.ShapeDtypeStruct(shape, BF),
        ],
        compiler_params=params(),
        name="conv_forward",
    )(order, projected, taps, bias)


def conv_back_body(order, grad_ref, total_ref, inner_ref, taps_ref, out_ref, sums_ref, held):
    step = pl.program_id(0)
    rows, group = inner_ref.shape[1], inner_ref.shape[2]

    @pl.when(step == 0)
    def clear():
        held[:, group:] = jnp.zeros_like(held[:, group:])
        sums_ref[...] = jnp.zeros_like(sums_ref)

    @pl.when(step > 0)
    def keep():
        held[:, group:] = held[:, :8]

    for row in range(rows):
        total = total_ref[0, row]
        sig = 1.0 / (1.0 + jnp.exp(-total))
        grad = grad_ref[0, row] * (sig * (1.0 + total * (1.0 - sig)))
        held[row, :group] = grad
        inner = inner_ref[0, row]
        back = None
        for tap in range(CONV):
            later = held[row, CONV - 1 - tap : CONV - 1 - tap + group]
            part = taps_ref[tap : tap + 1] * later
            back = part if back is None else back + part
            sums_ref[tap : tap + 1] += jnp.sum(inner * later, axis=0, keepdims=True)
        sums_ref[CONV : CONV + 1] += jnp.sum(grad, axis=0, keepdims=True)
        out_ref[0, row] = back.astype(BF)


def conv_back(order, grad, total, projected, taps):
    blocks, rows, group, width = grad.shape
    spec = pl.BlockSpec(
        (1, rows, group, width), lambda i, order: (order[blocks - 1 - i], 0, 0, 0)
    )
    return pl.pallas_call(
        conv_back_body,
        grid_spec=pltpu.PrefetchScalarGridSpec(
            num_scalar_prefetch=1,
            grid=(blocks,),
            in_specs=[spec, spec, spec, pl.BlockSpec((CONV, width), lambda i, order: (0, 0))],
            out_specs=[spec, pl.BlockSpec((8, width), lambda i, order: (0, 0))],
            scratch_shapes=[pltpu.VMEM((rows, group + 8, width), F32)],
        ),
        out_shape=[
            jax.ShapeDtypeStruct(grad.shape, BF),
            jax.ShapeDtypeStruct((8, width), F32),
        ],
        compiler_params=params(),
        name="conv_back",
    )(order, grad, total, projected, taps)


def widen(tile, width):
    return jnp.concatenate([tile] * (width // 128), axis=1)


def narrow(tile):
    total = tile[:, :128]
    for start in range(128, tile.shape[1], 128):
        total = total + tile[:, start : start + 128]
    return total


def scan_body(
    order, mixed_ref, step_ref, b_ref, c_ref, decay_ref, start_ref, core_ref, past_ref, end_ref, held
):
    @pl.when(pl.program_id(0) == 0)
    def begin():
        held[...] = start_ref[...]

    decay = decay_ref[...]
    rows, group, width = mixed_ref.shape[1:]

    def eight(turn, states):
        base = pl.multiple_of(turn * 8, 8)
        states = list(states)
        steps = [step_ref[0, row, pl.ds(base, 8), :] for row in range(rows)]
        drives = [steps[row] * mixed_ref[0, row, pl.ds(base, 8), :] for row in range(rows)]
        cores = [[] for row in range(rows)]
        for k in range(8):
            for row in range(rows):
                past_ref[0, row, base + k] = states[row]
                fade = jnp.exp(steps[row][k : k + 1] * decay)
                state = fade * states[row] + drives[row][k : k + 1] * widen(
                    b_ref[0, row, base + k], width
                )
                states[row] = state
                seen = widen(c_ref[0, row, base + k], width) * state
                cores[row].append(jnp.sum(seen, axis=0, keepdims=True))
        for row in range(rows):
            core_ref[0, row, pl.ds(base, 8), :] = jnp.concatenate(cores[row], axis=0)
        return tuple(states)

    states = lax.fori_loop(0, group // 8, eight, tuple(held[row] for row in range(rows)))
    for row in range(rows):
        held[row] = states[row]
        end_ref[row] = states[row]


def scan_forward(order, mixed, step, wide_b, wide_c, decay, start):
    blocks, rows, group, width = mixed.shape
    states = decay.shape[0]
    spec = pl.BlockSpec((1, rows, group, width), lambda i, order: (order[i], 0, 0, 0))
    maps = pl.BlockSpec((1, rows, group, states, 128), lambda i, order: (order[i], 0, 0, 0, 0))
    whole = pl.BlockSpec((rows, states, width), lambda i, order: (0, 0, 0))
    return pl.pallas_call(
        scan_body,
        grid_spec=pltpu.PrefetchScalarGridSpec(
            num_scalar_prefetch=1,
            grid=(blocks,),
            in_specs=[
                spec,
                spec,
                maps,
                maps,
                pl.BlockSpec((states, width), lambda i, order: (0, 0)),
                whole,
            ],
            out_specs=[
                spec,
                pl.BlockSpec(
                    (1, rows, group, states, width), lambda i, order: (order[i], 0, 0, 0, 0)
                ),
                whole,
            ],
            scratch_shapes=[pltpu.VMEM((rows, states, width), F32)],
        ),
        out_shape=[
            jax.ShapeDtypeStruct(mixed.shape, F32),
            jax.ShapeDtypeStruct((blocks, rows, group, states, width), F32),
            jax.ShapeDtypeStruct(start.shape, F32),
        ],
        compiler_params=params(),
        name="scan_forward",
    )(order, mixed, step, wide_b, wide_c, decay, start)


def scan_back_body(
    order,
    mixed_ref,
    step_ref,
    b_ref,
    c_ref,
    grad_ref,
    past_ref,
    decay_ref,
    end_ref,
    dmixed_ref,
    dstep_ref,
    db_ref,
    dc_ref,
    ddecay_ref,
    dstart_ref,
    held,
    after,
):
    @pl.when(pl.program_id(0) == 0)
    def begin():
        held[...] = jnp.zeros_like(held)
        after[...] = end_ref[...]
        ddecay_ref[...] = jnp.zeros_like(ddecay_ref)

    decay = decay_ref[...]
    rows, group, width = mixed_ref.shape[1:]
    turns = group // 8

    def eight(turn, carry):
        base = pl.multiple_of((turns - 1 - turn) * 8, 8)
        backs, states, sums = list(carry[0]), list(carry[1]), carry[2]
        steps = [step_ref[0, row, pl.ds(base, 8), :] for row in range(rows)]
        inputs = [mixed_ref[0, row, pl.ds(base, 8), :] for row in range(rows)]
        grads = [grad_ref[0, row, pl.ds(base, 8), :] for row in range(rows)]
        drives = [steps[row] * inputs[row] for row in range(rows)]
        firsts = [[None] * 8 for row in range(rows)]
        seconds = [[None] * 8 for row in range(rows)]
        for k in reversed(range(8)):
            for row in range(rows):
                now = steps[row][k : k + 1]
                grad = grads[row][k : k + 1]
                past = past_ref[0, row, base + k]
                fade = jnp.exp(now * decay)
                back = widen(c_ref[0, row, base + k], width) * grad + backs[row]
                dc_ref[0, row, base + k] = narrow(states[row] * grad).astype(BF)
                firsts[row][k] = jnp.sum(
                    widen(b_ref[0, row, base + k], width) * back, axis=0, keepdims=True
                )
                db_ref[0, row, base + k] = narrow(back * drives[row][k : k + 1]).astype(BF)
                faded = fade * back
                flow = faded * past
                seconds[row][k] = jnp.sum(flow * decay, axis=0, keepdims=True)
                sums = sums + flow * now
                backs[row] = faded
                states[row] = past
        for row in range(rows):
            first = jnp.concatenate(firsts[row], axis=0)
            second = jnp.concatenate(seconds[row], axis=0)
            dmixed_ref[0, row, pl.ds(base, 8), :] = steps[row] * first
            dstep_ref[0, row, pl.ds(base, 8), :] = inputs[row] * first + second
        return (tuple(backs), tuple(states), sums)

    backs, states, sums = lax.fori_loop(
        0,
        turns,
        eight,
        (
            tuple(held[row] for row in range(rows)),
            tuple(after[row] for row in range(rows)),
            ddecay_ref[...],
        ),
    )
    ddecay_ref[...] = sums
    for row in range(rows):
        held[row] = backs[row]
        after[row] = states[row]
        dstart_ref[row] = backs[row]


def scan_back(order, mixed, step, wide_b, wide_c, grad, past, decay, end):
    blocks, rows, group, width = mixed.shape
    states = decay.shape[0]
    last = blocks - 1
    spec = pl.BlockSpec((1, rows, group, width), lambda i, order: (order[last - i], 0, 0, 0))
    maps = pl.BlockSpec(
        (1, rows, group, states, 128), lambda i, order: (order[last - i], 0, 0, 0, 0)
    )
    kept = pl.BlockSpec(
        (1, rows, group, states, width), lambda i, order: (order[last - i], 0, 0, 0, 0)
    )
    whole = pl.BlockSpec((rows, states, width), lambda i, order: (0, 0, 0))
    rates = pl.BlockSpec((states, width), lambda i, order: (0, 0))
    return pl.pallas_call(
        scan_back_body,
        grid_spec=pltpu.PrefetchScalarGridSpec(
            num_scalar_prefetch=1,
            grid=(blocks,),
            in_specs=[spec, spec, maps, maps, spec, kept, rates, whole],
            out_specs=[spec, spec, maps, maps, rates, whole],
            scratch_shapes=[
                pltpu.VMEM((rows, states, width), F32),
                pltpu.VMEM((rows, states, width), F32),
            ],
        ),
        out_shape=[
            jax.ShapeDtypeStruct(mixed.shape, F32),
            jax.ShapeDtypeStruct(mixed.shape, F32),
            jax.ShapeDtypeStruct((blocks, rows, group, states, 128), BF),
            jax.ShapeDtypeStruct((blocks, rows, group, states, 128), BF),
            jax.ShapeDtypeStruct(decay.shape, F32),
            jax.ShapeDtypeStruct(end.shape, F32),
        ],
        compiler_params=params(),
        name="scan_back",
    )(order, mixed, step, wide_b, wide_c, grad, past, decay, end)


def own_positions(shape, axis, first, member, group):
    index = first + lax.broadcasted_iota(jnp.int32, shape, axis)
    slot = index // group
    block = slot ^ member
    return block * group + index % group


def seen_cache(query, place, shape, group):
    index = lax.broadcasted_iota(jnp.int32, shape, 1)
    return (index + place * group) > query


def seen_own(query, key, length):
    return (key <= query) & ((key < length) | (key == query))


def attend_body(meta_ref, q_ref, ck_ref, cv_ref, k_ref, v_ref, out_ref, log_ref):
    count = q_ref.shape[0]
    first = pl.program_id(1) * count
    scale = HEAD_DIM ** (-0.5)
    queries = q_ref[...]
    pieces = ck_ref.shape[0]
    size = ck_ref.shape[1]
    tokens = k_ref.shape[0]
    member = meta_ref[1]
    group = tokens // pieces
    query = own_positions((count, 1), 0, first, member, group)
    scores = []
    for piece in range(pieces):
        score = dot(queries, ck_ref[piece], 1, 1) * scale
        inside = seen_cache(query, piece, (1, size), size)
        scores.append(jnp.where(inside, score, NEGATIVE))
    score = dot(queries, k_ref[...], 1, 1) * scale
    key = own_positions((1, tokens), 1, 0, member, group)
    scores.append(jnp.where(seen_own(query, key, meta_ref[0]), score, NEGATIVE))
    top = jnp.max(scores[0], axis=1, keepdims=True)
    for score in scores[1:]:
        top = jnp.maximum(top, jnp.max(score, axis=1, keepdims=True))
    total = jnp.zeros_like(top)
    result = jnp.zeros((count, HEAD_DIM), F32)
    for piece, score in enumerate(scores):
        part = jnp.exp(score - top)
        total = total + jnp.sum(part, axis=1, keepdims=True)
        contents = cv_ref[piece] if piece < pieces else v_ref[...]
        result = result + dot(part.astype(BF), contents, 1, 0)
    out_ref[...] = result / total
    log_ref[0] = jnp.broadcast_to(top + jnp.log(total), (count, 128))


def attend(meta, qkv, cached_keys, cached_contents):
    tokens, width = qkv.shape
    width = width // 3
    heads = width // HEAD_DIM
    count = 256
    shards, group, unused = cached_keys.shape
    own = lambda base: pl.BlockSpec((tokens, HEAD_DIM), lambda h, i, meta: (0, base + h))
    held = pl.BlockSpec((shards, group, HEAD_DIM), lambda h, i, meta: (0, 0, h))
    block = pl.BlockSpec((count, HEAD_DIM), lambda h, i, meta: (i, h))
    return pl.pallas_call(
        attend_body,
        grid_spec=pltpu.PrefetchScalarGridSpec(
            num_scalar_prefetch=1,
            grid=(heads, tokens // count),
            in_specs=[block, held, held, own(heads), own(2 * heads)],
            out_specs=[block, pl.BlockSpec((1, count, 128), lambda h, i, meta: (h, i, 0))],
        ),
        out_shape=[
            jax.ShapeDtypeStruct((tokens, width), F32),
            jax.ShapeDtypeStruct((heads, tokens, 128), F32),
        ],
        compiler_params=params(),
        name="attend",
    )(meta, qkv, cached_keys, cached_contents, qkv, qkv)


def attend_back_body(
    meta_ref,
    q_ref,
    grad_ref,
    out_ref,
    log_ref,
    ck_ref,
    cv_ref,
    k_ref,
    v_ref,
    dck_ref,
    dcv_ref,
    dq_ref,
    dk_ref,
    dv_ref,
    total,
    delta,
):
    piece = pl.program_id(1)
    pieces = pl.num_programs(1) - 1
    scale = HEAD_DIM ** (-0.5)
    queries = q_ref[...]
    grad = grad_ref[...]
    count = queries.shape[0]
    size = ck_ref.shape[1]
    member = meta_ref[1]
    group = count // (2 * pieces)
    query = own_positions((count, 1), 0, 0, member, group)

    @pl.when(piece == 0)
    def begin():
        total[...] = jnp.zeros_like(total)
        mine = jnp.sum(grad.astype(F32) * out_ref[...], axis=1, keepdims=True)
        delta[...] = jnp.broadcast_to(mine, delta.shape)

    def work(keys, contents, inside):
        score = dot(queries, keys, 1, 1) * scale
        part = jnp.exp(score - log_ref[0][:, :1])
        if inside is not None:
            part = jnp.where(inside, part, 0.0)
        dcontents = dot(part.astype(BF), grad, 0, 0)
        slope = dot(grad, contents, 1, 1)
        dscore = (part * (slope - delta[:, :1])).astype(BF)
        total[...] += dot(dscore, keys, 1, 0) * scale
        return dot(dscore, queries, 0, 0) * scale, dcontents

    def cached(inside):
        keys = ck_ref[...].reshape(2 * size, HEAD_DIM)
        contents = cv_ref[...].reshape(2 * size, HEAD_DIM)
        dkeys, dcontents = work(keys, contents, inside)
        dck_ref[...] = dkeys.astype(BF).reshape(2, size, HEAD_DIM)
        dcv_ref[...] = dcontents.astype(BF).reshape(2, size, HEAD_DIM)

    edge = piece * 2 * size < count

    @pl.when((piece < pieces) & edge)
    def near():
        cached(seen_cache(query, 2 * piece, (1, 2 * size), size))

    @pl.when((piece < pieces) & jnp.logical_not(edge))
    def far():
        cached(None)

    @pl.when(piece == pieces)
    def own():
        key = own_positions((1, count), 1, 0, member, group)
        dkeys, dcontents = work(k_ref[...], v_ref[...], seen_own(query, key, meta_ref[0]))
        dk_ref[...] = dkeys.astype(BF)
        dv_ref[...] = dcontents.astype(BF)
        dq_ref[...] = total[...].astype(BF)


def attend_back(meta, qkv, grad, out, log, cached_keys, cached_contents):
    tokens, width = grad.shape
    heads = width // HEAD_DIM
    shards, group, unused = cached_keys.shape
    pieces = shards // 2
    own = lambda base: pl.BlockSpec((tokens, HEAD_DIM), lambda h, i, meta: (0, base + h))
    place = lambda i: jnp.minimum(i, pieces - 1)
    held = pl.BlockSpec((2, group, HEAD_DIM), lambda h, i, meta: (place(i), 0, h))
    result = jax.ShapeDtypeStruct((tokens, width), BF)
    return pl.pallas_call(
        attend_back_body,
        grid_spec=pltpu.PrefetchScalarGridSpec(
            num_scalar_prefetch=1,
            grid=(heads, pieces + 1),
            in_specs=[
                own(0),
                own(0),
                own(0),
                pl.BlockSpec((1, tokens, 128), lambda h, i, meta: (h, 0, 0)),
                held,
                held,
                own(heads),
                own(2 * heads),
            ],
            out_specs=[
                held,
                held,
                own(0),
                own(0),
                own(0),
            ],
            scratch_shapes=[
                pltpu.VMEM((tokens, HEAD_DIM), F32),
                pltpu.VMEM((tokens, 128), F32),
            ],
        ),
        out_shape=[jax.ShapeDtypeStruct(cached_keys.shape, BF)] * 2 + [result, result, result],
        compiler_params=params(),
        name="attend_back",
    )(meta, qkv, grad, out, log, cached_keys, cached_contents, qkv, qkv)


def assemble(gots, moves, shape):
    def body(*refs):
        out_ref = refs[-1]
        for (row, column), height, (which, member, left, width) in moves:
            part = refs[which][member, :, left : left + width].astype(F32)
            out_ref[row : row + height, column : column + width] = part

    return pl.pallas_call(
        body,
        out_shape=jax.ShapeDtypeStruct(shape, F32),
        compiler_params=params(),
        name="assemble",
    )(*gots)


def silu_slope(values):
    sig = jax.nn.sigmoid(values)
    return sig * (1.0 + values * (1.0 - sig))


def norm_back(values, gain, grad):
    back = jax.vjp(rms_gain, values, gain)[1](grad)
    return back


def ffn_gate(normed, gate_up):
    both = dot(normed, gate_up, 1, 0)
    width = both.shape[1] // 2
    return both, (jax.nn.silu(both[:, :width]) * both[:, width:]).astype(BF)


def ffn_gate_back(grad_hidden, both):
    width = both.shape[1] // 2
    gate, up = both[:, :width], both[:, width:]
    return jnp.concatenate(
        [grad_hidden * up * silu_slope(gate), grad_hidden * jax.nn.silu(gate)], axis=1
    ).astype(BF)


def plane_local(
    activations,
    cotangent,
    carried_state,
    carried_kv,
    row_lengths,
    mamba_gain,
    mamba_in,
    conv_weight,
    conv_bias,
    selection,
    step_proj,
    step_bias,
    decay_log,
    skip_gain,
    mamba_out,
    first_gain,
    first_gate_up,
    first_down,
    attention_gain,
    attention_qkv,
    attention_out,
    second_gain,
    second_gate_up,
    second_down,
):
    rows, group, wide = activations.shape
    planes, inner = lax.axis_size(SQUARES), lax.axis_size("c")
    members = planes * inner
    u, c, y, x, v = (lax.axis_index(name) for name in EVERY)
    member = (y * 2 + x) * inner + c
    place = (y * 2 + x) * inner + v
    offset = jnp.arange(members) ^ member
    order = (((offset & 1) << 2) | (offset >> 1)).astype(jnp.int32)
    shard = mamba_gain.shape[0]
    channels = skip_gain.shape[0]
    width = channels * planes
    rank = step_proj.shape[0]
    states = decay_log.shape[0]
    units = first_down.shape[0]
    head_width = wide // planes
    cache_rows = carried_kv.shape[1]

    def parts_of(product_of):
        return product_of.astype(BF).reshape(members, rows, group, wide)

    gains = jnp.stack([mamba_gain, first_gain, attention_gain, second_gain], axis=1)
    gains = jnp.pad(gains, ((0, 0), (0, 124)))
    payload = mamba_in.reshape(shard, 2, members, width).transpose(2, 0, 1, 3)
    spread = jnp.broadcast_to(gains[None], (members,) + gains.shape)
    payload = payload.reshape(members, shard, 2 * width)
    payload = jnp.concatenate([payload[:, :, :width], spread, payload[:, :, width:]], axis=2)
    dealt = trade(payload, PLANE)
    tokens = swap_planes(tie(activations, payload))
    stream = tokens.astype(F32)
    own_inner = rows_of(gather_squares(dealt[:, :, : width + 128]))
    gains = own_inner[:, width : width + 4].T.astype(F32)
    own_inner = own_inner[:, :width]
    normed = gather_plane(tokens).reshape(-1, wide).astype(F32)
    normed = rms_gain(normed, gains[0]).astype(BF)


    cuts = (selection.shape[1], rank, CONV, 1, 1, states, 1)
    packed = jnp.concatenate(
        [
            selection.astype(F32),
            step_proj.astype(F32).T,
            conv_weight.astype(F32).T,
            conv_bias.astype(F32)[:, None],
            step_bias[:, None],
            decay_log.T,
            skip_gain[:, None],
        ],
        axis=1,
    )
    packed = jnp.pad(packed, ((0, 0), (0, -packed.shape[1] % 128)))
    packed = gather_small(relocate(tie(packed, tokens), False), SQUARES).reshape(width, -1)
    starts = [sum(cuts[:index]) for index in range(len(cuts) + 1)]
    pieces = [packed[:, starts[index] : starts[index + 1]] for index in range(len(cuts))]
    own_selection = pieces[0].astype(BF)
    own_step_proj = pieces[1].astype(BF)
    taps = pieces[2].T
    tap_bias = pieces[3].T
    own_step_bias = pieces[4].T
    decay = -jnp.exp(pieces[5].T)
    skip = pieces[6].T
    moved = jnp.concatenate([mamba_out, attention_out], axis=0)
    moved = relocate(tie(moved, packed), False)
    own_out = gather_squares(moved[:channels]).reshape(width, wide)
    start = lax.dynamic_slice_in_dim(carried_state, place * width, width, 2)
    marks = jnp.broadcast_to(row_lengths.astype(F32)[:, None, None], (rows, 8, width))
    start = swap_planes(tie(jnp.concatenate([start, marks], axis=1), packed))
    lengths = start[:, states, 0].astype(jnp.int32)
    start = start[:, :states]
    own_gate = rows_of(gather_squares(tie(dealt[:, :, width + 128 :], normed)))

    def hidden_columns(gate_up):
        split = gate_up.reshape(shard, 2, 2, 2, 2, 2, 2, units)
        return split.transpose(4, 5, 3, 0, 1, 2, 6, 7).reshape(members, shard, -1)

    split = attention_qkv.reshape(shard, 3, planes, head_width).transpose(2, 0, 1, 3)
    split = jnp.broadcast_to(
        split.reshape(planes, 1, shard, 3 * head_width), (planes, inner, shard, 3 * head_width)
    )
    split = split.reshape(members, shard, 3 * head_width)
    dealt_first = trade(tie(hidden_columns(first_gate_up), normed), PLANE)
    own_first_down = gather_squares(first_down).reshape(-1, wide)

    def heads_of(block):
        return jnp.stack(
            [
                block[r, :, g * head_width : (g + 1) * head_width]
                for g in range(planes)
                for r in range(rows)
            ]
        )

    late_keys = swap_planes(tie(carried_kv[:, :, :wide], tokens))
    cached_keys = trade(tie(heads_of(late_keys), normed), PLANE)
    late = jnp.concatenate([carried_kv[:, :, wide:], cotangent.reshape(rows, -1, wide)], axis=1)
    late = swap_planes(tie(late, normed))

    inner_part = dot(normed, own_inner, 1, 0).reshape(members, rows, group, width)
    total, mixed, mixed_low = conv_forward(order, inner_part, taps, tap_bias)
    flat_low = mixed_low.reshape(-1, width)
    select = sum_plane(dot(flat_low, own_selection, 1, 0).reshape(members, rows, group, -1))
    gate = dot(normed, own_gate, 1, 0).reshape(members, rows, group, width)
    select, dealt_first, cached_keys, late = settle(select, dealt_first, cached_keys, late)
    step_low = select[..., :rank].astype(BF).reshape(-1, rank)
    pre = dot(step_low, own_step_proj, 1, 1).reshape(members, rows, group, width) + own_step_bias
    blocks = jnp.zeros((members,), jnp.int32).at[order].set(jnp.arange(members, dtype=jnp.int32))
    positions = blocks[:, None] * group + jnp.arange(group)[None, :]
    valid = (positions[:, None, :] < lengths[None, :, None]).astype(F32)[..., None]
    step = jax.nn.softplus(pre) * valid
    cached_contents = trade(tie(heads_of(late[:, :cache_rows]), step), PLANE)
    wide_shape = (members, rows, group, states, 128)
    wide_b = jnp.broadcast_to(select[..., rank : rank + states, None], wide_shape)
    wide_c = jnp.broadcast_to(select[..., rank + states :, None], wide_shape)
    core, past, end = scan_forward(order, mixed, step, wide_b, wide_c, decay, start)
    core, cached_contents = settle(core, cached_contents)
    own_first = rows_of(gather_squares(dealt_first))
    dealt_qkv = trade(tie(split, core), PLANE)
    rear = gather_squares(jnp.concatenate([moved[channels:], second_down], axis=0))
    mixed_out = core + skip * mixed
    gated = (mixed_out * jax.nn.silu(gate)).astype(BF).reshape(-1, width)
    first_stream = stream + scatter_plane(parts_of(dot(gated, own_out, 1, 0)))
    first_stream, dealt_qkv = settle(first_stream, dealt_qkv)
    own_qkv = rows_of(gather_squares(dealt_qkv))

    first_normed = gather_plane(rms_gain(first_stream, gains[1]).astype(BF)).reshape(-1, wide)
    dealt_second = trade(tie(hidden_columns(second_gate_up), first_normed), PLANE)
    first_both, first_hidden = ffn_gate(first_normed, own_first)
    second_stream = first_stream + scatter_plane(parts_of(dot(first_hidden, own_first_down, 1, 0)))

    second_stream, dealt_second = settle(second_stream, dealt_second)
    own_second = rows_of(gather_squares(dealt_second))

    def rows_parts(product_of):
        return product_of.astype(BF).reshape(members, group, wide)

    grad = late[:, cache_rows:].reshape(rows, group, wide)
    own_attention_out = rear[:, :shard]
    own_attention_out = in_order(own_attention_out, other(own_attention_out, "c"), "c")
    own_attention_out = own_attention_out.reshape(-1, wide)
    own_second_down = rear[:, shard:].reshape(-1, wide)
    length = jnp.concatenate([lax.dynamic_slice_in_dim(lengths, c, 1), member[None]])
    normed_rows = rows_gather(rms_gain(second_stream, gains[2]).astype(BF)).reshape(-1, wide)
    qkv = dot(normed_rows, own_qkv, 1, 0).astype(BF)
    grad_whole = gather_plane(tie(grad, qkv)).reshape(-1, wide)
    grad = grad.astype(F32)
    attended, log = attend(length, qkv, cached_keys, cached_contents)
    attended_low = attended.astype(BF)
    third_stream = second_stream + rows_scatter(rows_parts(dot(attended_low, own_attention_out, 1, 0)))
    own_kv = qkv[:, head_width:].reshape(members, group, 2, head_width).transpose(0, 2, 1, 3)
    own_kv = tie(own_kv, third_stream).reshape(2, 2, inner, 2, group, head_width)

    second_normed = gather_plane(rms_gain(third_stream, gains[3]).astype(BF)).reshape(-1, wide)
    second_both, second_hidden = ffn_gate(second_normed, own_second)
    second_parts = parts_of(dot(second_hidden, own_second_down, 1, 0))
    fourth_stream = third_stream + scatter_plane(second_parts)
    def hidden_back(got):
        moves = []
        for column in range(2 * planes * members):
            part, uu, cc, yx, vv = column >> 5, column >> 4 & 1, column >> 3 & 1, column >> 1 & 3, column & 1
            source = (0, yx * 2 + cc, ((part * 2 + uu) * 2 + vv) * units, units)
            moves.append(((0, column * units), shard, source))
        return assemble([got], moves, (shard, 2 * planes * members * units))

    def cache_back(part):
        part = part.reshape(planes, rows, cache_rows, head_width)
        return swap_planes(jnp.concatenate([part[g] for g in range(planes)], axis=2))

    grad_both = ffn_gate_back(dot(grad_whole, own_second_down, 1, 1), second_both)
    grad_normed = scatter_plane(parts_of(dot(grad_both, own_second, 1, 1)))
    second_columns = reduce_squares(by_square(dot(second_normed, grad_both, 0, 0).astype(BF)))
    second_rows = dot(second_hidden, grad_whole, 0, 0).astype(BF)
    grad_stream, second_gain_grad = norm_back(third_stream, gains[3], grad_normed)
    grad = grad + grad_stream

    grad_rows = rows_gather(grad.astype(BF)).reshape(-1, wide)
    grad_attended = dot(grad_rows, own_attention_out, 1, 1).astype(BF)
    own_kv = kv_owners(tie(own_kv, grad_attended))
    returned = swap_planes(jnp.concatenate([fourth_stream.astype(BF), own_kv], axis=2))
    output, segment_kv = returned[..., :wide], returned[..., wide:]
    back_keys, back_contents, dq, dk, dv = attend_back(
        length, qkv, grad_attended, attended, log, cached_keys, cached_contents
    )
    grad_qkv = jnp.concatenate([dq, dk, dv], axis=1)
    grad_normed = rows_scatter(rows_parts(dot(grad_qkv, own_qkv, 1, 1)))
    grad_stream, attention_gain_grad = norm_back(second_stream, gains[2], grad_normed)
    grad = grad + grad_stream
    grad, second_columns = settle(grad, second_columns)

    grad_out = dot(attended_low, grad_rows, 0, 0).astype(BF).reshape(inner, planes, shard, wide)
    grad_out = pair_sum(grad_out, "c").astype(BF)
    attention_out_grad = reduce_squares(grad_out)
    second_down_grad = reduce_squares(second_rows.reshape(planes, units, wide)).astype(F32)
    qkv_columns = reduce_squares(by_square(dot(normed_rows, grad_qkv, 0, 0).astype(BF)))

    grad_whole = gather_plane(grad.astype(BF)).reshape(-1, wide)
    grad_whole, second_down_grad = settle(grad_whole, second_down_grad)
    back_keys = trade(tie(back_keys, grad_whole), PLANE)
    grad_both = ffn_gate_back(dot(grad_whole, own_first_down, 1, 1), first_both)
    grad_normed = scatter_plane(parts_of(dot(grad_both, own_first, 1, 1)))
    first_columns = reduce_squares(by_square(dot(first_normed, grad_both, 0, 0).astype(BF)))
    first_rows = dot(first_hidden, grad_whole, 0, 0).astype(BF)
    grad_stream, first_gain_grad = norm_back(first_stream, gains[1], grad_normed)
    grad = grad + grad_stream
    grad, qkv_columns, attention_out_grad = settle(grad, qkv_columns, attention_out_grad)
    first_down_grad = reduce_squares(first_rows.reshape(planes, units, wide)).astype(F32)

    grad_whole = gather_plane(grad.astype(BF)).reshape(-1, wide)
    grad_whole, back_keys = settle(grad_whole, back_keys)
    back_keys = cache_back(back_keys)
    second_got = trade(tie(second_columns, grad_whole), PLANE)
    grad_gated = dot(grad_whole, own_out, 1, 1).reshape(mixed.shape)
    grad_core = grad_gated * jax.nn.silu(gate)
    grad_core, second_got = settle(grad_core, second_got)
    second_gate_up_grad = hidden_back(second_got)
    back_contents = trade(tie(back_contents, grad_core), PLANE)
    grad_gate = (grad_gated * mixed_out * silu_slope(gate)).astype(BF).reshape(-1, width)
    skip_grad = jnp.sum(grad_core * mixed, axis=(0, 1, 2))
    grad_mixed, grad_step, grad_b, grad_c, grad_decay, grad_start = scan_back(
        order, mixed, step, wide_b, wide_c, grad_core, past, decay, end
    )
    new_state, grad_state = swap_planes(jnp.stack([end, grad_start]))
    grad_out = dot(gated, grad_whole, 0, 0).astype(BF).reshape(planes, channels, wide)
    out_rows = reduce_squares(grad_out)
    gate_columns = reduce_squares(by_square(dot(normed, grad_gate, 0, 0).astype(BF)))
    grad_step, back_contents, first_columns, first_down_grad = settle(
        grad_step, back_contents, first_columns, first_down_grad
    )
    back_contents = cache_back(back_contents)
    got = trade(tie(qkv_columns, grad_step), PLANE)
    grad_pre = grad_step * valid * jax.nn.sigmoid(pre)
    step_bias_grad = jnp.sum(grad_pre, axis=(0, 1, 2))
    grad_pre = grad_pre.astype(BF).reshape(-1, width)
    step_proj_grad = dot(grad_pre, step_low, 0, 0)
    grad_low = dot(grad_pre, own_step_proj, 1, 0).reshape(members, rows, group, rank)
    grad_select = sum_plane(jnp.concatenate(
            [grad_low] + [jnp.sum(part.astype(F32), axis=-1) for part in (grad_b, grad_c)], axis=-1
        ))
    grad_select = grad_select.astype(BF).reshape(-1, rank + 2 * states)
    grad_select, got, gate_columns, out_rows, back_keys = settle(
        grad_select, got, gate_columns, out_rows, back_keys
    )
    got = jnp.sum(got.reshape(planes, inner, shard, -1).astype(F32), axis=1)
    moves = []
    for owner in range(planes):
        for part in range(3):
            source = (0, owner, part * head_width, head_width)
            moves.append(((0, part * wide + owner * head_width), shard, source))
    attention_qkv_grad = assemble([got], moves, (shard, 3 * wide))
    first_got = trade(tie(first_columns, grad_select), PLANE)
    selection_grad = dot(flat_low, grad_select, 0, 0)
    grad_mixed = (
        grad_mixed
        + grad_core * skip
        + dot(grad_select, own_selection, 1, 1).reshape(mixed.shape)
    )
    grad_inner, tap_sums = conv_back(order, grad_mixed, total, inner_part, taps)
    grad_inner, first_got = settle(grad_inner.reshape(-1, width), first_got)
    first_gate_up_grad = hidden_back(first_got)
    inner_columns = by_square(dot(normed, grad_inner, 0, 0).astype(BF))
    grad_inner = tie(grad_inner, inner_columns)
    inner_columns = reduce_squares(inner_columns)
    parts = dot(grad_inner, own_inner, 1, 1) + dot(grad_gate, own_gate, 1, 1)
    gate_columns = trade(tie(gate_columns, grad_inner), PLANE)
    moved = relocate(jnp.concatenate([out_rows, attention_out_grad], axis=0), True).astype(F32)
    mamba_out_grad, attention_out_grad = moved[:channels], moved[channels:]
    inner_columns = trade(inner_columns, PLANE)
    grad_normed = scatter_plane(parts_of(parts))
    grad_stream, mamba_gain_grad = norm_back(stream, gains[0], grad_normed)
    grad_input = swap_planes(grad + grad_stream)
    moves = []
    for which in range(2):
        for owner in range(members):
            column = (which * members + owner) * width
            moves.append(((0, column), shard, (which, owner, 0, width)))
    mamba_in_grad = assemble([inner_columns, gate_columns], moves, mamba_in.shape)
    packed = jnp.concatenate(
        [
            selection_grad,
            step_proj_grad,
            tap_sums[: CONV + 1].T,
            step_bias_grad[:, None],
            (grad_decay * decay).T,
            skip_grad[:, None],
        ],
        axis=1,
    )
    packed = jnp.pad(packed, ((0, 0), (0, -packed.shape[1] % 128)))
    packed = pair_sum(pair_sum(packed.reshape(2, 2, channels, -1), "u"), "v")
    packed = relocate(packed, True)
    pieces = [packed[:, starts[index] : starts[index + 1]] for index in range(len(cuts))]

    gain_grads = jnp.stack([mamba_gain_grad, first_gain_grad, attention_gain_grad, second_gain_grad])
    index = (u * 2 + c) * members + place
    gain_grads = lax.dynamic_slice_in_dim(total_small(gain_grads), index * shard, shard, 1)
    return (
        output,
        new_state,
        segment_kv,
        grad_input,
        grad_state,
        jnp.concatenate([back_keys, back_contents], axis=2).astype(F32),
        gain_grads[0],
        mamba_in_grad,
        pieces[2].T,
        pieces[3][:, 0],
        pieces[0],
        pieces[1].T,
        pieces[4][:, 0],
        pieces[5].T,
        pieces[6][:, 0],
        mamba_out_grad,
        gain_grads[1],
        first_gate_up_grad,
        first_down_grad,
        gain_grads[2],
        attention_qkv_grad,
        attention_out_grad,
        gain_grads[3],
        second_gate_up_grad,
        second_down_grad,
    )


def placements(dp, seq):
    every = dp + seq
    places = (
        P(dp, seq, None),
        P(dp, seq, None),
        P(dp, None, None),
        P(dp, seq, None),
        P(dp),
        P(every),
        P(every, None),
        P(None, every),
        P(every),
        P(every, None),
        P(None, every),
        P(every),
        P(None, every),
        P(every),
        P(every, None),
        P(every),
        P(every, None),
        P(every, None),
        P(every),
        P(every, None),
        P(every, None),
        P(every),
        P(every, None),
        P(every, None),

    )
    results = (
        P(dp, seq, None),
        P(dp, None, seq),
        P(dp, seq, None),
        P(dp, seq, None),
        P(dp, None, seq),
        P(dp, seq, None),
        P(every),
        P(every, None),
        P(None, every),
        P(every),
        P(every, None),
        P(None, every),
        P(every),
        P(None, every),
        P(every),
        P(every, None),
        P(every),
        P(every, None),
        P(every, None),
        P(every),
        P(every, None),
        P(every, None),
        P(every),
        P(every, None),
        P(every, None),

    )
    return places, results


def plane_fits(mesh):
    dp, seq = mesh.shape["dp"], mesh.shape["seq"]
    return dp == 4 and seq == 2 * dp


def solution(mesh):
    if not plane_fits(mesh):
        places, results = placements(("dp",), ("seq",))
        return jax.shard_map(
            local, mesh=mesh, in_specs=places, out_specs=results, check_vma=False
        )
    dp, seq = mesh.shape["dp"], mesh.shape["seq"]
    devices = mesh.devices.reshape(dp // 2, 2, seq // 4, 2, 2)
    places, results = placements(("u", "c"), ("y", "x", "v"))
    return jax.shard_map(
        plane_local,
        mesh=Mesh(devices, EVERY),
        in_specs=places,
        out_specs=results,
        check_vma=False,
    )
```

```python
import jax
import jax.numpy as jnp
from jax import lax
from jax.experimental import pallas as pl
from jax.experimental.pallas import tpu as pltpu
from jax.sharding import Mesh
from jax.sharding import PartitionSpec as P

HEAD_DIM = 128
CONV = 4
WINDOW = 2048


EPSILON = 1e-05
NEGATIVE = -1e30


def shifted(block, axis, distance):
    devices = range(lax.axis_size(axis))
    route = [(i - distance, i) for i in devices if i - distance in devices]
    return lax.ppermute(block, axis, route)


def carried_in(part, axis, combine, identity, reverse):
    count = lax.axis_size(axis)
    place = lax.axis_index(axis)
    ahead = count - 1 - place if reverse else place
    gathered = jax.tree.map(lambda a: lax.all_gather(a, axis), part)
    state = jax.tree.map(lambda a, e: jnp.zeros_like(a) + jnp.asarray(e, a.dtype), part, identity)

    def one(lap, state):
        source = count - 1 - lap if reverse else lap
        return combine(
            state, jax.tree.map(lambda a: lax.dynamic_index_in_dim(a, source, 0, False), gathered)
        )

    return lax.fori_loop(0, ahead, one, state)


def rms_gain(values, gain):
    return values * lax.rsqrt(jnp.mean(values * values, axis=-1, keepdims=True) + EPSILON) * gain


def product(left, right):
    return lax.dot_general(
        left, right, (((left.ndim - 1,), (0,)), ((), ())), preferred_element_type=jnp.float32
    )


def product_back(left, right):
    return lax.dot_general(
        left, right, (((left.ndim - 1,), (1,)), ((), ())), preferred_element_type=jnp.float32
    )


def outer(left, right):
    flat_left = left.reshape(-1, left.shape[-1])
    flat_right = right.reshape(-1, right.shape[-1])
    return lax.dot_general(
        flat_left, flat_right, (((0,), (0,)), ((), ())), preferred_element_type=jnp.float32
    )


def fetch_front(shards):
    return (
        lax.all_gather(shards[0], ("dp", "seq"), axis=0, tiled=True),
        lax.all_gather(shards[1], ("dp", "seq"), axis=0, tiled=True),
        lax.all_gather(shards[2], ("dp", "seq"), axis=1, tiled=True),
        lax.all_gather(shards[3], ("dp", "seq"), axis=0, tiled=True),
        lax.all_gather(shards[4], ("dp", "seq"), axis=0, tiled=True),
        lax.all_gather(shards[5], ("dp", "seq"), axis=1, tiled=True),
        lax.all_gather(shards[6].astype(jnp.bfloat16), ("dp", "seq"), axis=0, tiled=True).astype(
            jnp.float32
        ),
        lax.all_gather(shards[7].astype(jnp.bfloat16), ("dp", "seq"), axis=1, tiled=True).astype(
            jnp.float32
        ),
        lax.all_gather(shards[8].astype(jnp.bfloat16), ("dp", "seq"), axis=0, tiled=True).astype(
            jnp.float32
        ),
        lax.all_gather(shards[9], ("dp", "seq"), axis=0, tiled=True),
        lax.all_gather(shards[10], ("dp", "seq"), axis=0, tiled=True),
        lax.all_gather(shards[11], ("dp", "seq"), axis=0, tiled=True),
        lax.all_gather(shards[12], ("dp", "seq"), axis=0, tiled=True),
    )


def settle_front(grads):
    return (
        lax.psum_scatter(grads[0], ("dp", "seq"), scatter_dimension=0, tiled=True),
        lax.psum_scatter(grads[1], ("dp", "seq"), scatter_dimension=0, tiled=True),
        lax.psum_scatter(grads[2], ("dp", "seq"), scatter_dimension=1, tiled=True),
        lax.psum_scatter(grads[3], ("dp", "seq"), scatter_dimension=0, tiled=True),
        lax.psum_scatter(grads[4], ("dp", "seq"), scatter_dimension=0, tiled=True),
        lax.psum_scatter(grads[5], ("dp", "seq"), scatter_dimension=1, tiled=True),
        lax.psum_scatter(grads[6], ("dp", "seq"), scatter_dimension=0, tiled=True),
        lax.psum_scatter(grads[7], ("dp", "seq"), scatter_dimension=1, tiled=True),
        lax.psum_scatter(grads[8], ("dp", "seq"), scatter_dimension=0, tiled=True),
        lax.psum_scatter(grads[9], ("dp", "seq"), scatter_dimension=0, tiled=True),
        lax.psum_scatter(grads[10], ("dp", "seq"), scatter_dimension=0, tiled=True),
        lax.psum_scatter(grads[11], ("dp", "seq"), scatter_dimension=0, tiled=True),
        lax.psum_scatter(grads[12], ("dp", "seq"), scatter_dimension=0, tiled=True),
    )


def fetch_rear(shards):
    return (
        lax.all_gather(shards[0], ("dp", "seq"), axis=0, tiled=True),
        lax.all_gather(shards[1], ("dp", "seq"), axis=0, tiled=True),
        lax.all_gather(shards[2], ("dp", "seq"), axis=0, tiled=True),
        lax.all_gather(shards[3], ("dp", "seq"), axis=0, tiled=True),
        lax.all_gather(shards[4], ("dp", "seq"), axis=0, tiled=True),
        lax.all_gather(shards[5], ("dp", "seq"), axis=0, tiled=True),
    )


def settle_rear(grads):
    return (
        lax.psum_scatter(grads[0], ("dp", "seq"), scatter_dimension=0, tiled=True),
        lax.psum_scatter(grads[1], ("dp", "seq"), scatter_dimension=0, tiled=True),
        lax.psum_scatter(grads[2], ("dp", "seq"), scatter_dimension=0, tiled=True),
        lax.psum_scatter(grads[3], ("dp", "seq"), scatter_dimension=0, tiled=True),
        lax.psum_scatter(grads[4], ("dp", "seq"), scatter_dimension=0, tiled=True),
        lax.psum_scatter(grads[5], ("dp", "seq"), scatter_dimension=0, tiled=True),
    )


def ffn_forward(values, weights):
    gain, gate_up, down = weights
    width = down.shape[0]
    normed = rms_gain(values, gain.astype(jnp.float32)).astype(jnp.bfloat16)
    both = product(normed, gate_up)
    hidden = (jax.nn.silu(both[..., :width]) * both[..., width:]).astype(jnp.bfloat16)
    return (values + product(hidden, down), (normed, both, hidden))


def ffn_backward(values, grad, weights, kept):
    gain, gate_up, down = weights
    normed, both, hidden = kept
    width = down.shape[0]
    grad_low = grad.astype(jnp.bfloat16)
    grad_down = outer(hidden, grad_low)
    grad_hidden = product_back(grad_low, down)

    def ffn_gating(pair):
        return jax.nn.silu(pair[..., :width]) * pair[..., width:]

    unused, gating_back = jax.vjp(ffn_gating, both)
    grad_both = gating_back(grad_hidden)[0].astype(jnp.bfloat16)
    grad_gate_up = outer(normed, grad_both)
    grad_normed = product_back(grad_both, gate_up)
    unused, norm_back = jax.vjp(rms_gain, values, gain.astype(jnp.float32))
    grad_values, grad_gain = norm_back(grad_normed)
    return (grad + grad_values, (grad_gain, grad_gate_up, grad_down))


def convolve(before, inner, conv_weight, conv_bias):
    group = inner.shape[1]
    padded = jnp.concatenate([before, inner], axis=1)
    total = conv_bias
    for index in range(CONV):
        total = total + conv_weight[index] * padded[:, index : index + group]
    return jax.nn.silu(total)


def recurrence(decay):

    def advance(carry, slot):
        mixed_now, step_now, input_now, output_now = slot
        carry = (
            jnp.exp(step_now[:, None, :] * decay) * carry
            + (step_now * mixed_now)[:, None, :] * input_now[:, :, None]
        )
        return (carry, jnp.sum(output_now[:, :, None] * carry, axis=1))

    return advance


def selective(mixed, step, inputs_b, outputs_c, decay, state):
    slots = tuple((jnp.moveaxis(item, 1, 0) for item in (mixed, step, inputs_b, outputs_c)))
    state_end, core = lax.scan(recurrence(decay), state, slots, unroll=8)
    return (jnp.moveaxis(core, 0, 1), state_end)


def chain(earlier, later):
    return (earlier[0] * later[0], later[0] * earlier[1] + later[1])


def chain_both(earlier, later):
    return (
        earlier[0] * later[0],
        later[0] * earlier[1] + later[1],
        earlier[2] * later[2],
        earlier[2] * later[3] + earlier[3],
    )


def stepping(pre, step_bias, valid):
    return jax.nn.softplus(pre + step_bias) * valid[..., None]


def mamba_forward(values, lengths, carried_state, weights):
    (
        gain,
        mamba_in,
        conv_weight,
        conv_bias,
        selection,
        step_proj,
        step_bias,
        decay_log,
        skip_gain,
        mamba_out,
    ) = weights
    rows, group, width = values.shape
    inner_width = mamba_out.shape[0]
    rank = step_proj.shape[0]
    states = decay_log.shape[0]
    shard = lax.axis_index("seq")
    positions = shard * group + jnp.arange(group)
    valid = (positions[None, :] < lengths[:, None]).astype(jnp.float32)
    normed = rms_gain(values, gain.astype(jnp.float32)).astype(jnp.bfloat16)
    projected = product(normed, mamba_in)
    inner = projected[..., :inner_width]
    gate = projected[..., inner_width:]
    before = shifted(inner[:, group - CONV + 1 :], "seq", 1)
    mixed = convolve(before, inner, conv_weight.astype(jnp.float32), conv_bias.astype(jnp.float32))
    mixed_low = mixed.astype(jnp.bfloat16)
    select = product(mixed_low, selection)
    step_low = select[..., :rank].astype(jnp.bfloat16)
    inputs_b = select[..., rank : rank + states]
    outputs_c = select[..., rank + states :]
    pre = product(step_low, step_proj)
    step = stepping(pre, step_bias.astype(jnp.float32), valid)
    decay = -jnp.exp(decay_log.astype(jnp.float32))
    empty = jnp.zeros((rows, states, inner_width), jnp.float32)
    local_end = selective(mixed, step, inputs_b, outputs_c, decay, empty)[1]
    through = jnp.exp(decay * jnp.sum(step, axis=1)[:, None, :])
    prefix_decay, prefix_state = carried_in(
        (through, local_end), "seq", chain, (jnp.ones_like(through), empty), False
    )
    state = prefix_decay * carried_state + prefix_state
    core, state_end = selective(mixed, step, inputs_b, outputs_c, decay, state)
    mixed_out = core + skip_gain.astype(jnp.float32) * mixed
    gated = (mixed_out * jax.nn.silu(gate)).astype(jnp.bfloat16)
    kept = (
        valid,
        normed,
        projected,
        before,
        mixed,
        mixed_low,
        step_low,
        pre,
        step,
        inputs_b,
        outputs_c,
        decay,
        state,
        through,
        prefix_decay,
        mixed_out,
        gated,
        local_end,
        state_end,
    )
    return (values + product(gated, mamba_out), kept)


def mamba_backward(values, grad, weights, kept):
    (
        gain,
        mamba_in,
        conv_weight,
        conv_bias,
        selection,
        step_proj,
        step_bias,
        decay_log,
        skip_gain,
        mamba_out,
    ) = weights
    (
        valid,
        normed,
        projected,
        before,
        mixed,
        mixed_low,
        step_low,
        pre,
        step,
        inputs_b,
        outputs_c,
        decay,
        state,
        through,
        prefix_decay,
        mixed_out,
        gated,
        local_end,
        state_end,
    ) = kept
    group = values.shape[1]
    inner_width = mamba_out.shape[0]
    grad_low = grad.astype(jnp.bfloat16)
    grad_out = outer(gated, grad_low)
    grad_gated = product_back(grad_low, mamba_out)
    gate = projected[..., inner_width:]

    def mamba_gating(mixed_part, gate_part):
        return mixed_part * jax.nn.silu(gate_part)

    unused, gating_back = jax.vjp(mamba_gating, mixed_out, gate)
    grad_mixed_out, grad_gate = gating_back(grad_gated)
    skip = skip_gain.astype(jnp.float32)
    grad_skip = jnp.sum(grad_mixed_out * mixed, axis=(0, 1))
    unused, scan_back = jax.vjp(selective, mixed, step, inputs_b, outputs_c, decay, state)
    zero = jnp.zeros_like(state)
    ones = jnp.ones_like(state)
    own = scan_back((grad_mixed_out, zero))[5]
    suffix = carried_in(
        (through, own, through, local_end), "seq", chain_both, (ones, zero, ones, zero), True
    )
    final = suffix[2] * state_end + suffix[3]
    piece_width = inner_width // lax.axis_size("seq")
    new_state = lax.dynamic_slice_in_dim(final, lax.axis_index("seq") * piece_width, piece_width, 2)
    grad_state = lax.psum_scatter(prefix_decay * own, "seq", scatter_dimension=2, tiled=True)
    grad_mixed, grad_step, grad_inputs, grad_outputs, grad_decay, unused_state = scan_back(
        (grad_mixed_out, suffix[1])
    )
    grad_mixed = grad_mixed + grad_mixed_out * skip
    unused, step_back = jax.vjp(
        lambda pre_part, bias_part: stepping(pre_part, bias_part, valid),
        pre,
        step_bias.astype(jnp.float32),
    )
    grad_pre, grad_step_bias = step_back(grad_step)
    grad_pre_low = grad_pre.astype(jnp.bfloat16)
    grad_step_proj = outer(step_low, grad_pre_low)
    grad_step_low = product_back(grad_pre_low, step_proj)
    grad_select = jnp.concatenate([grad_step_low, grad_inputs, grad_outputs], axis=-1).astype(
        jnp.bfloat16
    )
    grad_selection = outer(mixed_low, grad_select)
    grad_mixed = grad_mixed + product_back(grad_select, selection)
    inner = projected[..., :inner_width]
    unused, conv_back = jax.vjp(
        convolve, before, inner, conv_weight.astype(jnp.float32), conv_bias.astype(jnp.float32)
    )
    grad_before, grad_inner, grad_conv_weight, grad_conv_bias = conv_back(grad_mixed)
    returned = shifted(grad_before, "seq", -1)
    grad_inner = jnp.concatenate(
        [grad_inner[:, : group - CONV + 1], grad_inner[:, group - CONV + 1 :] + returned], axis=1
    )
    grad_projected = jnp.concatenate([grad_inner, grad_gate], axis=-1).astype(jnp.bfloat16)
    grad_in = outer(normed, grad_projected)
    grad_normed = product_back(grad_projected, mamba_in)
    unused, norm_back = jax.vjp(rms_gain, values, gain.astype(jnp.float32))
    grad_values, grad_gain = norm_back(grad_normed)
    grads = (
        grad_gain,
        grad_in,
        grad_conv_weight,
        grad_conv_bias,
        grad_selection,
        grad_step_proj,
        grad_step_bias,
        grad_decay * decay,
        grad_skip,
        grad_out,
    )
    return (grad + grad_values, grads, grad_state, new_state)


def key_positions(start, count, cache_rows, group):
    index = start + jnp.arange(count)
    owner = index // (cache_rows + group)
    offset = index % (cache_rows + group)
    return jnp.where(
        offset < cache_rows,
        owner * cache_rows + offset - WINDOW,
        owner * group + offset - cache_rows,
    )


def visible(query_pos, key_pos, lengths):
    near = (key_pos[None, :] > query_pos[:, None] - WINDOW) & (
        key_pos[None, :] <= query_pos[:, None]
    )
    real = (key_pos[None, None, :] < lengths[:, None, None]) | (
        key_pos[None, None, :] == query_pos[None, :, None]
    )
    return (near[None] & real)[:, :, None, :]


def blockwise(step_fn, carry, piece, size):
    count = jax.tree.leaves(piece)[0].shape[1]
    blocks = count // size

    def split(item):
        return jnp.moveaxis(item.reshape((item.shape[0], blocks, size) + item.shape[2:]), 1, 0)

    def turn(inner, pair):
        return (step_fn(inner, pair[1], pair[0] * size), None)

    carry, unused = lax.scan(turn, carry, (jnp.arange(blocks), jax.tree.map(split, piece)))
    return carry


def over_keys(local_kv, fold, init):
    return fold(init, lax.all_gather(local_kv, "seq", axis=1, tiled=True), jnp.int32(0))


def attention_forward(values, lengths, carried_kv, weights):
    gain, qkv_proj, out_proj = weights
    rows, group, width = values.shape
    heads = width // HEAD_DIM
    cache_rows = carried_kv.shape[1]
    size = cache_rows + group
    scale = HEAD_DIM ** (-0.5)
    query_pos = lax.axis_index("seq") * group + jnp.arange(group)
    normed = rms_gain(values, gain.astype(jnp.float32)).astype(jnp.bfloat16)
    qkv = product(normed, qkv_proj).astype(jnp.bfloat16)
    queries = qkv[..., :width].reshape(rows, group, heads, HEAD_DIM)
    segment_kv = qkv[..., width:]
    local_kv = jnp.concatenate([carried_kv, segment_kv], axis=1)

    def one_block(carry, piece, start):
        count = piece.shape[1]
        inside = visible(query_pos, key_positions(start, count, cache_rows, group), lengths)

        def one_work(state):
            top, total, accum = state
            keys = piece[..., :width].reshape(rows, count, heads, HEAD_DIM)
            contents = piece[..., width:].reshape(rows, count, heads, HEAD_DIM)
            scores = (
                jnp.einsum("rqhd,rkhd->rqhk", queries, keys, preferred_element_type=jnp.float32)
                * scale
            )
            new_top = jnp.maximum(top, jnp.max(jnp.where(inside, scores, NEGATIVE), axis=-1))
            weights_now = jnp.exp(jnp.where(inside, scores - new_top[..., None], NEGATIVE))
            factor = jnp.exp(top - new_top)
            total = total * factor + jnp.sum(weights_now, axis=-1)
            accum = accum * factor[..., None] + jnp.einsum(
                "rqhk,rkhd->rqhd",
                weights_now.astype(jnp.bfloat16),
                contents,
                preferred_element_type=jnp.float32,
            )
            return (new_top, total, accum)

        return lax.cond(jnp.any(inside), one_work, lambda state: state, carry)

    init = (
        jnp.full((rows, group, heads), NEGATIVE, jnp.float32),
        jnp.zeros((rows, group, heads), jnp.float32),
        jnp.zeros((rows, group, heads, HEAD_DIM), jnp.float32),
    )
    top, total, accum = over_keys(
        local_kv, lambda carry, piece, start: blockwise(one_block, carry, piece, size), init
    )
    attended = accum / total[..., None]
    logsum = top + jnp.log(total)
    attended_low = attended.astype(jnp.bfloat16).reshape(rows, group, width)
    kept = (normed, queries, local_kv, attended, attended_low, logsum, query_pos)
    return (values + product(attended_low, out_proj), segment_kv, kept)


def attention_backward(values, grad, lengths, weights, kept):
    gain, qkv_proj, out_proj = weights
    normed, queries, local_kv, attended, attended_low, logsum, query_pos = kept
    rows, group, width = values.shape
    heads = width // HEAD_DIM
    size = local_kv.shape[1]
    cache_rows = size - group
    scale = HEAD_DIM ** (-0.5)
    grad_low = grad.astype(jnp.bfloat16)
    grad_out = outer(attended_low, grad_low)
    grad_attended = (
        product_back(grad_low, out_proj).astype(jnp.bfloat16).reshape(rows, group, heads, HEAD_DIM)
    )
    delta = jnp.sum(grad_attended.astype(jnp.float32) * attended, axis=-1)

    def query_block(carry, piece, start):
        count = piece.shape[1]
        inside = visible(query_pos, key_positions(start, count, cache_rows, group), lengths)

        def query_work(grad_queries):
            keys = piece[..., :width].reshape(rows, count, heads, HEAD_DIM)
            contents = piece[..., width:].reshape(rows, count, heads, HEAD_DIM)
            scores = (
                jnp.einsum("rqhd,rkhd->rqhk", queries, keys, preferred_element_type=jnp.float32)
                * scale
            )
            weights_now = jnp.exp(jnp.where(inside, scores - logsum[..., None], NEGATIVE))
            grad_weights = jnp.einsum(
                "rqhd,rkhd->rqhk", grad_attended, contents, preferred_element_type=jnp.float32
            )
            grad_scores = (weights_now * (grad_weights - delta[..., None])).astype(jnp.bfloat16)
            return (
                grad_queries
                + jnp.einsum(
                    "rqhk,rkhd->rqhd", grad_scores, keys, preferred_element_type=jnp.float32
                )
                * scale
            )

        return lax.cond(jnp.any(inside), query_work, lambda state: state, carry)

    grad_queries = over_keys(
        local_kv,
        lambda carry, piece, start: blockwise(query_block, carry, piece, size),
        jnp.zeros((rows, group, heads, HEAD_DIM), jnp.float32),
    )
    whole_logsum, whole_delta = (
        lax.all_gather(logsum, "seq", axis=1, tiled=True),
        lax.all_gather(delta, "seq", axis=1, tiled=True),
    )
    own_pos = key_positions(lax.axis_index("seq") * size, size, cache_rows, group)
    own_keys = local_kv[..., :width].reshape(rows, size, heads, HEAD_DIM)
    own_contents = local_kv[..., width:].reshape(rows, size, heads, HEAD_DIM)

    def key_block(carry, piece, start):
        part_queries, part_grads = piece
        count = part_queries.shape[1]
        inside = visible(start + jnp.arange(count), own_pos, lengths)

        def key_work(state):
            grad_keys, grad_contents = state
            part_logsum = lax.dynamic_slice_in_dim(whole_logsum, start, count, 1)
            part_delta = lax.dynamic_slice_in_dim(whole_delta, start, count, 1)
            scores = (
                jnp.einsum(
                    "rqhd,rkhd->rqhk", part_queries, own_keys, preferred_element_type=jnp.float32
                )
                * scale
            )
            weights_now = jnp.exp(jnp.where(inside, scores - part_logsum[..., None], NEGATIVE))
            grad_contents = grad_contents + jnp.einsum(
                "rqhk,rqhd->rkhd",
                weights_now.astype(jnp.bfloat16),
                part_grads,
                preferred_element_type=jnp.float32,
            )
            grad_weights = jnp.einsum(
                "rqhd,rkhd->rqhk", part_grads, own_contents, preferred_element_type=jnp.float32
            )
            grad_scores = (weights_now * (grad_weights - part_delta[..., None])).astype(
                jnp.bfloat16
            )
            grad_keys = (
                grad_keys
                + jnp.einsum(
                    "rqhk,rqhd->rkhd", grad_scores, part_queries, preferred_element_type=jnp.float32
                )
                * scale
            )
            return (grad_keys, grad_contents)

        return lax.cond(jnp.any(inside), key_work, lambda state: state, carry)

    empty = jnp.zeros((rows, size, heads, HEAD_DIM), jnp.float32)
    grad_keys, grad_contents = blockwise(
        key_block,
        (empty, empty),
        (
            lax.all_gather(queries, "seq", axis=1, tiled=True),
            lax.all_gather(grad_attended, "seq", axis=1, tiled=True),
        ),
        group,
    )
    grad_local = jnp.concatenate(
        [grad_keys.reshape(rows, size, width), grad_contents.reshape(rows, size, width)], axis=-1
    )
    grad_cache = grad_local[:, :cache_rows]
    grad_qkv = jnp.concatenate(
        [grad_queries.reshape(rows, group, width), grad_local[:, cache_rows:]], axis=-1
    ).astype(jnp.bfloat16)
    grad_qkv_proj = outer(normed, grad_qkv)
    grad_normed = product_back(grad_qkv, qkv_proj)
    unused, norm_back = jax.vjp(rms_gain, values, gain.astype(jnp.float32))
    grad_values, grad_gain = norm_back(grad_normed)
    return (grad + grad_values, (grad_gain, grad_qkv_proj, grad_out), grad_cache)


def local(
    activations,
    cotangent,
    carried_state,
    carried_kv,
    row_lengths,
    mamba_gain,
    mamba_in,
    conv_weight,
    conv_bias,
    selection,
    step_proj,
    step_bias,
    decay_log,
    skip_gain,
    mamba_out,
    first_gain,
    first_gate_up,
    first_down,
    attention_gain,
    attention_qkv,
    attention_out,
    second_gain,
    second_gate_up,
    second_down,
):
    front_shards = (
        mamba_gain,
        mamba_in,
        conv_weight,
        conv_bias,
        selection,
        step_proj,
        step_bias,
        decay_log,
        skip_gain,
        mamba_out,
        first_gain,
        first_gate_up,
        first_down,
    )
    rear_shards = (
        attention_gain,
        attention_qkv,
        attention_out,
        second_gain,
        second_gate_up,
        second_down,
    )
    stream = activations.astype(jnp.float32)
    front_whole = fetch_front(front_shards)
    first_stream, mamba_kept = mamba_forward(stream, row_lengths, carried_state, front_whole[:10])
    second_stream, first_kept = ffn_forward(first_stream, front_whole[10:])
    rear_whole = fetch_rear(rear_shards)
    third_stream, segment_kv, attention_kept = attention_forward(
        second_stream, row_lengths, carried_kv, rear_whole[:3]
    )
    fourth_stream, second_kept = ffn_forward(third_stream, rear_whole[3:])
    grad = cotangent.astype(jnp.float32)
    rear_back = fetch_rear(rear_shards)
    grad, second_grads = ffn_backward(third_stream, grad, rear_back[3:], second_kept)
    grad, attention_grads, grad_cache = attention_backward(
        second_stream, grad, row_lengths, rear_back[:3], attention_kept
    )
    rear_grads = settle_rear(attention_grads + second_grads)
    front_back = fetch_front(front_shards)
    grad, first_grads = ffn_backward(first_stream, grad, front_back[10:], first_kept)
    grad, mamba_grads, grad_state, new_state = mamba_backward(
        stream, grad, front_back[:10], mamba_kept
    )
    front_grads = settle_front(mamba_grads + first_grads)
    return (
        fourth_stream.astype(jnp.bfloat16),
        new_state,
        segment_kv,
        grad,
        grad_state,
        grad_cache,
        front_grads[0],
        front_grads[1],
        front_grads[2],
        front_grads[3],
        front_grads[4],
        front_grads[5],
        front_grads[6],
        front_grads[7],
        front_grads[8],
        front_grads[9],
        front_grads[10],
        front_grads[11],
        front_grads[12],
        rear_grads[0],
        rear_grads[1],
        rear_grads[2],
        rear_grads[3],
        rear_grads[4],
        rear_grads[5],
    )


EVERY = ("u", "c", "y", "x", "v")
PLANE = ("y", "x", "c")
SQUARES = ("u", "v")
BF = jnp.bfloat16
F32 = jnp.float32


def params(**more):
    return pltpu.CompilerParams(vmem_limit_bytes=32 * 2**20, **more)


def bit_route(move):
    route = []
    for place in range(2 ** len(EVERY)):
        bits = [place >> (len(EVERY) - 1 - k) & 1 for k in range(len(EVERY))]
        goal = 0
        for bit in move(*bits):
            goal = 2 * goal + bit
        if goal != place:
            route.append((place, goal))
    return route


def swap_planes(block):
    away = lax.axis_index("c") != lax.axis_index("v")
    route = bit_route(lambda u, c, y, x, v: (u, v, y, x, c))
    return jnp.where(away, lax.ppermute(block, EVERY, route), block)


def other(block, axis):
    return lax.ppermute(block, axis, [(0, 1), (1, 0)])


def gather_line(block):
    from_y = other(block, "y")
    return jnp.stack([block, other(block, "x"), from_y, other(from_y, "x")])


def gather_plane(block):
    own = gather_line(block)
    return jnp.concatenate([own, other(own, "c")], axis=0)


def scatter_line(mine, kind):
    to_y = (mine[2] + other(mine[3].astype(kind), "x").astype(F32)).astype(kind)
    from_x = other(mine[1].astype(kind), "x").astype(F32)
    return mine[0] + from_x + other(to_y, "y").astype(F32)


def scatter_plane(parts):
    half = parts.shape[0] // 2
    mine = parts[:half].astype(F32) + other(parts[half:], "c").astype(F32)
    return scatter_line(mine, parts.dtype)


def sum_plane(parts):
    return gather_plane(scatter_plane(parts))


def trade(block, axes):
    return lax.all_to_all(block, axes, 0, 0, tiled=True)


def gather_small(block, axes):
    for axis in reversed(axes):
        block = in_order(block, other(block, axis), axis)
    return block


def total_small(block):
    block = block + other(block, "c")
    for axes in (("y", "x"), ("u", "v")):
        turned = [
            lax.ppermute(block, axes, [(k, k ^ turn) for k in range(4)]) for turn in (1, 2, 3)
        ]
        block = block + sum(turned)
    return block


def pair_sum(parts, axis):
    here = lax.axis_index(axis)
    theirs = other(lax.dynamic_index_in_dim(parts, 1 - here, 0, False), axis)
    mine = lax.dynamic_index_in_dim(parts, here, 0, False)
    return mine.astype(F32) + theirs.astype(F32)


def reduce_squares(parts):
    return lax.psum_scatter(parts, SQUARES, scatter_dimension=0)


def gather_squares(block):
    return lax.all_gather(block, SQUARES, axis=0)


def settle(stage, *pieces):
    return lax.optimization_barrier((stage,) + pieces)


def tie(value, *stages):
    return lax.optimization_barrier((value,) + stages)[0]


def in_order(mine, theirs, axis):
    first = lax.axis_index(axis) == 0
    return jnp.stack([jnp.where(first, mine, theirs), jnp.where(first, theirs, mine)])


def kv_owners(parts):
    for axis in PLANE:
        lead = parts.ndim - {"y": 6, "x": 5, "c": 4}[axis]
        stay = lax.index_in_dim(parts, 0, lead, False)
        leave = lax.index_in_dim(parts, 1, lead, False)
        parts = in_order(stay, other(leave, axis), axis)
    side, y_size, c_size, two, count, width = parts.shape
    return parts.transpose(0, 4, 3, 2, 1, 5).reshape(side, count, two * y_size * c_size * width)


def rows_gather(block):
    here = lax.axis_index("c")
    mine = lax.dynamic_index_in_dim(block, here, 0, False)
    theirs = lax.dynamic_index_in_dim(block, 1 - here, 0, False)
    return gather_line(jnp.stack([mine, other(theirs, "c")]))


def rows_scatter(parts):
    parts = parts.reshape((4, 2) + parts.shape[1:])
    pair = scatter_line(parts.astype(F32), parts.dtype)
    return in_order(pair[0], other(pair[1].astype(parts.dtype), "c").astype(F32), "c")


def rows_of(gathered):
    squares, members, rows, width = gathered.shape
    split = gathered.reshape(2, 2, members // 2, 2, rows, width)
    return split.transpose(0, 3, 2, 1, 4, 5).reshape(squares * members * rows, width)


def by_square(grad):
    total, width = grad.shape
    split = grad.reshape(2, 2, 4, 2, total // 32, width).transpose(0, 3, 2, 1, 4, 5)
    return split.reshape(4, 8, total // 32, width)


def relocate(block, back):
    route = bit_route(lambda u, c, y, x, v: (x, y, u, c, v))
    moving = jnp.zeros((2 ** len(EVERY),), bool).at[jnp.array([place for place, goal in route])].set(True)
    here = lax.axis_index(EVERY)
    moved = lax.ppermute(block, EVERY, [(goal, place) for place, goal in route] if back else route)
    return jnp.where(moving[here], moved, block)


def dot(left, right, left_dim, right_dim):
    return lax.dot_general(
        left, right, (((left_dim,), (right_dim,)), ((), ())), preferred_element_type=F32
    )


def conv_body(order, inner_ref, taps_ref, bias_ref, total_ref, mixed_ref, low_ref, held):
    step = pl.program_id(0)
    rows, group = inner_ref.shape[1], inner_ref.shape[2]

    @pl.when(step == 0)
    def clear():
        held[:, :8] = jnp.zeros_like(held[:, :8])

    @pl.when(step > 0)
    def keep():
        held[:, :8] = held[:, group:]

    for row in range(rows):
        held[row, 8:] = inner_ref[0, row]
        total = bias_ref[...] + taps_ref[0:1] * held[row, 5 : 5 + group]
        for tap in range(1, CONV):
            total = total + taps_ref[tap : tap + 1] * held[row, 5 + tap : 5 + tap + group]
        mixed = total / (1.0 + jnp.exp(-total))
        total_ref[0, row] = total
        mixed_ref[0, row] = mixed
        low_ref[0, row] = mixed.astype(BF)


def conv_forward(order, projected, taps, bias):
    blocks, rows, group, width = projected.shape
    spec = pl.BlockSpec((1, rows, group, width), lambda i, order: (order[i], 0, 0, 0))
    shape = (blocks, rows, group, width)
    return pl.pallas_call(
        conv_body,
        grid_spec=pltpu.PrefetchScalarGridSpec(
            num_scalar_prefetch=1,
            grid=(blocks,),
            in_specs=[
                spec,
                pl.BlockSpec((CONV, width), lambda i, order: (0, 0)),
                pl.BlockSpec((1, width), lambda i, order: (0, 0)),
            ],
            out_specs=[spec, spec, spec],
            scratch_shapes=[pltpu.VMEM((rows, group + 8, width), F32)],
        ),
        out_shape=[
            jax.ShapeDtypeStruct(shape, F32),
            jax.ShapeDtypeStruct(shape, F32),
            jax.ShapeDtypeStruct(shape, BF),
        ],
        compiler_params=params(),
        name="conv_forward",
    )(order, projected, taps, bias)


def conv_back_body(order, grad_ref, total_ref, inner_ref, taps_ref, out_ref, sums_ref, held):
    step = pl.program_id(0)
    rows, group = inner_ref.shape[1], inner_ref.shape[2]

    @pl.when(step == 0)
    def clear():
        held[:, group:] = jnp.zeros_like(held[:, group:])
        sums_ref[...] = jnp.zeros_like(sums_ref)

    @pl.when(step > 0)
    def keep():
        held[:, group:] = held[:, :8]

    for row in range(rows):
        total = total_ref[0, row]
        sig = 1.0 / (1.0 + jnp.exp(-total))
        grad = grad_ref[0, row] * (sig * (1.0 + total * (1.0 - sig)))
        held[row, :group] = grad
        inner = inner_ref[0, row]
        back = None
        for tap in range(CONV):
            later = held[row, CONV - 1 - tap : CONV - 1 - tap + group]
            part = taps_ref[tap : tap + 1] * later
            back = part if back is None else back + part
            sums_ref[tap : tap + 1] += jnp.sum(inner * later, axis=0, keepdims=True)
        sums_ref[CONV : CONV + 1] += jnp.sum(grad, axis=0, keepdims=True)
        out_ref[0, row] = back.astype(BF)


def conv_back(order, grad, total, projected, taps):
    blocks, rows, group, width = grad.shape
    spec = pl.BlockSpec(
        (1, rows, group, width), lambda i, order: (order[blocks - 1 - i], 0, 0, 0)
    )
    return pl.pallas_call(
        conv_back_body,
        grid_spec=pltpu.PrefetchScalarGridSpec(
            num_scalar_prefetch=1,
            grid=(blocks,),
            in_specs=[spec, spec, spec, pl.BlockSpec((CONV, width), lambda i, order: (0, 0))],
            out_specs=[spec, pl.BlockSpec((8, width), lambda i, order: (0, 0))],
            scratch_shapes=[pltpu.VMEM((rows, group + 8, width), F32)],
        ),
        out_shape=[
            jax.ShapeDtypeStruct(grad.shape, BF),
            jax.ShapeDtypeStruct((8, width), F32),
        ],
        compiler_params=params(),
        name="conv_back",
    )(order, grad, total, projected, taps)


def widen(tile, width):
    return jnp.concatenate([tile] * (width // 128), axis=1)


def narrow(tile):
    total = tile[:, :128]
    for start in range(128, tile.shape[1], 128):
        total = total + tile[:, start : start + 128]
    return total


def scan_body(
    order, mixed_ref, step_ref, b_ref, c_ref, decay_ref, start_ref, core_ref, past_ref, end_ref, held
):
    @pl.when(pl.program_id(0) == 0)
    def begin():
        held[...] = start_ref[...]

    decay = decay_ref[...]
    rows, group, width = mixed_ref.shape[1:]

    def eight(turn, states):
        base = pl.multiple_of(turn * 8, 8)
        states = list(states)
        steps = [step_ref[0, row, pl.ds(base, 8), :] for row in range(rows)]
        drives = [steps[row] * mixed_ref[0, row, pl.ds(base, 8), :] for row in range(rows)]
        cores = [[] for row in range(rows)]
        for k in range(8):
            for row in range(rows):
                past_ref[0, row, base + k] = states[row]
                fade = jnp.exp(steps[row][k : k + 1] * decay)
                state = fade * states[row] + drives[row][k : k + 1] * widen(
                    b_ref[0, row, base + k], width
                )
                states[row] = state
                seen = widen(c_ref[0, row, base + k], width) * state
                cores[row].append(jnp.sum(seen, axis=0, keepdims=True))
        for row in range(rows):
            core_ref[0, row, pl.ds(base, 8), :] = jnp.concatenate(cores[row], axis=0)
        return tuple(states)

    states = lax.fori_loop(0, group // 8, eight, tuple(held[row] for row in range(rows)))
    for row in range(rows):
        held[row] = states[row]
        end_ref[row] = states[row]


def scan_forward(order, mixed, step, wide_b, wide_c, decay, start):
    blocks, rows, group, width = mixed.shape
    states = decay.shape[0]
    spec = pl.BlockSpec((1, rows, group, width), lambda i, order: (order[i], 0, 0, 0))
    maps = pl.BlockSpec((1, rows, group, states, 128), lambda i, order: (order[i], 0, 0, 0, 0))
    whole = pl.BlockSpec((rows, states, width), lambda i, order: (0, 0, 0))
    return pl.pallas_call(
        scan_body,
        grid_spec=pltpu.PrefetchScalarGridSpec(
            num_scalar_prefetch=1,
            grid=(blocks,),
            in_specs=[
                spec,
                spec,
                maps,
                maps,
                pl.BlockSpec((states, width), lambda i, order: (0, 0)),
                whole,
            ],
            out_specs=[
                spec,
                pl.BlockSpec(
                    (1, rows, group, states, width), lambda i, order: (order[i], 0, 0, 0, 0)
                ),
                whole,
            ],
            scratch_shapes=[pltpu.VMEM((rows, states, width), F32)],
        ),
        out_shape=[
            jax.ShapeDtypeStruct(mixed.shape, F32),
            jax.ShapeDtypeStruct((blocks, rows, group, states, width), F32),
            jax.ShapeDtypeStruct(start.shape, F32),
        ],
        compiler_params=params(),
        name="scan_forward",
    )(order, mixed, step, wide_b, wide_c, decay, start)


def scan_back_body(
    order,
    mixed_ref,
    step_ref,
    b_ref,
    c_ref,
    grad_ref,
    past_ref,
    decay_ref,
    end_ref,
    dmixed_ref,
    dstep_ref,
    db_ref,
    dc_ref,
    ddecay_ref,
    dstart_ref,
    held,
    after,
):
    @pl.when(pl.program_id(0) == 0)
    def begin():
        held[...] = jnp.zeros_like(held)
        after[...] = end_ref[...]
        ddecay_ref[...] = jnp.zeros_like(ddecay_ref)

    decay = decay_ref[...]
    rows, group, width = mixed_ref.shape[1:]
    turns = group // 8

    def eight(turn, carry):
        base = pl.multiple_of((turns - 1 - turn) * 8, 8)
        backs, states, sums = list(carry[0]), list(carry[1]), carry[2]
        steps = [step_ref[0, row, pl.ds(base, 8), :] for row in range(rows)]
        inputs = [mixed_ref[0, row, pl.ds(base, 8), :] for row in range(rows)]
        grads = [grad_ref[0, row, pl.ds(base, 8), :] for row in range(rows)]
        drives = [steps[row] * inputs[row] for row in range(rows)]
        firsts = [[None] * 8 for row in range(rows)]
        seconds = [[None] * 8 for row in range(rows)]
        for k in reversed(range(8)):
            for row in range(rows):
                now = steps[row][k : k + 1]
                grad = grads[row][k : k + 1]
                past = past_ref[0, row, base + k]
                fade = jnp.exp(now * decay)
                back = widen(c_ref[0, row, base + k], width) * grad + backs[row]
                dc_ref[0, row, base + k] = narrow(states[row] * grad).astype(BF)
                firsts[row][k] = jnp.sum(
                    widen(b_ref[0, row, base + k], width) * back, axis=0, keepdims=True
                )
                db_ref[0, row, base + k] = narrow(back * drives[row][k : k + 1]).astype(BF)
                faded = fade * back
                flow = faded * past
                seconds[row][k] = jnp.sum(flow * decay, axis=0, keepdims=True)
                sums = sums + flow * now
                backs[row] = faded
                states[row] = past
        for row in range(rows):
            first = jnp.concatenate(firsts[row], axis=0)
            second = jnp.concatenate(seconds[row], axis=0)
            dmixed_ref[0, row, pl.ds(base, 8), :] = steps[row] * first
            dstep_ref[0, row, pl.ds(base, 8), :] = inputs[row] * first + second
        return (tuple(backs), tuple(states), sums)

    backs, states, sums = lax.fori_loop(
        0,
        turns,
        eight,
        (
            tuple(held[row] for row in range(rows)),
            tuple(after[row] for row in range(rows)),
            ddecay_ref[...],
        ),
    )
    ddecay_ref[...] = sums
    for row in range(rows):
        held[row] = backs[row]
        after[row] = states[row]
        dstart_ref[row] = backs[row]


def scan_back(order, mixed, step, wide_b, wide_c, grad, past, decay, end):
    blocks, rows, group, width = mixed.shape
    states = decay.shape[0]
    last = blocks - 1
    spec = pl.BlockSpec((1, rows, group, width), lambda i, order: (order[last - i], 0, 0, 0))
    maps = pl.BlockSpec(
        (1, rows, group, states, 128), lambda i, order: (order[last - i], 0, 0, 0, 0)
    )
    kept = pl.BlockSpec(
        (1, rows, group, states, width), lambda i, order: (order[last - i], 0, 0, 0, 0)
    )
    whole = pl.BlockSpec((rows, states, width), lambda i, order: (0, 0, 0))
    rates = pl.BlockSpec((states, width), lambda i, order: (0, 0))
    return pl.pallas_call(
        scan_back_body,
        grid_spec=pltpu.PrefetchScalarGridSpec(
            num_scalar_prefetch=1,
            grid=(blocks,),
            in_specs=[spec, spec, maps, maps, spec, kept, rates, whole],
            out_specs=[spec, spec, maps, maps, rates, whole],
            scratch_shapes=[
                pltpu.VMEM((rows, states, width), F32),
                pltpu.VMEM((rows, states, width), F32),
            ],
        ),
        out_shape=[
            jax.ShapeDtypeStruct(mixed.shape, F32),
            jax.ShapeDtypeStruct(mixed.shape, F32),
            jax.ShapeDtypeStruct((blocks, rows, group, states, 128), BF),
            jax.ShapeDtypeStruct((blocks, rows, group, states, 128), BF),
            jax.ShapeDtypeStruct(decay.shape, F32),
            jax.ShapeDtypeStruct(end.shape, F32),
        ],
        compiler_params=params(),
        name="scan_back",
    )(order, mixed, step, wide_b, wide_c, grad, past, decay, end)


def own_positions(shape, axis, first, member, group):
    index = first + lax.broadcasted_iota(jnp.int32, shape, axis)
    slot = index // group
    block = slot ^ member
    return block * group + index % group


def seen_cache(query, place, shape, group):
    index = lax.broadcasted_iota(jnp.int32, shape, 1)
    return (index + place * group) > query


def seen_own(query, key, length):
    return (key <= query) & ((key < length) | (key == query))


def attend_body(meta_ref, q_ref, ck_ref, cv_ref, k_ref, v_ref, out_ref, log_ref):
    count = q_ref.shape[0]
    first = pl.program_id(1) * count
    scale = HEAD_DIM ** (-0.5)
    queries = q_ref[...]
    pieces = ck_ref.shape[0]
    size = ck_ref.shape[1]
    tokens = k_ref.shape[0]
    member = meta_ref[1]
    group = tokens // pieces
    query = own_positions((count, 1), 0, first, member, group)
    scores = []
    for piece in range(pieces):
        score = dot(queries, ck_ref[piece], 1, 1) * scale
        inside = seen_cache(query, piece, (1, size), size)
        scores.append(jnp.where(inside, score, NEGATIVE))
    score = dot(queries, k_ref[...], 1, 1) * scale
    key = own_positions((1, tokens), 1, 0, member, group)
    scores.append(jnp.where(seen_own(query, key, meta_ref[0]), score, NEGATIVE))
    top = jnp.max(scores[0], axis=1, keepdims=True)
    for score in scores[1:]:
        top = jnp.maximum(top, jnp.max(score, axis=1, keepdims=True))
    total = jnp.zeros_like(top)
    result = jnp.zeros((count, HEAD_DIM), F32)
    for piece, score in enumerate(scores):
        part = jnp.exp(score - top)
        total = total + jnp.sum(part, axis=1, keepdims=True)
        contents = cv_ref[piece] if piece < pieces else v_ref[...]
        result = result + dot(part.astype(BF), contents, 1, 0)
    out_ref[...] = result / total
    log_ref[0] = jnp.broadcast_to(top + jnp.log(total), (count, 128))


def attend(meta, qkv, cached_keys, cached_contents):
    tokens, width = qkv.shape
    width = width // 3
    heads = width // HEAD_DIM
    count = 256
    shards, group, unused = cached_keys.shape
    own = lambda base: pl.BlockSpec((tokens, HEAD_DIM), lambda h, i, meta: (0, base + h))
    held = pl.BlockSpec((shards, group, HEAD_DIM), lambda h, i, meta: (0, 0, h))
    block = pl.BlockSpec((count, HEAD_DIM), lambda h, i, meta: (i, h))
    return pl.pallas_call(
        attend_body,
        grid_spec=pltpu.PrefetchScalarGridSpec(
            num_scalar_prefetch=1,
            grid=(heads, tokens // count),
            in_specs=[block, held, held, own(heads), own(2 * heads)],
            out_specs=[block, pl.BlockSpec((1, count, 128), lambda h, i, meta: (h, i, 0))],
        ),
        out_shape=[
            jax.ShapeDtypeStruct((tokens, width), F32),
            jax.ShapeDtypeStruct((heads, tokens, 128), F32),
        ],
        compiler_params=params(),
        name="attend",
    )(meta, qkv, cached_keys, cached_contents, qkv, qkv)


def attend_back_body(
    meta_ref,
    q_ref,
    grad_ref,
    out_ref,
    log_ref,
    ck_ref,
    cv_ref,
    k_ref,
    v_ref,
    dck_ref,
    dcv_ref,
    dq_ref,
    dk_ref,
    dv_ref,
    total,
    delta,
):
    piece = pl.program_id(1)
    pieces = pl.num_programs(1) - 1
    scale = HEAD_DIM ** (-0.5)
    queries = q_ref[...]
    grad = grad_ref[...]
    count = queries.shape[0]
    size = ck_ref.shape[1]
    member = meta_ref[1]
    group = count // (2 * pieces)
    query = own_positions((count, 1), 0, 0, member, group)

    @pl.when(piece == 0)
    def begin():
        total[...] = jnp.zeros_like(total)
        mine = jnp.sum(grad.astype(F32) * out_ref[...], axis=1, keepdims=True)
        delta[...] = jnp.broadcast_to(mine, delta.shape)

    def work(keys, contents, inside):
        score = dot(queries, keys, 1, 1) * scale
        part = jnp.exp(score - log_ref[0][:, :1])
        if inside is not None:
            part = jnp.where(inside, part, 0.0)
        dcontents = dot(part.astype(BF), grad, 0, 0)
        slope = dot(grad, contents, 1, 1)
        dscore = (part * (slope - delta[:, :1])).astype(BF)
        total[...] += dot(dscore, keys, 1, 0) * scale
        return dot(dscore, queries, 0, 0) * scale, dcontents

    def cached(inside):
        keys = ck_ref[...].reshape(2 * size, HEAD_DIM)
        contents = cv_ref[...].reshape(2 * size, HEAD_DIM)
        dkeys, dcontents = work(keys, contents, inside)
        dck_ref[...] = dkeys.astype(BF).reshape(2, size, HEAD_DIM)
        dcv_ref[...] = dcontents.astype(BF).reshape(2, size, HEAD_DIM)

    edge = piece * 2 * size < count

    @pl.when((piece < pieces) & edge)
    def near():
        cached(seen_cache(query, 2 * piece, (1, 2 * size), size))

    @pl.when((piece < pieces) & jnp.logical_not(edge))
    def far():
        cached(None)

    @pl.when(piece == pieces)
    def own():
        key = own_positions((1, count), 1, 0, member, group)
        dkeys, dcontents = work(k_ref[...], v_ref[...], seen_own(query, key, meta_ref[0]))
        dk_ref[...] = dkeys.astype(BF)
        dv_ref[...] = dcontents.astype(BF)
        dq_ref[...] = total[...].astype(BF)


def attend_back(meta, qkv, grad, out, log, cached_keys, cached_contents):
    tokens, width = grad.shape
    heads = width // HEAD_DIM
    shards, group, unused = cached_keys.shape
    pieces = shards // 2
    own = lambda base: pl.BlockSpec((tokens, HEAD_DIM), lambda h, i, meta: (0, base + h))
    place = lambda i: jnp.minimum(i, pieces - 1)
    held = pl.BlockSpec((2, group, HEAD_DIM), lambda h, i, meta: (place(i), 0, h))
    result = jax.ShapeDtypeStruct((tokens, width), BF)
    return pl.pallas_call(
        attend_back_body,
        grid_spec=pltpu.PrefetchScalarGridSpec(
            num_scalar_prefetch=1,
            grid=(heads, pieces + 1),
            in_specs=[
                own(0),
                own(0),
                own(0),
                pl.BlockSpec((1, tokens, 128), lambda h, i, meta: (h, 0, 0)),
                held,
                held,
                own(heads),
                own(2 * heads),
            ],
            out_specs=[
                held,
                held,
                own(0),
                own(0),
                own(0),
            ],
            scratch_shapes=[
                pltpu.VMEM((tokens, HEAD_DIM), F32),
                pltpu.VMEM((tokens, 128), F32),
            ],
        ),
        out_shape=[jax.ShapeDtypeStruct(cached_keys.shape, BF)] * 2 + [result, result, result],
        compiler_params=params(),
        name="attend_back",
    )(meta, qkv, grad, out, log, cached_keys, cached_contents, qkv, qkv)


def assemble(gots, moves, shape):
    def body(*refs):
        out_ref = refs[-1]
        for (row, column), height, (which, member, left, width) in moves:
            part = refs[which][member, :, left : left + width].astype(F32)
            out_ref[row : row + height, column : column + width] = part

    return pl.pallas_call(
        body,
        out_shape=jax.ShapeDtypeStruct(shape, F32),
        compiler_params=params(),
        name="assemble",
    )(*gots)


def silu_slope(values):
    sig = jax.nn.sigmoid(values)
    return sig * (1.0 + values * (1.0 - sig))


def norm_back(values, gain, grad):
    back = jax.vjp(rms_gain, values, gain)[1](grad)
    return back


def ffn_gate(normed, gate_up):
    both = dot(normed, gate_up, 1, 0)
    width = both.shape[1] // 2
    return both, (jax.nn.silu(both[:, :width]) * both[:, width:]).astype(BF)


def ffn_gate_back(grad_hidden, both):
    width = both.shape[1] // 2
    gate, up = both[:, :width], both[:, width:]
    return jnp.concatenate(
        [grad_hidden * up * silu_slope(gate), grad_hidden * jax.nn.silu(gate)], axis=1
    ).astype(BF)


def plane_local(
    activations,
    cotangent,
    carried_state,
    carried_kv,
    row_lengths,
    mamba_gain,
    mamba_in,
    conv_weight,
    conv_bias,
    selection,
    step_proj,
    step_bias,
    decay_log,
    skip_gain,
    mamba_out,
    first_gain,
    first_gate_up,
    first_down,
    attention_gain,
    attention_qkv,
    attention_out,
    second_gain,
    second_gate_up,
    second_down,
):
    rows, group, wide = activations.shape
    planes, inner = lax.axis_size(SQUARES), lax.axis_size("c")
    members = planes * inner
    u, c, y, x, v = (lax.axis_index(name) for name in EVERY)
    member = (y * 2 + x) * inner + c
    place = (y * 2 + x) * inner + v
    offset = jnp.arange(members) ^ member
    order = (((offset & 1) << 2) | (offset >> 1)).astype(jnp.int32)
    shard = mamba_gain.shape[0]
    channels = skip_gain.shape[0]
    width = channels * planes
    rank = step_proj.shape[0]
    states = decay_log.shape[0]
    units = first_down.shape[0]
    head_width = wide // planes
    cache_rows = carried_kv.shape[1]

    def parts_of(product_of):
        return product_of.astype(BF).reshape(members, rows, group, wide)

    gains = jnp.stack([mamba_gain, first_gain, attention_gain, second_gain], axis=1)
    gains = jnp.pad(gains, ((0, 0), (0, 124)))
    payload = mamba_in.reshape(shard, 2, members, width).transpose(2, 0, 1, 3)
    spread = jnp.broadcast_to(gains[None], (members,) + gains.shape)
    payload = payload.reshape(members, shard, 2 * width)
    payload = jnp.concatenate([payload[:, :, :width], spread, payload[:, :, width:]], axis=2)
    dealt = trade(payload, PLANE)
    tokens = swap_planes(tie(activations, payload))
    stream = tokens.astype(F32)
    own_inner = rows_of(gather_squares(dealt[:, :, : width + 128]))
    gains = own_inner[:, width : width + 4].T.astype(F32)
    own_inner = own_inner[:, :width]
    normed = gather_plane(tie(tokens, dealt)).reshape(-1, wide).astype(F32)
    normed = rms_gain(normed, gains[0]).astype(BF)


    cuts = (selection.shape[1], rank, CONV, 1, 1, states, 1)
    packed = jnp.concatenate(
        [
            selection.astype(F32),
            step_proj.astype(F32).T,
            conv_weight.astype(F32).T,
            conv_bias.astype(F32)[:, None],
            step_bias[:, None],
            decay_log.T,
            skip_gain[:, None],
        ],
        axis=1,
    )
    packed = jnp.pad(packed, ((0, 0), (0, -packed.shape[1] % 128)))
    packed = gather_small(relocate(tie(packed, tokens), False), SQUARES).reshape(width, -1)
    starts = [sum(cuts[:index]) for index in range(len(cuts) + 1)]
    pieces = [packed[:, starts[index] : starts[index + 1]] for index in range(len(cuts))]
    own_selection = pieces[0].astype(BF)
    own_step_proj = pieces[1].astype(BF)
    taps = pieces[2].T
    tap_bias = pieces[3].T
    own_step_bias = pieces[4].T
    decay = -jnp.exp(pieces[5].T)
    skip = pieces[6].T
    moved = jnp.concatenate([mamba_out, attention_out], axis=0)
    moved = relocate(tie(moved, packed), False)
    own_out = gather_squares(moved[:channels]).reshape(width, wide)
    start = lax.dynamic_slice_in_dim(carried_state, place * width, width, 2)
    marks = jnp.broadcast_to(row_lengths.astype(F32)[:, None, None], (rows, 8, width))
    start = swap_planes(tie(jnp.concatenate([start, marks], axis=1), packed))
    lengths = start[:, states, 0].astype(jnp.int32)
    start = start[:, :states]
    own_gate = rows_of(gather_squares(tie(dealt[:, :, width + 128 :], normed)))

    def hidden_columns(gate_up):
        split = gate_up.reshape(shard, 2, 2, 2, 2, 2, 2, units)
        return split.transpose(4, 5, 3, 0, 1, 2, 6, 7).reshape(members, shard, -1)

    split = attention_qkv.reshape(shard, 3, planes, head_width).transpose(2, 0, 1, 3)
    split = jnp.broadcast_to(
        split.reshape(planes, 1, shard, 3 * head_width), (planes, inner, shard, 3 * head_width)
    )
    split = split.reshape(members, shard, 3 * head_width)
    dealt_first = trade(tie(hidden_columns(first_gate_up), normed), PLANE)
    own_first_down = gather_squares(first_down).reshape(-1, wide)

    def heads_of(block):
        return jnp.stack(
            [
                block[r, :, g * head_width : (g + 1) * head_width]
                for g in range(planes)
                for r in range(rows)
            ]
        )

    late_keys = swap_planes(tie(carried_kv[:, :, :wide], tokens))
    cached_keys = trade(tie(heads_of(late_keys), normed), PLANE)
    late = jnp.concatenate([carried_kv[:, :, wide:], cotangent.reshape(rows, -1, wide)], axis=1)
    late = swap_planes(tie(late, normed))

    inner_part = dot(normed, own_inner, 1, 0).reshape(members, rows, group, width)
    total, mixed, mixed_low = conv_forward(order, inner_part, taps, tap_bias)
    flat_low = mixed_low.reshape(-1, width)
    select = sum_plane(dot(flat_low, own_selection, 1, 0).reshape(members, rows, group, -1))
    gate = dot(normed, own_gate, 1, 0).reshape(members, rows, group, width)
    select, dealt_first, cached_keys, late = settle(select, dealt_first, cached_keys, late)
    step_low = select[..., :rank].astype(BF).reshape(-1, rank)
    pre = dot(step_low, own_step_proj, 1, 1).reshape(members, rows, group, width) + own_step_bias
    blocks = jnp.zeros((members,), jnp.int32).at[order].set(jnp.arange(members, dtype=jnp.int32))
    positions = blocks[:, None] * group + jnp.arange(group)[None, :]
    valid = (positions[:, None, :] < lengths[None, :, None]).astype(F32)[..., None]
    step = jax.nn.softplus(pre) * valid
    cached_contents = trade(tie(heads_of(late[:, :cache_rows]), step), PLANE)
    wide_shape = (members, rows, group, states, 128)
    wide_b = jnp.broadcast_to(select[..., rank : rank + states, None], wide_shape)
    wide_c = jnp.broadcast_to(select[..., rank + states :, None], wide_shape)
    core, past, end = scan_forward(order, mixed, step, wide_b, wide_c, decay, start)
    core, cached_contents = settle(core, cached_contents)
    own_first = rows_of(gather_squares(dealt_first))
    dealt_qkv = trade(tie(split, core), PLANE)
    rear = gather_squares(jnp.concatenate([moved[channels:], second_down], axis=0))
    mixed_out = core + skip * mixed
    gated = (mixed_out * jax.nn.silu(gate)).astype(BF).reshape(-1, width)
    first_stream = stream + scatter_plane(parts_of(dot(gated, own_out, 1, 0)))
    first_stream, dealt_qkv = settle(first_stream, dealt_qkv)
    own_qkv = rows_of(gather_squares(dealt_qkv))

    first_normed = gather_plane(rms_gain(first_stream, gains[1]).astype(BF)).reshape(-1, wide)
    dealt_second = trade(tie(hidden_columns(second_gate_up), first_normed), PLANE)
    first_both, first_hidden = ffn_gate(first_normed, own_first)
    second_stream = first_stream + scatter_plane(parts_of(dot(first_hidden, own_first_down, 1, 0)))

    second_stream, dealt_second = settle(second_stream, dealt_second)
    own_second = rows_of(gather_squares(dealt_second))

    def rows_parts(product_of):
        return product_of.astype(BF).reshape(members, group, wide)

    grad = late[:, cache_rows:].reshape(rows, group, wide)
    own_attention_out = rear[:, :shard]
    own_attention_out = in_order(own_attention_out, other(own_attention_out, "c"), "c")
    own_attention_out = own_attention_out.reshape(-1, wide)
    own_second_down = rear[:, shard:].reshape(-1, wide)
    length = jnp.concatenate([lax.dynamic_slice_in_dim(lengths, c, 1), member[None]])
    normed_rows = rows_gather(rms_gain(second_stream, gains[2]).astype(BF)).reshape(-1, wide)
    qkv = dot(normed_rows, own_qkv, 1, 0).astype(BF)
    grad_whole = gather_plane(tie(grad, qkv)).reshape(-1, wide)
    grad = grad.astype(F32)
    attended, log = attend(length, qkv, cached_keys, cached_contents)
    attended_low = attended.astype(BF)
    third_stream = second_stream + rows_scatter(rows_parts(dot(attended_low, own_attention_out, 1, 0)))
    own_kv = qkv[:, head_width:].reshape(members, group, 2, head_width).transpose(0, 2, 1, 3)
    own_kv = tie(own_kv, third_stream).reshape(2, 2, inner, 2, group, head_width)

    second_normed = gather_plane(rms_gain(third_stream, gains[3]).astype(BF)).reshape(-1, wide)
    second_both, second_hidden = ffn_gate(second_normed, own_second)
    second_parts = parts_of(dot(second_hidden, own_second_down, 1, 0))
    fourth_stream = third_stream + scatter_plane(second_parts)
    def hidden_back(got):
        moves = []
        for column in range(2 * planes * members):
            part, uu, cc, yx, vv = column >> 5, column >> 4 & 1, column >> 3 & 1, column >> 1 & 3, column & 1
            source = (0, yx * 2 + cc, ((part * 2 + uu) * 2 + vv) * units, units)
            moves.append(((0, column * units), shard, source))
        return assemble([got], moves, (shard, 2 * planes * members * units))

    def cache_back(part):
        part = part.reshape(planes, rows, cache_rows, head_width)
        return swap_planes(jnp.concatenate([part[g] for g in range(planes)], axis=2))

    grad_both = ffn_gate_back(dot(grad_whole, own_second_down, 1, 1), second_both)
    grad_normed = scatter_plane(parts_of(dot(grad_both, own_second, 1, 1)))
    second_columns = reduce_squares(by_square(dot(second_normed, grad_both, 0, 0).astype(BF)))
    second_rows = dot(second_hidden, grad_whole, 0, 0).astype(BF)
    grad_stream, second_gain_grad = norm_back(third_stream, gains[3], grad_normed)
    grad = grad + grad_stream

    grad_rows = rows_gather(grad.astype(BF)).reshape(-1, wide)
    grad_attended = dot(grad_rows, own_attention_out, 1, 1).astype(BF)
    own_kv = kv_owners(tie(own_kv, grad_attended))
    returned = swap_planes(jnp.concatenate([fourth_stream.astype(BF), own_kv], axis=2))
    output, segment_kv = returned[..., :wide], returned[..., wide:]
    back_keys, back_contents, dq, dk, dv = attend_back(
        length, qkv, grad_attended, attended, log, cached_keys, cached_contents
    )
    grad_qkv = jnp.concatenate([dq, dk, dv], axis=1)
    grad_normed = rows_scatter(rows_parts(dot(grad_qkv, own_qkv, 1, 1)))
    grad_stream, attention_gain_grad = norm_back(second_stream, gains[2], grad_normed)
    grad = grad + grad_stream
    grad, second_columns = settle(grad, second_columns)

    grad_out = dot(attended_low, grad_rows, 0, 0).astype(BF).reshape(inner, planes, shard, wide)
    grad_out = pair_sum(grad_out, "c").astype(BF)
    attention_out_grad = reduce_squares(grad_out)
    second_down_grad = reduce_squares(second_rows.reshape(planes, units, wide)).astype(F32)
    qkv_columns = reduce_squares(by_square(dot(normed_rows, grad_qkv, 0, 0).astype(BF)))

    grad_whole = gather_plane(grad.astype(BF)).reshape(-1, wide)
    grad_whole, second_down_grad = settle(grad_whole, second_down_grad)
    back_keys = trade(tie(back_keys, grad_whole), PLANE)
    grad_both = ffn_gate_back(dot(grad_whole, own_first_down, 1, 1), first_both)
    grad_normed = scatter_plane(parts_of(dot(grad_both, own_first, 1, 1)))
    first_columns = reduce_squares(by_square(dot(first_normed, grad_both, 0, 0).astype(BF)))
    first_rows = dot(first_hidden, grad_whole, 0, 0).astype(BF)
    grad_stream, first_gain_grad = norm_back(first_stream, gains[1], grad_normed)
    grad = grad + grad_stream
    grad, qkv_columns, attention_out_grad = settle(grad, qkv_columns, attention_out_grad)
    first_down_grad = reduce_squares(first_rows.reshape(planes, units, wide)).astype(F32)

    grad_whole = gather_plane(grad.astype(BF)).reshape(-1, wide)
    grad_whole, back_keys = settle(grad_whole, back_keys)
    back_keys = cache_back(back_keys)
    second_got = trade(tie(second_columns, grad_whole), PLANE)
    grad_gated = dot(grad_whole, own_out, 1, 1).reshape(mixed.shape)
    grad_core = grad_gated * jax.nn.silu(gate)
    grad_core, second_got = settle(grad_core, second_got)
    second_gate_up_grad = hidden_back(second_got)
    back_contents = trade(tie(back_contents, grad_core), PLANE)
    grad_gate = (grad_gated * mixed_out * silu_slope(gate)).astype(BF).reshape(-1, width)
    skip_grad = jnp.sum(grad_core * mixed, axis=(0, 1, 2))
    grad_mixed, grad_step, grad_b, grad_c, grad_decay, grad_start = scan_back(
        order, mixed, step, wide_b, wide_c, grad_core, past, decay, end
    )
    new_state, grad_state = swap_planes(jnp.stack([end, grad_start]))
    grad_out = dot(gated, grad_whole, 0, 0).astype(BF).reshape(planes, channels, wide)
    out_rows = reduce_squares(grad_out)
    gate_columns = reduce_squares(by_square(dot(normed, grad_gate, 0, 0).astype(BF)))
    grad_step, back_contents, first_columns, first_down_grad = settle(
        grad_step, back_contents, first_columns, first_down_grad
    )
    back_contents = cache_back(back_contents)
    got = trade(tie(qkv_columns, grad_step), PLANE)
    grad_pre = grad_step * valid * jax.nn.sigmoid(pre)
    step_bias_grad = jnp.sum(grad_pre, axis=(0, 1, 2))
    grad_pre = grad_pre.astype(BF).reshape(-1, width)
    step_proj_grad = dot(grad_pre, step_low, 0, 0)
    grad_low = dot(grad_pre, own_step_proj, 1, 0).reshape(members, rows, group, rank)
    grad_select = sum_plane(jnp.concatenate(
            [grad_low] + [jnp.sum(part.astype(F32), axis=-1) for part in (grad_b, grad_c)], axis=-1
        ))
    grad_select = grad_select.astype(BF).reshape(-1, rank + 2 * states)
    grad_select, got, gate_columns, out_rows, back_keys = settle(
        grad_select, got, gate_columns, out_rows, back_keys
    )
    got = jnp.sum(got.reshape(planes, inner, shard, -1).astype(F32), axis=1)
    moves = []
    for owner in range(planes):
        for part in range(3):
            source = (0, owner, part * head_width, head_width)
            moves.append(((0, part * wide + owner * head_width), shard, source))
    attention_qkv_grad = assemble([got], moves, (shard, 3 * wide))
    selection_grad = dot(flat_low, grad_select, 0, 0)
    grad_mixed = (
        grad_mixed
        + grad_core * skip
        + dot(grad_select, own_selection, 1, 1).reshape(mixed.shape)
    )
    grad_inner, tap_sums = conv_back(order, grad_mixed, total, inner_part, taps)
    grad_inner = grad_inner.reshape(-1, width)
    first_got = trade(tie(first_columns, grad_inner), PLANE)
    first_gate_up_grad = hidden_back(first_got)
    inner_columns = by_square(dot(normed, grad_inner, 0, 0).astype(BF))
    grad_inner = tie(grad_inner, inner_columns)
    inner_columns = reduce_squares(inner_columns)
    parts = dot(grad_inner, own_inner, 1, 1) + dot(grad_gate, own_gate, 1, 1)
    gate_columns = trade(tie(gate_columns, grad_inner), PLANE)
    moved = relocate(jnp.concatenate([out_rows, attention_out_grad], axis=0), True).astype(F32)
    mamba_out_grad, attention_out_grad = moved[:channels], moved[channels:]
    grad_normed = scatter_plane(parts_of(parts))
    grad_normed, inner_columns = settle(grad_normed, inner_columns)
    inner_columns = trade(inner_columns, PLANE)
    grad_stream, mamba_gain_grad = norm_back(stream, gains[0], grad_normed)
    grad_input = swap_planes(grad + grad_stream)
    moves = []
    for which in range(2):
        for owner in range(members):
            column = (which * members + owner) * width
            moves.append(((0, column), shard, (which, owner, 0, width)))
    mamba_in_grad = assemble([inner_columns, gate_columns], moves, mamba_in.shape)
    packed = jnp.concatenate(
        [
            selection_grad,
            step_proj_grad,
            tap_sums[: CONV + 1].T,
            step_bias_grad[:, None],
            (grad_decay * decay).T,
            skip_grad[:, None],
        ],
        axis=1,
    )
    packed = jnp.pad(packed, ((0, 0), (0, -packed.shape[1] % 128)))
    packed = pair_sum(pair_sum(packed.reshape(2, 2, channels, -1), "u"), "v")
    packed = relocate(packed, True)
    pieces = [packed[:, starts[index] : starts[index + 1]] for index in range(len(cuts))]

    gain_grads = jnp.stack([mamba_gain_grad, first_gain_grad, attention_gain_grad, second_gain_grad])
    index = (u * 2 + c) * members + place
    gain_grads = lax.dynamic_slice_in_dim(total_small(gain_grads), index * shard, shard, 1)
    return (
        output,
        new_state,
        segment_kv,
        grad_input,
        grad_state,
        jnp.concatenate([back_keys, back_contents], axis=2).astype(F32),
        gain_grads[0],
        mamba_in_grad,
        pieces[2].T,
        pieces[3][:, 0],
        pieces[0],
        pieces[1].T,
        pieces[4][:, 0],
        pieces[5].T,
        pieces[6][:, 0],
        mamba_out_grad,
        gain_grads[1],
        first_gate_up_grad,
        first_down_grad,
        gain_grads[2],
        attention_qkv_grad,
        attention_out_grad,
        gain_grads[3],
        second_gate_up_grad,
        second_down_grad,
    )


def placements(dp, seq):
    every = dp + seq
    places = (
        P(dp, seq, None),
        P(dp, seq, None),
        P(dp, None, None),
        P(dp, seq, None),
        P(dp),
        P(every),
        P(every, None),
        P(None, every),
        P(every),
        P(every, None),
        P(None, every),
        P(every),
        P(None, every),
        P(every),
        P(every, None),
        P(every),
        P(every, None),
        P(every, None),
        P(every),
        P(every, None),
        P(every, None),
        P(every),
        P(every, None),
        P(every, None),

    )
    results = (
        P(dp, seq, None),
        P(dp, None, seq),
        P(dp, seq, None),
        P(dp, seq, None),
        P(dp, None, seq),
        P(dp, seq, None),
        P(every),
        P(every, None),
        P(None, every),
        P(every),
        P(every, None),
        P(None, every),
        P(every),
        P(None, every),
        P(every),
        P(every, None),
        P(every),
        P(every, None),
        P(every, None),
        P(every),
        P(every, None),
        P(every, None),
        P(every),
        P(every, None),
        P(every, None),

    )
    return places, results


def plane_fits(mesh):
    dp, seq = mesh.shape["dp"], mesh.shape["seq"]
    return dp == 4 and seq == 2 * dp


def solution(mesh):
    if not plane_fits(mesh):
        places, results = placements(("dp",), ("seq",))
        return jax.shard_map(
            local, mesh=mesh, in_specs=places, out_specs=results, check_vma=False
        )
    dp, seq = mesh.shape["dp"], mesh.shape["seq"]
    devices = mesh.devices.reshape(dp // 2, 2, seq // 4, 2, 2)
    places, results = placements(("u", "c"), ("y", "x", "v"))
    return jax.shard_map(
        plane_local,
        mesh=Mesh(devices, EVERY),
        in_specs=places,
        out_specs=results,
        check_vma=False,
    )
```

```python
import jax
import jax.numpy as jnp
from jax import lax
from jax.experimental import pallas as pl
from jax.experimental.pallas import tpu as pltpu
from jax.sharding import Mesh
from jax.sharding import PartitionSpec as P

HEAD_DIM = 128
CONV = 4
WINDOW = 2048


EPSILON = 1e-05
NEGATIVE = -1e30


def shifted(block, axis, distance):
    devices = range(lax.axis_size(axis))
    route = [(i - distance, i) for i in devices if i - distance in devices]
    return lax.ppermute(block, axis, route)


def carried_in(part, axis, combine, identity, reverse):
    count = lax.axis_size(axis)
    place = lax.axis_index(axis)
    ahead = count - 1 - place if reverse else place
    gathered = jax.tree.map(lambda a: lax.all_gather(a, axis), part)
    state = jax.tree.map(lambda a, e: jnp.zeros_like(a) + jnp.asarray(e, a.dtype), part, identity)

    def one(lap, state):
        source = count - 1 - lap if reverse else lap
        return combine(
            state, jax.tree.map(lambda a: lax.dynamic_index_in_dim(a, source, 0, False), gathered)
        )

    return lax.fori_loop(0, ahead, one, state)


def rms_gain(values, gain):
    return values * lax.rsqrt(jnp.mean(values * values, axis=-1, keepdims=True) + EPSILON) * gain


def product(left, right):
    return lax.dot_general(
        left, right, (((left.ndim - 1,), (0,)), ((), ())), preferred_element_type=jnp.float32
    )


def product_back(left, right):
    return lax.dot_general(
        left, right, (((left.ndim - 1,), (1,)), ((), ())), preferred_element_type=jnp.float32
    )


def outer(left, right):
    flat_left = left.reshape(-1, left.shape[-1])
    flat_right = right.reshape(-1, right.shape[-1])
    return lax.dot_general(
        flat_left, flat_right, (((0,), (0,)), ((), ())), preferred_element_type=jnp.float32
    )


def fetch_front(shards):
    return (
        lax.all_gather(shards[0], ("dp", "seq"), axis=0, tiled=True),
        lax.all_gather(shards[1], ("dp", "seq"), axis=0, tiled=True),
        lax.all_gather(shards[2], ("dp", "seq"), axis=1, tiled=True),
        lax.all_gather(shards[3], ("dp", "seq"), axis=0, tiled=True),
        lax.all_gather(shards[4], ("dp", "seq"), axis=0, tiled=True),
        lax.all_gather(shards[5], ("dp", "seq"), axis=1, tiled=True),
        lax.all_gather(shards[6].astype(jnp.bfloat16), ("dp", "seq"), axis=0, tiled=True).astype(
            jnp.float32
        ),
        lax.all_gather(shards[7].astype(jnp.bfloat16), ("dp", "seq"), axis=1, tiled=True).astype(
            jnp.float32
        ),
        lax.all_gather(shards[8].astype(jnp.bfloat16), ("dp", "seq"), axis=0, tiled=True).astype(
            jnp.float32
        ),
        lax.all_gather(shards[9], ("dp", "seq"), axis=0, tiled=True),
        lax.all_gather(shards[10], ("dp", "seq"), axis=0, tiled=True),
        lax.all_gather(shards[11], ("dp", "seq"), axis=0, tiled=True),
        lax.all_gather(shards[12], ("dp", "seq"), axis=0, tiled=True),
    )


def settle_front(grads):
    return (
        lax.psum_scatter(grads[0], ("dp", "seq"), scatter_dimension=0, tiled=True),
        lax.psum_scatter(grads[1], ("dp", "seq"), scatter_dimension=0, tiled=True),
        lax.psum_scatter(grads[2], ("dp", "seq"), scatter_dimension=1, tiled=True),
        lax.psum_scatter(grads[3], ("dp", "seq"), scatter_dimension=0, tiled=True),
        lax.psum_scatter(grads[4], ("dp", "seq"), scatter_dimension=0, tiled=True),
        lax.psum_scatter(grads[5], ("dp", "seq"), scatter_dimension=1, tiled=True),
        lax.psum_scatter(grads[6], ("dp", "seq"), scatter_dimension=0, tiled=True),
        lax.psum_scatter(grads[7], ("dp", "seq"), scatter_dimension=1, tiled=True),
        lax.psum_scatter(grads[8], ("dp", "seq"), scatter_dimension=0, tiled=True),
        lax.psum_scatter(grads[9], ("dp", "seq"), scatter_dimension=0, tiled=True),
        lax.psum_scatter(grads[10], ("dp", "seq"), scatter_dimension=0, tiled=True),
        lax.psum_scatter(grads[11], ("dp", "seq"), scatter_dimension=0, tiled=True),
        lax.psum_scatter(grads[12], ("dp", "seq"), scatter_dimension=0, tiled=True),
    )


def fetch_rear(shards):
    return (
        lax.all_gather(shards[0], ("dp", "seq"), axis=0, tiled=True),
        lax.all_gather(shards[1], ("dp", "seq"), axis=0, tiled=True),
        lax.all_gather(shards[2], ("dp", "seq"), axis=0, tiled=True),
        lax.all_gather(shards[3], ("dp", "seq"), axis=0, tiled=True),
        lax.all_gather(shards[4], ("dp", "seq"), axis=0, tiled=True),
        lax.all_gather(shards[5], ("dp", "seq"), axis=0, tiled=True),
    )


def settle_rear(grads):
    return (
        lax.psum_scatter(grads[0], ("dp", "seq"), scatter_dimension=0, tiled=True),
        lax.psum_scatter(grads[1], ("dp", "seq"), scatter_dimension=0, tiled=True),
        lax.psum_scatter(grads[2], ("dp", "seq"), scatter_dimension=0, tiled=True),
        lax.psum_scatter(grads[3], ("dp", "seq"), scatter_dimension=0, tiled=True),
        lax.psum_scatter(grads[4], ("dp", "seq"), scatter_dimension=0, tiled=True),
        lax.psum_scatter(grads[5], ("dp", "seq"), scatter_dimension=0, tiled=True),
    )


def ffn_forward(values, weights):
    gain, gate_up, down = weights
    width = down.shape[0]
    normed = rms_gain(values, gain.astype(jnp.float32)).astype(jnp.bfloat16)
    both = product(normed, gate_up)
    hidden = (jax.nn.silu(both[..., :width]) * both[..., width:]).astype(jnp.bfloat16)
    return (values + product(hidden, down), (normed, both, hidden))


def ffn_backward(values, grad, weights, kept):
    gain, gate_up, down = weights
    normed, both, hidden = kept
    width = down.shape[0]
    grad_low = grad.astype(jnp.bfloat16)
    grad_down = outer(hidden, grad_low)
    grad_hidden = product_back(grad_low, down)

    def ffn_gating(pair):
        return jax.nn.silu(pair[..., :width]) * pair[..., width:]

    unused, gating_back = jax.vjp(ffn_gating, both)
    grad_both = gating_back(grad_hidden)[0].astype(jnp.bfloat16)
    grad_gate_up = outer(normed, grad_both)
    grad_normed = product_back(grad_both, gate_up)
    unused, norm_back = jax.vjp(rms_gain, values, gain.astype(jnp.float32))
    grad_values, grad_gain = norm_back(grad_normed)
    return (grad + grad_values, (grad_gain, grad_gate_up, grad_down))


def convolve(before, inner, conv_weight, conv_bias):
    group = inner.shape[1]
    padded = jnp.concatenate([before, inner], axis=1)
    total = conv_bias
    for index in range(CONV):
        total = total + conv_weight[index] * padded[:, index : index + group]
    return jax.nn.silu(total)


def recurrence(decay):

    def advance(carry, slot):
        mixed_now, step_now, input_now, output_now = slot
        carry = (
            jnp.exp(step_now[:, None, :] * decay) * carry
            + (step_now * mixed_now)[:, None, :] * input_now[:, :, None]
        )
        return (carry, jnp.sum(output_now[:, :, None] * carry, axis=1))

    return advance


def selective(mixed, step, inputs_b, outputs_c, decay, state):
    slots = tuple((jnp.moveaxis(item, 1, 0) for item in (mixed, step, inputs_b, outputs_c)))
    state_end, core = lax.scan(recurrence(decay), state, slots, unroll=8)
    return (jnp.moveaxis(core, 0, 1), state_end)


def chain(earlier, later):
    return (earlier[0] * later[0], later[0] * earlier[1] + later[1])


def chain_both(earlier, later):
    return (
        earlier[0] * later[0],
        later[0] * earlier[1] + later[1],
        earlier[2] * later[2],
        earlier[2] * later[3] + earlier[3],
    )


def stepping(pre, step_bias, valid):
    return jax.nn.softplus(pre + step_bias) * valid[..., None]


def mamba_forward(values, lengths, carried_state, weights):
    (
        gain,
        mamba_in,
        conv_weight,
        conv_bias,
        selection,
        step_proj,
        step_bias,
        decay_log,
        skip_gain,
        mamba_out,
    ) = weights
    rows, group, width = values.shape
    inner_width = mamba_out.shape[0]
    rank = step_proj.shape[0]
    states = decay_log.shape[0]
    shard = lax.axis_index("seq")
    positions = shard * group + jnp.arange(group)
    valid = (positions[None, :] < lengths[:, None]).astype(jnp.float32)
    normed = rms_gain(values, gain.astype(jnp.float32)).astype(jnp.bfloat16)
    projected = product(normed, mamba_in)
    inner = projected[..., :inner_width]
    gate = projected[..., inner_width:]
    before = shifted(inner[:, group - CONV + 1 :], "seq", 1)
    mixed = convolve(before, inner, conv_weight.astype(jnp.float32), conv_bias.astype(jnp.float32))
    mixed_low = mixed.astype(jnp.bfloat16)
    select = product(mixed_low, selection)
    step_low = select[..., :rank].astype(jnp.bfloat16)
    inputs_b = select[..., rank : rank + states]
    outputs_c = select[..., rank + states :]
    pre = product(step_low, step_proj)
    step = stepping(pre, step_bias.astype(jnp.float32), valid)
    decay = -jnp.exp(decay_log.astype(jnp.float32))
    empty = jnp.zeros((rows, states, inner_width), jnp.float32)
    local_end = selective(mixed, step, inputs_b, outputs_c, decay, empty)[1]
    through = jnp.exp(decay * jnp.sum(step, axis=1)[:, None, :])
    prefix_decay, prefix_state = carried_in(
        (through, local_end), "seq", chain, (jnp.ones_like(through), empty), False
    )
    state = prefix_decay * carried_state + prefix_state
    core, state_end = selective(mixed, step, inputs_b, outputs_c, decay, state)
    mixed_out = core + skip_gain.astype(jnp.float32) * mixed
    gated = (mixed_out * jax.nn.silu(gate)).astype(jnp.bfloat16)
    kept = (
        valid,
        normed,
        projected,
        before,
        mixed,
        mixed_low,
        step_low,
        pre,
        step,
        inputs_b,
        outputs_c,
        decay,
        state,
        through,
        prefix_decay,
        mixed_out,
        gated,
        local_end,
        state_end,
    )
    return (values + product(gated, mamba_out), kept)


def mamba_backward(values, grad, weights, kept):
    (
        gain,
        mamba_in,
        conv_weight,
        conv_bias,
        selection,
        step_proj,
        step_bias,
        decay_log,
        skip_gain,
        mamba_out,
    ) = weights
    (
        valid,
        normed,
        projected,
        before,
        mixed,
        mixed_low,
        step_low,
        pre,
        step,
        inputs_b,
        outputs_c,
        decay,
        state,
        through,
        prefix_decay,
        mixed_out,
        gated,
        local_end,
        state_end,
    ) = kept
    group = values.shape[1]
    inner_width = mamba_out.shape[0]
    grad_low = grad.astype(jnp.bfloat16)
    grad_out = outer(gated, grad_low)
    grad_gated = product_back(grad_low, mamba_out)
    gate = projected[..., inner_width:]

    def mamba_gating(mixed_part, gate_part):
        return mixed_part * jax.nn.silu(gate_part)

    unused, gating_back = jax.vjp(mamba_gating, mixed_out, gate)
    grad_mixed_out, grad_gate = gating_back(grad_gated)
    skip = skip_gain.astype(jnp.float32)
    grad_skip = jnp.sum(grad_mixed_out * mixed, axis=(0, 1))
    unused, scan_back = jax.vjp(selective, mixed, step, inputs_b, outputs_c, decay, state)
    zero = jnp.zeros_like(state)
    ones = jnp.ones_like(state)
    own = scan_back((grad_mixed_out, zero))[5]
    suffix = carried_in(
        (through, own, through, local_end), "seq", chain_both, (ones, zero, ones, zero), True
    )
    final = suffix[2] * state_end + suffix[3]
    piece_width = inner_width // lax.axis_size("seq")
    new_state = lax.dynamic_slice_in_dim(final, lax.axis_index("seq") * piece_width, piece_width, 2)
    grad_state = lax.psum_scatter(prefix_decay * own, "seq", scatter_dimension=2, tiled=True)
    grad_mixed, grad_step, grad_inputs, grad_outputs, grad_decay, unused_state = scan_back(
        (grad_mixed_out, suffix[1])
    )
    grad_mixed = grad_mixed + grad_mixed_out * skip
    unused, step_back = jax.vjp(
        lambda pre_part, bias_part: stepping(pre_part, bias_part, valid),
        pre,
        step_bias.astype(jnp.float32),
    )
    grad_pre, grad_step_bias = step_back(grad_step)
    grad_pre_low = grad_pre.astype(jnp.bfloat16)
    grad_step_proj = outer(step_low, grad_pre_low)
    grad_step_low = product_back(grad_pre_low, step_proj)
    grad_select = jnp.concatenate([grad_step_low, grad_inputs, grad_outputs], axis=-1).astype(
        jnp.bfloat16
    )
    grad_selection = outer(mixed_low, grad_select)
    grad_mixed = grad_mixed + product_back(grad_select, selection)
    inner = projected[..., :inner_width]
    unused, conv_back = jax.vjp(
        convolve, before, inner, conv_weight.astype(jnp.float32), conv_bias.astype(jnp.float32)
    )
    grad_before, grad_inner, grad_conv_weight, grad_conv_bias = conv_back(grad_mixed)
    returned = shifted(grad_before, "seq", -1)
    grad_inner = jnp.concatenate(
        [grad_inner[:, : group - CONV + 1], grad_inner[:, group - CONV + 1 :] + returned], axis=1
    )
    grad_projected = jnp.concatenate([grad_inner, grad_gate], axis=-1).astype(jnp.bfloat16)
    grad_in = outer(normed, grad_projected)
    grad_normed = product_back(grad_projected, mamba_in)
    unused, norm_back = jax.vjp(rms_gain, values, gain.astype(jnp.float32))
    grad_values, grad_gain = norm_back(grad_normed)
    grads = (
        grad_gain,
        grad_in,
        grad_conv_weight,
        grad_conv_bias,
        grad_selection,
        grad_step_proj,
        grad_step_bias,
        grad_decay * decay,
        grad_skip,
        grad_out,
    )
    return (grad + grad_values, grads, grad_state, new_state)


def key_positions(start, count, cache_rows, group):
    index = start + jnp.arange(count)
    owner = index // (cache_rows + group)
    offset = index % (cache_rows + group)
    return jnp.where(
        offset < cache_rows,
        owner * cache_rows + offset - WINDOW,
        owner * group + offset - cache_rows,
    )


def visible(query_pos, key_pos, lengths):
    near = (key_pos[None, :] > query_pos[:, None] - WINDOW) & (
        key_pos[None, :] <= query_pos[:, None]
    )
    real = (key_pos[None, None, :] < lengths[:, None, None]) | (
        key_pos[None, None, :] == query_pos[None, :, None]
    )
    return (near[None] & real)[:, :, None, :]


def blockwise(step_fn, carry, piece, size):
    count = jax.tree.leaves(piece)[0].shape[1]
    blocks = count // size

    def split(item):
        return jnp.moveaxis(item.reshape((item.shape[0], blocks, size) + item.shape[2:]), 1, 0)

    def turn(inner, pair):
        return (step_fn(inner, pair[1], pair[0] * size), None)

    carry, unused = lax.scan(turn, carry, (jnp.arange(blocks), jax.tree.map(split, piece)))
    return carry


def over_keys(local_kv, fold, init):
    return fold(init, lax.all_gather(local_kv, "seq", axis=1, tiled=True), jnp.int32(0))


def attention_forward(values, lengths, carried_kv, weights):
    gain, qkv_proj, out_proj = weights
    rows, group, width = values.shape
    heads = width // HEAD_DIM
    cache_rows = carried_kv.shape[1]
    size = cache_rows + group
    scale = HEAD_DIM ** (-0.5)
    query_pos = lax.axis_index("seq") * group + jnp.arange(group)
    normed = rms_gain(values, gain.astype(jnp.float32)).astype(jnp.bfloat16)
    qkv = product(normed, qkv_proj).astype(jnp.bfloat16)
    queries = qkv[..., :width].reshape(rows, group, heads, HEAD_DIM)
    segment_kv = qkv[..., width:]
    local_kv = jnp.concatenate([carried_kv, segment_kv], axis=1)

    def one_block(carry, piece, start):
        count = piece.shape[1]
        inside = visible(query_pos, key_positions(start, count, cache_rows, group), lengths)

        def one_work(state):
            top, total, accum = state
            keys = piece[..., :width].reshape(rows, count, heads, HEAD_DIM)
            contents = piece[..., width:].reshape(rows, count, heads, HEAD_DIM)
            scores = (
                jnp.einsum("rqhd,rkhd->rqhk", queries, keys, preferred_element_type=jnp.float32)
                * scale
            )
            new_top = jnp.maximum(top, jnp.max(jnp.where(inside, scores, NEGATIVE), axis=-1))
            weights_now = jnp.exp(jnp.where(inside, scores - new_top[..., None], NEGATIVE))
            factor = jnp.exp(top - new_top)
            total = total * factor + jnp.sum(weights_now, axis=-1)
            accum = accum * factor[..., None] + jnp.einsum(
                "rqhk,rkhd->rqhd",
                weights_now.astype(jnp.bfloat16),
                contents,
                preferred_element_type=jnp.float32,
            )
            return (new_top, total, accum)

        return lax.cond(jnp.any(inside), one_work, lambda state: state, carry)

    init = (
        jnp.full((rows, group, heads), NEGATIVE, jnp.float32),
        jnp.zeros((rows, group, heads), jnp.float32),
        jnp.zeros((rows, group, heads, HEAD_DIM), jnp.float32),
    )
    top, total, accum = over_keys(
        local_kv, lambda carry, piece, start: blockwise(one_block, carry, piece, size), init
    )
    attended = accum / total[..., None]
    logsum = top + jnp.log(total)
    attended_low = attended.astype(jnp.bfloat16).reshape(rows, group, width)
    kept = (normed, queries, local_kv, attended, attended_low, logsum, query_pos)
    return (values + product(attended_low, out_proj), segment_kv, kept)


def attention_backward(values, grad, lengths, weights, kept):
    gain, qkv_proj, out_proj = weights
    normed, queries, local_kv, attended, attended_low, logsum, query_pos = kept
    rows, group, width = values.shape
    heads = width // HEAD_DIM
    size = local_kv.shape[1]
    cache_rows = size - group
    scale = HEAD_DIM ** (-0.5)
    grad_low = grad.astype(jnp.bfloat16)
    grad_out = outer(attended_low, grad_low)
    grad_attended = (
        product_back(grad_low, out_proj).astype(jnp.bfloat16).reshape(rows, group, heads, HEAD_DIM)
    )
    delta = jnp.sum(grad_attended.astype(jnp.float32) * attended, axis=-1)

    def query_block(carry, piece, start):
        count = piece.shape[1]
        inside = visible(query_pos, key_positions(start, count, cache_rows, group), lengths)

        def query_work(grad_queries):
            keys = piece[..., :width].reshape(rows, count, heads, HEAD_DIM)
            contents = piece[..., width:].reshape(rows, count, heads, HEAD_DIM)
            scores = (
                jnp.einsum("rqhd,rkhd->rqhk", queries, keys, preferred_element_type=jnp.float32)
                * scale
            )
            weights_now = jnp.exp(jnp.where(inside, scores - logsum[..., None], NEGATIVE))
            grad_weights = jnp.einsum(
                "rqhd,rkhd->rqhk", grad_attended, contents, preferred_element_type=jnp.float32
            )
            grad_scores = (weights_now * (grad_weights - delta[..., None])).astype(jnp.bfloat16)
            return (
                grad_queries
                + jnp.einsum(
                    "rqhk,rkhd->rqhd", grad_scores, keys, preferred_element_type=jnp.float32
                )
                * scale
            )

        return lax.cond(jnp.any(inside), query_work, lambda state: state, carry)

    grad_queries = over_keys(
        local_kv,
        lambda carry, piece, start: blockwise(query_block, carry, piece, size),
        jnp.zeros((rows, group, heads, HEAD_DIM), jnp.float32),
    )
    whole_logsum, whole_delta = (
        lax.all_gather(logsum, "seq", axis=1, tiled=True),
        lax.all_gather(delta, "seq", axis=1, tiled=True),
    )
    own_pos = key_positions(lax.axis_index("seq") * size, size, cache_rows, group)
    own_keys = local_kv[..., :width].reshape(rows, size, heads, HEAD_DIM)
    own_contents = local_kv[..., width:].reshape(rows, size, heads, HEAD_DIM)

    def key_block(carry, piece, start):
        part_queries, part_grads = piece
        count = part_queries.shape[1]
        inside = visible(start + jnp.arange(count), own_pos, lengths)

        def key_work(state):
            grad_keys, grad_contents = state
            part_logsum = lax.dynamic_slice_in_dim(whole_logsum, start, count, 1)
            part_delta = lax.dynamic_slice_in_dim(whole_delta, start, count, 1)
            scores = (
                jnp.einsum(
                    "rqhd,rkhd->rqhk", part_queries, own_keys, preferred_element_type=jnp.float32
                )
                * scale
            )
            weights_now = jnp.exp(jnp.where(inside, scores - part_logsum[..., None], NEGATIVE))
            grad_contents = grad_contents + jnp.einsum(
                "rqhk,rqhd->rkhd",
                weights_now.astype(jnp.bfloat16),
                part_grads,
                preferred_element_type=jnp.float32,
            )
            grad_weights = jnp.einsum(
                "rqhd,rkhd->rqhk", part_grads, own_contents, preferred_element_type=jnp.float32
            )
            grad_scores = (weights_now * (grad_weights - part_delta[..., None])).astype(
                jnp.bfloat16
            )
            grad_keys = (
                grad_keys
                + jnp.einsum(
                    "rqhk,rqhd->rkhd", grad_scores, part_queries, preferred_element_type=jnp.float32
                )
                * scale
            )
            return (grad_keys, grad_contents)

        return lax.cond(jnp.any(inside), key_work, lambda state: state, carry)

    empty = jnp.zeros((rows, size, heads, HEAD_DIM), jnp.float32)
    grad_keys, grad_contents = blockwise(
        key_block,
        (empty, empty),
        (
            lax.all_gather(queries, "seq", axis=1, tiled=True),
            lax.all_gather(grad_attended, "seq", axis=1, tiled=True),
        ),
        group,
    )
    grad_local = jnp.concatenate(
        [grad_keys.reshape(rows, size, width), grad_contents.reshape(rows, size, width)], axis=-1
    )
    grad_cache = grad_local[:, :cache_rows]
    grad_qkv = jnp.concatenate(
        [grad_queries.reshape(rows, group, width), grad_local[:, cache_rows:]], axis=-1
    ).astype(jnp.bfloat16)
    grad_qkv_proj = outer(normed, grad_qkv)
    grad_normed = product_back(grad_qkv, qkv_proj)
    unused, norm_back = jax.vjp(rms_gain, values, gain.astype(jnp.float32))
    grad_values, grad_gain = norm_back(grad_normed)
    return (grad + grad_values, (grad_gain, grad_qkv_proj, grad_out), grad_cache)


def local(
    activations,
    cotangent,
    carried_state,
    carried_kv,
    row_lengths,
    mamba_gain,
    mamba_in,
    conv_weight,
    conv_bias,
    selection,
    step_proj,
    step_bias,
    decay_log,
    skip_gain,
    mamba_out,
    first_gain,
    first_gate_up,
    first_down,
    attention_gain,
    attention_qkv,
    attention_out,
    second_gain,
    second_gate_up,
    second_down,
):
    front_shards = (
        mamba_gain,
        mamba_in,
        conv_weight,
        conv_bias,
        selection,
        step_proj,
        step_bias,
        decay_log,
        skip_gain,
        mamba_out,
        first_gain,
        first_gate_up,
        first_down,
    )
    rear_shards = (
        attention_gain,
        attention_qkv,
        attention_out,
        second_gain,
        second_gate_up,
        second_down,
    )
    stream = activations.astype(jnp.float32)
    front_whole = fetch_front(front_shards)
    first_stream, mamba_kept = mamba_forward(stream, row_lengths, carried_state, front_whole[:10])
    second_stream, first_kept = ffn_forward(first_stream, front_whole[10:])
    rear_whole = fetch_rear(rear_shards)
    third_stream, segment_kv, attention_kept = attention_forward(
        second_stream, row_lengths, carried_kv, rear_whole[:3]
    )
    fourth_stream, second_kept = ffn_forward(third_stream, rear_whole[3:])
    grad = cotangent.astype(jnp.float32)
    rear_back = fetch_rear(rear_shards)
    grad, second_grads = ffn_backward(third_stream, grad, rear_back[3:], second_kept)
    grad, attention_grads, grad_cache = attention_backward(
        second_stream, grad, row_lengths, rear_back[:3], attention_kept
    )
    rear_grads = settle_rear(attention_grads + second_grads)
    front_back = fetch_front(front_shards)
    grad, first_grads = ffn_backward(first_stream, grad, front_back[10:], first_kept)
    grad, mamba_grads, grad_state, new_state = mamba_backward(
        stream, grad, front_back[:10], mamba_kept
    )
    front_grads = settle_front(mamba_grads + first_grads)
    return (
        fourth_stream.astype(jnp.bfloat16),
        new_state,
        segment_kv,
        grad,
        grad_state,
        grad_cache,
        front_grads[0],
        front_grads[1],
        front_grads[2],
        front_grads[3],
        front_grads[4],
        front_grads[5],
        front_grads[6],
        front_grads[7],
        front_grads[8],
        front_grads[9],
        front_grads[10],
        front_grads[11],
        front_grads[12],
        rear_grads[0],
        rear_grads[1],
        rear_grads[2],
        rear_grads[3],
        rear_grads[4],
        rear_grads[5],
    )


EVERY = ("u", "c", "y", "x", "v")
PLANE = ("y", "x", "c")
SQUARES = ("u", "v")
BF = jnp.bfloat16
F32 = jnp.float32


def params(**more):
    return pltpu.CompilerParams(vmem_limit_bytes=32 * 2**20, **more)


def bit_route(move):
    route = []
    for place in range(2 ** len(EVERY)):
        bits = [place >> (len(EVERY) - 1 - k) & 1 for k in range(len(EVERY))]
        goal = 0
        for bit in move(*bits):
            goal = 2 * goal + bit
        if goal != place:
            route.append((place, goal))
    return route


def swap_planes(block):
    away = lax.axis_index("c") != lax.axis_index("v")
    route = bit_route(lambda u, c, y, x, v: (u, v, y, x, c))
    return jnp.where(away, lax.ppermute(block, EVERY, route), block)


def other(block, axis):
    return lax.ppermute(block, axis, [(0, 1), (1, 0)])


def gather_line(block):
    from_y = other(block, "y")
    return jnp.stack([block, other(block, "x"), from_y, other(from_y, "x")])


def gather_plane(block):
    own = gather_line(block)
    return jnp.concatenate([own, other(own, "c")], axis=0)


def scatter_line(mine, kind):
    to_y = (mine[2] + other(mine[3].astype(kind), "x").astype(F32)).astype(kind)
    from_x = other(mine[1].astype(kind), "x").astype(F32)
    return mine[0] + from_x + other(to_y, "y").astype(F32)


def scatter_plane(parts):
    half = parts.shape[0] // 2
    mine = parts[:half].astype(F32) + other(parts[half:], "c").astype(F32)
    return scatter_line(mine, parts.dtype)


def sum_plane(parts):
    return gather_plane(scatter_plane(parts))


def trade(block, axes):
    return lax.all_to_all(block, axes, 0, 0, tiled=True)


def gather_small(block, axes):
    for axis in reversed(axes):
        block = in_order(block, other(block, axis), axis)
    return block


def total_small(block):
    block = block + other(block, "c")
    for axes in (("y", "x"), ("u", "v")):
        turned = [
            lax.ppermute(block, axes, [(k, k ^ turn) for k in range(4)]) for turn in (1, 2, 3)
        ]
        block = block + sum(turned)
    return block


def pair_sum(parts, axis):
    here = lax.axis_index(axis)
    theirs = other(lax.dynamic_index_in_dim(parts, 1 - here, 0, False), axis)
    mine = lax.dynamic_index_in_dim(parts, here, 0, False)
    return mine.astype(F32) + theirs.astype(F32)


def reduce_squares(parts):
    return lax.psum_scatter(parts, SQUARES, scatter_dimension=0)


def gather_squares(block):
    return lax.all_gather(block, SQUARES, axis=0)


def settle(stage, *pieces):
    return lax.optimization_barrier((stage,) + pieces)


def tie(value, *stages):
    return lax.optimization_barrier((value,) + stages)[0]


def in_order(mine, theirs, axis):
    first = lax.axis_index(axis) == 0
    return jnp.stack([jnp.where(first, mine, theirs), jnp.where(first, theirs, mine)])


def kv_owners(parts):
    for axis in PLANE:
        lead = parts.ndim - {"y": 6, "x": 5, "c": 4}[axis]
        stay = lax.index_in_dim(parts, 0, lead, False)
        leave = lax.index_in_dim(parts, 1, lead, False)
        parts = in_order(stay, other(leave, axis), axis)
    side, y_size, c_size, two, count, width = parts.shape
    return parts.transpose(0, 4, 3, 2, 1, 5).reshape(side, count, two * y_size * c_size * width)


def rows_gather(block):
    here = lax.axis_index("c")
    mine = lax.dynamic_index_in_dim(block, here, 0, False)
    theirs = lax.dynamic_index_in_dim(block, 1 - here, 0, False)
    return gather_line(jnp.stack([mine, other(theirs, "c")]))


def rows_scatter(parts):
    parts = parts.reshape((4, 2) + parts.shape[1:])
    pair = scatter_line(parts.astype(F32), parts.dtype)
    return in_order(pair[0], other(pair[1].astype(parts.dtype), "c").astype(F32), "c")


def rows_of(gathered):
    squares, members, rows, width = gathered.shape
    split = gathered.reshape(2, 2, members // 2, 2, rows, width)
    return split.transpose(0, 3, 2, 1, 4, 5).reshape(squares * members * rows, width)


def by_square(grad):
    total, width = grad.shape
    split = grad.reshape(2, 2, 4, 2, total // 32, width).transpose(0, 3, 2, 1, 4, 5)
    return split.reshape(4, 8, total // 32, width)


def relocate(block, back):
    route = bit_route(lambda u, c, y, x, v: (x, y, u, c, v))
    moving = jnp.zeros((2 ** len(EVERY),), bool).at[jnp.array([place for place, goal in route])].set(True)
    here = lax.axis_index(EVERY)
    moved = lax.ppermute(block, EVERY, [(goal, place) for place, goal in route] if back else route)
    return jnp.where(moving[here], moved, block)


def dot(left, right, left_dim, right_dim):
    return lax.dot_general(
        left, right, (((left_dim,), (right_dim,)), ((), ())), preferred_element_type=F32
    )


def conv_body(order, inner_ref, taps_ref, bias_ref, total_ref, mixed_ref, low_ref, held):
    step = pl.program_id(0)
    rows, group = inner_ref.shape[1], inner_ref.shape[2]

    @pl.when(step == 0)
    def clear():
        held[:, :8] = jnp.zeros_like(held[:, :8])

    @pl.when(step > 0)
    def keep():
        held[:, :8] = held[:, group:]

    for row in range(rows):
        held[row, 8:] = inner_ref[0, row]
        total = bias_ref[...] + taps_ref[0:1] * held[row, 5 : 5 + group]
        for tap in range(1, CONV):
            total = total + taps_ref[tap : tap + 1] * held[row, 5 + tap : 5 + tap + group]
        mixed = total / (1.0 + jnp.exp(-total))
        total_ref[0, row] = total
        mixed_ref[0, row] = mixed
        low_ref[0, row] = mixed.astype(BF)


def conv_forward(order, projected, taps, bias):
    blocks, rows, group, width = projected.shape
    spec = pl.BlockSpec((1, rows, group, width), lambda i, order: (order[i], 0, 0, 0))
    shape = (blocks, rows, group, width)
    return pl.pallas_call(
        conv_body,
        grid_spec=pltpu.PrefetchScalarGridSpec(
            num_scalar_prefetch=1,
            grid=(blocks,),
            in_specs=[
                spec,
                pl.BlockSpec((CONV, width), lambda i, order: (0, 0)),
                pl.BlockSpec((1, width), lambda i, order: (0, 0)),
            ],
            out_specs=[spec, spec, spec],
            scratch_shapes=[pltpu.VMEM((rows, group + 8, width), F32)],
        ),
        out_shape=[
            jax.ShapeDtypeStruct(shape, F32),
            jax.ShapeDtypeStruct(shape, F32),
            jax.ShapeDtypeStruct(shape, BF),
        ],
        compiler_params=params(),
        name="conv_forward",
    )(order, projected, taps, bias)


def conv_back_body(order, grad_ref, total_ref, inner_ref, taps_ref, out_ref, sums_ref, held):
    step = pl.program_id(0)
    rows, group = inner_ref.shape[1], inner_ref.shape[2]

    @pl.when(step == 0)
    def clear():
        held[:, group:] = jnp.zeros_like(held[:, group:])
        sums_ref[...] = jnp.zeros_like(sums_ref)

    @pl.when(step > 0)
    def keep():
        held[:, group:] = held[:, :8]

    for row in range(rows):
        total = total_ref[0, row]
        sig = 1.0 / (1.0 + jnp.exp(-total))
        grad = grad_ref[0, row] * (sig * (1.0 + total * (1.0 - sig)))
        held[row, :group] = grad
        inner = inner_ref[0, row]
        back = None
        for tap in range(CONV):
            later = held[row, CONV - 1 - tap : CONV - 1 - tap + group]
            part = taps_ref[tap : tap + 1] * later
            back = part if back is None else back + part
            sums_ref[tap : tap + 1] += jnp.sum(inner * later, axis=0, keepdims=True)
        sums_ref[CONV : CONV + 1] += jnp.sum(grad, axis=0, keepdims=True)
        out_ref[0, row] = back.astype(BF)


def conv_back(order, grad, total, projected, taps):
    blocks, rows, group, width = grad.shape
    spec = pl.BlockSpec(
        (1, rows, group, width), lambda i, order: (order[blocks - 1 - i], 0, 0, 0)
    )
    return pl.pallas_call(
        conv_back_body,
        grid_spec=pltpu.PrefetchScalarGridSpec(
            num_scalar_prefetch=1,
            grid=(blocks,),
            in_specs=[spec, spec, spec, pl.BlockSpec((CONV, width), lambda i, order: (0, 0))],
            out_specs=[spec, pl.BlockSpec((8, width), lambda i, order: (0, 0))],
            scratch_shapes=[pltpu.VMEM((rows, group + 8, width), F32)],
        ),
        out_shape=[
            jax.ShapeDtypeStruct(grad.shape, BF),
            jax.ShapeDtypeStruct((8, width), F32),
        ],
        compiler_params=params(),
        name="conv_back",
    )(order, grad, total, projected, taps)


def widen(tile, width):
    return jnp.concatenate([tile] * (width // 128), axis=1)


def narrow(tile):
    total = tile[:, :128]
    for start in range(128, tile.shape[1], 128):
        total = total + tile[:, start : start + 128]
    return total


def scan_body(
    order, mixed_ref, step_ref, b_ref, c_ref, decay_ref, start_ref, core_ref, past_ref, end_ref, held
):
    @pl.when(pl.program_id(0) == 0)
    def begin():
        held[...] = start_ref[...]

    decay = decay_ref[...]
    rows, group, width = mixed_ref.shape[1:]

    def eight(turn, states):
        base = pl.multiple_of(turn * 8, 8)
        states = list(states)
        steps = [step_ref[0, row, pl.ds(base, 8), :] for row in range(rows)]
        drives = [steps[row] * mixed_ref[0, row, pl.ds(base, 8), :] for row in range(rows)]
        cores = [[] for row in range(rows)]
        for k in range(8):
            for row in range(rows):
                past_ref[0, row, base + k] = states[row]
                fade = jnp.exp(steps[row][k : k + 1] * decay)
                state = fade * states[row] + drives[row][k : k + 1] * widen(
                    b_ref[0, row, base + k], width
                )
                states[row] = state
                seen = widen(c_ref[0, row, base + k], width) * state
                cores[row].append(jnp.sum(seen, axis=0, keepdims=True))
        for row in range(rows):
            core_ref[0, row, pl.ds(base, 8), :] = jnp.concatenate(cores[row], axis=0)
        return tuple(states)

    states = lax.fori_loop(0, group // 8, eight, tuple(held[row] for row in range(rows)))
    for row in range(rows):
        held[row] = states[row]
        end_ref[row] = states[row]


def scan_forward(order, mixed, step, wide_b, wide_c, decay, start):
    blocks, rows, group, width = mixed.shape
    states = decay.shape[0]
    spec = pl.BlockSpec((1, rows, group, width), lambda i, order: (order[i], 0, 0, 0))
    maps = pl.BlockSpec((1, rows, group, states, 128), lambda i, order: (order[i], 0, 0, 0, 0))
    whole = pl.BlockSpec((rows, states, width), lambda i, order: (0, 0, 0))
    return pl.pallas_call(
        scan_body,
        grid_spec=pltpu.PrefetchScalarGridSpec(
            num_scalar_prefetch=1,
            grid=(blocks,),
            in_specs=[
                spec,
                spec,
                maps,
                maps,
                pl.BlockSpec((states, width), lambda i, order: (0, 0)),
                whole,
            ],
            out_specs=[
                spec,
                pl.BlockSpec(
                    (1, rows, group, states, width), lambda i, order: (order[i], 0, 0, 0, 0)
                ),
                whole,
            ],
            scratch_shapes=[pltpu.VMEM((rows, states, width), F32)],
        ),
        out_shape=[
            jax.ShapeDtypeStruct(mixed.shape, F32),
            jax.ShapeDtypeStruct((blocks, rows, group, states, width), F32),
            jax.ShapeDtypeStruct(start.shape, F32),
        ],
        compiler_params=params(),
        name="scan_forward",
    )(order, mixed, step, wide_b, wide_c, decay, start)


def scan_back_body(
    order,
    mixed_ref,
    step_ref,
    b_ref,
    c_ref,
    grad_ref,
    past_ref,
    decay_ref,
    end_ref,
    dmixed_ref,
    dstep_ref,
    db_ref,
    dc_ref,
    ddecay_ref,
    dstart_ref,
    held,
    after,
):
    @pl.when(pl.program_id(0) == 0)
    def begin():
        held[...] = jnp.zeros_like(held)
        after[...] = end_ref[...]
        ddecay_ref[...] = jnp.zeros_like(ddecay_ref)

    decay = decay_ref[...]
    rows, group, width = mixed_ref.shape[1:]
    turns = group // 8

    def eight(turn, carry):
        base = pl.multiple_of((turns - 1 - turn) * 8, 8)
        backs, states, sums = list(carry[0]), list(carry[1]), carry[2]
        steps = [step_ref[0, row, pl.ds(base, 8), :] for row in range(rows)]
        inputs = [mixed_ref[0, row, pl.ds(base, 8), :] for row in range(rows)]
        grads = [grad_ref[0, row, pl.ds(base, 8), :] for row in range(rows)]
        drives = [steps[row] * inputs[row] for row in range(rows)]
        firsts = [[None] * 8 for row in range(rows)]
        seconds = [[None] * 8 for row in range(rows)]
        for k in reversed(range(8)):
            for row in range(rows):
                now = steps[row][k : k + 1]
                grad = grads[row][k : k + 1]
                past = past_ref[0, row, base + k]
                fade = jnp.exp(now * decay)
                back = widen(c_ref[0, row, base + k], width) * grad + backs[row]
                dc_ref[0, row, base + k] = narrow(states[row] * grad).astype(BF)
                firsts[row][k] = jnp.sum(
                    widen(b_ref[0, row, base + k], width) * back, axis=0, keepdims=True
                )
                db_ref[0, row, base + k] = narrow(back * drives[row][k : k + 1]).astype(BF)
                faded = fade * back
                flow = faded * past
                seconds[row][k] = jnp.sum(flow * decay, axis=0, keepdims=True)
                sums = sums + flow * now
                backs[row] = faded
                states[row] = past
        for row in range(rows):
            first = jnp.concatenate(firsts[row], axis=0)
            second = jnp.concatenate(seconds[row], axis=0)
            dmixed_ref[0, row, pl.ds(base, 8), :] = steps[row] * first
            dstep_ref[0, row, pl.ds(base, 8), :] = inputs[row] * first + second
        return (tuple(backs), tuple(states), sums)

    backs, states, sums = lax.fori_loop(
        0,
        turns,
        eight,
        (
            tuple(held[row] for row in range(rows)),
            tuple(after[row] for row in range(rows)),
            ddecay_ref[...],
        ),
    )
    ddecay_ref[...] = sums
    for row in range(rows):
        held[row] = backs[row]
        after[row] = states[row]
        dstart_ref[row] = backs[row]


def scan_back(order, mixed, step, wide_b, wide_c, grad, past, decay, end):
    blocks, rows, group, width = mixed.shape
    states = decay.shape[0]
    last = blocks - 1
    spec = pl.BlockSpec((1, rows, group, width), lambda i, order: (order[last - i], 0, 0, 0))
    maps = pl.BlockSpec(
        (1, rows, group, states, 128), lambda i, order: (order[last - i], 0, 0, 0, 0)
    )
    kept = pl.BlockSpec(
        (1, rows, group, states, width), lambda i, order: (order[last - i], 0, 0, 0, 0)
    )
    whole = pl.BlockSpec((rows, states, width), lambda i, order: (0, 0, 0))
    rates = pl.BlockSpec((states, width), lambda i, order: (0, 0))
    return pl.pallas_call(
        scan_back_body,
        grid_spec=pltpu.PrefetchScalarGridSpec(
            num_scalar_prefetch=1,
            grid=(blocks,),
            in_specs=[spec, spec, maps, maps, spec, kept, rates, whole],
            out_specs=[spec, spec, maps, maps, rates, whole],
            scratch_shapes=[
                pltpu.VMEM((rows, states, width), F32),
                pltpu.VMEM((rows, states, width), F32),
            ],
        ),
        out_shape=[
            jax.ShapeDtypeStruct(mixed.shape, F32),
            jax.ShapeDtypeStruct(mixed.shape, F32),
            jax.ShapeDtypeStruct((blocks, rows, group, states, 128), BF),
            jax.ShapeDtypeStruct((blocks, rows, group, states, 128), BF),
            jax.ShapeDtypeStruct(decay.shape, F32),
            jax.ShapeDtypeStruct(end.shape, F32),
        ],
        compiler_params=params(),
        name="scan_back",
    )(order, mixed, step, wide_b, wide_c, grad, past, decay, end)


def own_positions(shape, axis, first, member, group):
    index = first + lax.broadcasted_iota(jnp.int32, shape, axis)
    slot = index // group
    block = slot ^ member
    return block * group + index % group


def seen_cache(query, place, shape, group):
    index = lax.broadcasted_iota(jnp.int32, shape, 1)
    return (index + place * group) > query


def seen_own(query, key, length):
    return (key <= query) & ((key < length) | (key == query))


def attend_body(meta_ref, q_ref, ck_ref, cv_ref, k_ref, v_ref, out_ref, log_ref):
    count = q_ref.shape[0]
    first = pl.program_id(1) * count
    scale = HEAD_DIM ** (-0.5)
    queries = q_ref[...]
    pieces = ck_ref.shape[0]
    size = ck_ref.shape[1]
    tokens = k_ref.shape[0]
    member = meta_ref[1]
    group = tokens // pieces
    query = own_positions((count, 1), 0, first, member, group)
    scores = []
    for piece in range(pieces):
        score = dot(queries, ck_ref[piece], 1, 1) * scale
        inside = seen_cache(query, piece, (1, size), size)
        scores.append(jnp.where(inside, score, NEGATIVE))
    score = dot(queries, k_ref[...], 1, 1) * scale
    key = own_positions((1, tokens), 1, 0, member, group)
    scores.append(jnp.where(seen_own(query, key, meta_ref[0]), score, NEGATIVE))
    top = jnp.max(scores[0], axis=1, keepdims=True)
    for score in scores[1:]:
        top = jnp.maximum(top, jnp.max(score, axis=1, keepdims=True))
    total = jnp.zeros_like(top)
    result = jnp.zeros((count, HEAD_DIM), F32)
    for piece, score in enumerate(scores):
        part = jnp.exp(score - top)
        total = total + jnp.sum(part, axis=1, keepdims=True)
        contents = cv_ref[piece] if piece < pieces else v_ref[...]
        result = result + dot(part.astype(BF), contents, 1, 0)
    out_ref[...] = result / total
    log_ref[0] = jnp.broadcast_to(top + jnp.log(total), (count, 128))


def attend(meta, qkv, cached_keys, cached_contents):
    tokens, width = qkv.shape
    width = width // 3
    heads = width // HEAD_DIM
    count = 256
    shards, group, unused = cached_keys.shape
    own = lambda base: pl.BlockSpec((tokens, HEAD_DIM), lambda h, i, meta: (0, base + h))
    held = pl.BlockSpec((shards, group, HEAD_DIM), lambda h, i, meta: (0, 0, h))
    block = pl.BlockSpec((count, HEAD_DIM), lambda h, i, meta: (i, h))
    return pl.pallas_call(
        attend_body,
        grid_spec=pltpu.PrefetchScalarGridSpec(
            num_scalar_prefetch=1,
            grid=(heads, tokens // count),
            in_specs=[block, held, held, own(heads), own(2 * heads)],
            out_specs=[block, pl.BlockSpec((1, count, 128), lambda h, i, meta: (h, i, 0))],
        ),
        out_shape=[
            jax.ShapeDtypeStruct((tokens, width), F32),
            jax.ShapeDtypeStruct((heads, tokens, 128), F32),
        ],
        compiler_params=params(),
        name="attend",
    )(meta, qkv, cached_keys, cached_contents, qkv, qkv)


def attend_back_body(
    meta_ref,
    q_ref,
    grad_ref,
    out_ref,
    log_ref,
    ck_ref,
    cv_ref,
    k_ref,
    v_ref,
    dck_ref,
    dcv_ref,
    dq_ref,
    dk_ref,
    dv_ref,
    total,
    delta,
):
    piece = pl.program_id(1)
    pieces = pl.num_programs(1) - 1
    scale = HEAD_DIM ** (-0.5)
    queries = q_ref[...]
    grad = grad_ref[...]
    count = queries.shape[0]
    size = ck_ref.shape[1]
    member = meta_ref[1]
    group = count // (2 * pieces)
    query = own_positions((count, 1), 0, 0, member, group)

    @pl.when(piece == 0)
    def begin():
        total[...] = jnp.zeros_like(total)
        mine = jnp.sum(grad.astype(F32) * out_ref[...], axis=1, keepdims=True)
        delta[...] = jnp.broadcast_to(mine, delta.shape)

    def work(keys, contents, inside):
        score = dot(queries, keys, 1, 1) * scale
        part = jnp.exp(score - log_ref[0][:, :1])
        if inside is not None:
            part = jnp.where(inside, part, 0.0)
        dcontents = dot(part.astype(BF), grad, 0, 0)
        slope = dot(grad, contents, 1, 1)
        dscore = (part * (slope - delta[:, :1])).astype(BF)
        total[...] += dot(dscore, keys, 1, 0) * scale
        return dot(dscore, queries, 0, 0) * scale, dcontents

    def cached(inside):
        keys = ck_ref[...].reshape(2 * size, HEAD_DIM)
        contents = cv_ref[...].reshape(2 * size, HEAD_DIM)
        dkeys, dcontents = work(keys, contents, inside)
        dck_ref[...] = dkeys.astype(BF).reshape(2, size, HEAD_DIM)
        dcv_ref[...] = dcontents.astype(BF).reshape(2, size, HEAD_DIM)

    edge = piece * 2 * size < count

    @pl.when((piece < pieces) & edge)
    def near():
        cached(seen_cache(query, 2 * piece, (1, 2 * size), size))

    @pl.when((piece < pieces) & jnp.logical_not(edge))
    def far():
        cached(None)

    @pl.when(piece == pieces)
    def own():
        key = own_positions((1, count), 1, 0, member, group)
        dkeys, dcontents = work(k_ref[...], v_ref[...], seen_own(query, key, meta_ref[0]))
        dk_ref[...] = dkeys.astype(BF)
        dv_ref[...] = dcontents.astype(BF)
        dq_ref[...] = total[...].astype(BF)


def attend_back(meta, qkv, grad, out, log, cached_keys, cached_contents):
    tokens, width = grad.shape
    heads = width // HEAD_DIM
    shards, group, unused = cached_keys.shape
    pieces = shards // 2
    own = lambda base: pl.BlockSpec((tokens, HEAD_DIM), lambda h, i, meta: (0, base + h))
    place = lambda i: jnp.minimum(i, pieces - 1)
    held = pl.BlockSpec((2, group, HEAD_DIM), lambda h, i, meta: (place(i), 0, h))
    result = jax.ShapeDtypeStruct((tokens, width), BF)
    return pl.pallas_call(
        attend_back_body,
        grid_spec=pltpu.PrefetchScalarGridSpec(
            num_scalar_prefetch=1,
            grid=(heads, pieces + 1),
            in_specs=[
                own(0),
                own(0),
                own(0),
                pl.BlockSpec((1, tokens, 128), lambda h, i, meta: (h, 0, 0)),
                held,
                held,
                own(heads),
                own(2 * heads),
            ],
            out_specs=[
                held,
                held,
                own(0),
                own(0),
                own(0),
            ],
            scratch_shapes=[
                pltpu.VMEM((tokens, HEAD_DIM), F32),
                pltpu.VMEM((tokens, 128), F32),
            ],
        ),
        out_shape=[jax.ShapeDtypeStruct(cached_keys.shape, BF)] * 2 + [result, result, result],
        compiler_params=params(),
        name="attend_back",
    )(meta, qkv, grad, out, log, cached_keys, cached_contents, qkv, qkv)


def assemble(gots, moves, shape):
    def body(*refs):
        out_ref = refs[-1]
        for (row, column), height, (which, member, left, width) in moves:
            part = refs[which][member, :, left : left + width].astype(F32)
            out_ref[row : row + height, column : column + width] = part

    return pl.pallas_call(
        body,
        out_shape=jax.ShapeDtypeStruct(shape, F32),
        compiler_params=params(),
        name="assemble",
    )(*gots)


def silu_slope(values):
    sig = jax.nn.sigmoid(values)
    return sig * (1.0 + values * (1.0 - sig))


def norm_back(values, gain, grad):
    back = jax.vjp(rms_gain, values, gain)[1](grad)
    return back


def ffn_gate(normed, gate_up):
    both = dot(normed, gate_up, 1, 0)
    width = both.shape[1] // 2
    return both, (jax.nn.silu(both[:, :width]) * both[:, width:]).astype(BF)


def ffn_gate_back(grad_hidden, both):
    width = both.shape[1] // 2
    gate, up = both[:, :width], both[:, width:]
    return jnp.concatenate(
        [grad_hidden * up * silu_slope(gate), grad_hidden * jax.nn.silu(gate)], axis=1
    ).astype(BF)


def plane_local(
    activations,
    cotangent,
    carried_state,
    carried_kv,
    row_lengths,
    mamba_gain,
    mamba_in,
    conv_weight,
    conv_bias,
    selection,
    step_proj,
    step_bias,
    decay_log,
    skip_gain,
    mamba_out,
    first_gain,
    first_gate_up,
    first_down,
    attention_gain,
    attention_qkv,
    attention_out,
    second_gain,
    second_gate_up,
    second_down,
):
    rows, group, wide = activations.shape
    planes, inner = lax.axis_size(SQUARES), lax.axis_size("c")
    members = planes * inner
    u, c, y, x, v = (lax.axis_index(name) for name in EVERY)
    member = (y * 2 + x) * inner + c
    place = (y * 2 + x) * inner + v
    offset = jnp.arange(members) ^ member
    order = (((offset & 1) << 2) | (offset >> 1)).astype(jnp.int32)
    shard = mamba_gain.shape[0]
    channels = skip_gain.shape[0]
    width = channels * planes
    rank = step_proj.shape[0]
    states = decay_log.shape[0]
    units = first_down.shape[0]
    head_width = wide // planes
    cache_rows = carried_kv.shape[1]

    def parts_of(product_of):
        return product_of.astype(BF).reshape(members, rows, group, wide)

    gains = jnp.stack([mamba_gain, first_gain, attention_gain, second_gain], axis=1)
    gains = jnp.pad(gains, ((0, 0), (0, 124)))
    payload = mamba_in.reshape(shard, 2, members, width).transpose(2, 0, 1, 3)
    spread = jnp.broadcast_to(gains[None], (members,) + gains.shape)
    payload = payload.reshape(members, shard, 2 * width)
    payload = jnp.concatenate([payload[:, :, :width], spread, payload[:, :, width:]], axis=2)
    dealt = trade(payload, PLANE)
    tokens = swap_planes(tie(activations, payload))
    stream = tokens.astype(F32)
    own_inner = rows_of(gather_squares(dealt[:, :, : width + 128]))
    gains = own_inner[:, width : width + 4].T.astype(F32)
    own_inner = own_inner[:, :width]
    normed = gather_plane(tie(tokens, dealt)).reshape(-1, wide).astype(F32)
    normed = rms_gain(normed, gains[0]).astype(BF)


    cuts = (selection.shape[1], rank, CONV, 1, 1, states, 1)
    packed = jnp.concatenate(
        [
            selection.astype(F32),
            step_proj.astype(F32).T,
            conv_weight.astype(F32).T,
            conv_bias.astype(F32)[:, None],
            step_bias[:, None],
            decay_log.T,
            skip_gain[:, None],
        ],
        axis=1,
    )
    packed = jnp.pad(packed, ((0, 0), (0, -packed.shape[1] % 128)))
    packed = gather_small(relocate(tie(packed, tokens), False), SQUARES).reshape(width, -1)
    starts = [sum(cuts[:index]) for index in range(len(cuts) + 1)]
    pieces = [packed[:, starts[index] : starts[index + 1]] for index in range(len(cuts))]
    own_selection = pieces[0].astype(BF)
    own_step_proj = pieces[1].astype(BF)
    taps = pieces[2].T
    tap_bias = pieces[3].T
    own_step_bias = pieces[4].T
    decay = -jnp.exp(pieces[5].T)
    skip = pieces[6].T
    moved = jnp.concatenate([mamba_out, attention_out], axis=0)
    moved = relocate(tie(moved, packed), False)
    own_out = gather_squares(moved[:channels]).reshape(width, wide)
    start = lax.dynamic_slice_in_dim(carried_state, place * width, width, 2)
    marks = jnp.broadcast_to(row_lengths.astype(F32)[:, None, None], (rows, 8, width))
    start = swap_planes(tie(jnp.concatenate([start, marks], axis=1), packed))
    lengths = start[:, states, 0].astype(jnp.int32)
    start = start[:, :states]
    own_gate = rows_of(gather_squares(tie(dealt[:, :, width + 128 :], normed)))

    def hidden_columns(gate_up):
        split = gate_up.reshape(shard, 2, 2, 2, 2, 2, 2, units)
        return split.transpose(4, 5, 3, 0, 1, 2, 6, 7).reshape(members, shard, -1)

    split = attention_qkv.reshape(shard, 3, planes, head_width).transpose(2, 0, 1, 3)
    split = jnp.broadcast_to(
        split.reshape(planes, 1, shard, 3 * head_width), (planes, inner, shard, 3 * head_width)
    )
    split = split.reshape(members, shard, 3 * head_width)
    dealt_first = trade(tie(hidden_columns(first_gate_up), normed), PLANE)
    own_first_down = gather_squares(first_down).reshape(-1, wide)

    def heads_of(block):
        return jnp.stack(
            [
                block[r, :, g * head_width : (g + 1) * head_width]
                for g in range(planes)
                for r in range(rows)
            ]
        )

    late_keys = swap_planes(tie(carried_kv[:, :, :wide], tokens))
    cached_keys = trade(tie(heads_of(late_keys), normed), PLANE)
    late = jnp.concatenate([carried_kv[:, :, wide:], cotangent.reshape(rows, -1, wide)], axis=1)
    late = swap_planes(tie(late, normed))

    inner_part = dot(normed, own_inner, 1, 0).reshape(members, rows, group, width)
    total, mixed, mixed_low = conv_forward(order, inner_part, taps, tap_bias)
    flat_low = mixed_low.reshape(-1, width)
    select = sum_plane(dot(flat_low, own_selection, 1, 0).reshape(members, rows, group, -1))
    gate = dot(normed, own_gate, 1, 0).reshape(members, rows, group, width)
    select, dealt_first, cached_keys, late = settle(select, dealt_first, cached_keys, late)
    step_low = select[..., :rank].astype(BF).reshape(-1, rank)
    pre = dot(step_low, own_step_proj, 1, 1).reshape(members, rows, group, width) + own_step_bias
    blocks = jnp.zeros((members,), jnp.int32).at[order].set(jnp.arange(members, dtype=jnp.int32))
    positions = blocks[:, None] * group + jnp.arange(group)[None, :]
    valid = (positions[:, None, :] < lengths[None, :, None]).astype(F32)[..., None]
    step = jax.nn.softplus(pre) * valid
    cached_contents = trade(tie(heads_of(late[:, :cache_rows]), step), PLANE)
    wide_shape = (members, rows, group, states, 128)
    wide_b = jnp.broadcast_to(select[..., rank : rank + states, None], wide_shape)
    wide_c = jnp.broadcast_to(select[..., rank + states :, None], wide_shape)
    core, past, end = scan_forward(order, mixed, step, wide_b, wide_c, decay, start)
    core, cached_contents = settle(core, cached_contents)
    own_first = rows_of(gather_squares(dealt_first))
    dealt_qkv = trade(tie(split, core), PLANE)
    rear = gather_squares(jnp.concatenate([moved[channels:], second_down], axis=0))
    mixed_out = core + skip * mixed
    gated = (mixed_out * jax.nn.silu(gate)).astype(BF).reshape(-1, width)
    first_stream = stream + scatter_plane(parts_of(dot(gated, own_out, 1, 0)))
    first_stream, dealt_qkv = settle(first_stream, dealt_qkv)
    own_qkv = rows_of(gather_squares(dealt_qkv))

    first_normed = gather_plane(rms_gain(first_stream, gains[1]).astype(BF)).reshape(-1, wide)
    dealt_second = trade(tie(hidden_columns(second_gate_up), first_normed), PLANE)
    first_both, first_hidden = ffn_gate(first_normed, own_first)
    second_stream = first_stream + scatter_plane(parts_of(dot(first_hidden, own_first_down, 1, 0)))

    second_stream, dealt_second = settle(second_stream, dealt_second)
    own_second = rows_of(gather_squares(dealt_second))

    def rows_parts(product_of):
        return product_of.astype(BF).reshape(members, group, wide)

    grad = late[:, cache_rows:].reshape(rows, group, wide)
    own_attention_out = rear[:, :shard]
    own_attention_out = in_order(own_attention_out, other(own_attention_out, "c"), "c")
    own_attention_out = own_attention_out.reshape(-1, wide)
    own_second_down = rear[:, shard:].reshape(-1, wide)
    length = jnp.concatenate([lax.dynamic_slice_in_dim(lengths, c, 1), member[None]])
    normed_rows = rows_gather(rms_gain(second_stream, gains[2]).astype(BF)).reshape(-1, wide)
    qkv = dot(normed_rows, own_qkv, 1, 0).astype(BF)
    grad_whole = gather_plane(tie(grad, qkv)).reshape(-1, wide)
    grad = grad.astype(F32)
    attended, log = attend(length, qkv, cached_keys, cached_contents)
    attended_low = attended.astype(BF)
    third_stream = second_stream + rows_scatter(rows_parts(dot(attended_low, own_attention_out, 1, 0)))
    own_kv = qkv[:, head_width:].reshape(members, group, 2, head_width).transpose(0, 2, 1, 3)
    own_kv = tie(own_kv, third_stream).reshape(2, 2, inner, 2, group, head_width)

    second_normed = gather_plane(rms_gain(third_stream, gains[3]).astype(BF)).reshape(-1, wide)
    second_both, second_hidden = ffn_gate(second_normed, own_second)
    second_parts = parts_of(dot(second_hidden, own_second_down, 1, 0))
    fourth_stream = third_stream + scatter_plane(second_parts)
    def hidden_back(got):
        moves = []
        for column in range(2 * planes * members):
            part, uu, cc, yx, vv = column >> 5, column >> 4 & 1, column >> 3 & 1, column >> 1 & 3, column & 1
            source = (0, yx * 2 + cc, ((part * 2 + uu) * 2 + vv) * units, units)
            moves.append(((0, column * units), shard, source))
        return assemble([got], moves, (shard, 2 * planes * members * units))

    def cache_back(part):
        part = part.reshape(planes, rows, cache_rows, head_width)
        return swap_planes(jnp.concatenate([part[g] for g in range(planes)], axis=2))

    grad_both = ffn_gate_back(dot(grad_whole, own_second_down, 1, 1), second_both)
    grad_normed = scatter_plane(parts_of(dot(grad_both, own_second, 1, 1)))
    second_columns = reduce_squares(by_square(dot(second_normed, grad_both, 0, 0).astype(BF)))
    second_rows = dot(second_hidden, grad_whole, 0, 0).astype(BF)
    grad_stream, second_gain_grad = norm_back(third_stream, gains[3], grad_normed)
    grad = grad + grad_stream

    grad_rows = rows_gather(grad.astype(BF)).reshape(-1, wide)
    grad_attended = dot(grad_rows, own_attention_out, 1, 1).astype(BF)
    own_kv = kv_owners(tie(own_kv, grad_attended))
    returned = swap_planes(jnp.concatenate([fourth_stream.astype(BF), own_kv], axis=2))
    output, segment_kv = returned[..., :wide], returned[..., wide:]
    back_keys, back_contents, dq, dk, dv = attend_back(
        length, qkv, grad_attended, attended, log, cached_keys, cached_contents
    )
    grad_qkv = jnp.concatenate([dq, dk, dv], axis=1)
    grad_normed = rows_scatter(rows_parts(dot(grad_qkv, own_qkv, 1, 1)))
    grad_stream, attention_gain_grad = norm_back(second_stream, gains[2], grad_normed)
    grad = grad + grad_stream
    grad, second_columns = settle(grad, second_columns)

    grad_out = dot(attended_low, grad_rows, 0, 0).astype(BF).reshape(inner, planes, shard, wide)
    grad_out = pair_sum(grad_out, "c").astype(BF)
    attention_out_grad = reduce_squares(grad_out)
    second_down_grad = reduce_squares(second_rows.reshape(planes, units, wide)).astype(F32)
    qkv_columns = reduce_squares(by_square(dot(normed_rows, grad_qkv, 0, 0).astype(BF)))

    grad_whole = gather_plane(grad.astype(BF)).reshape(-1, wide)
    grad_whole, second_down_grad = settle(grad_whole, second_down_grad)
    back_keys = trade(tie(back_keys, grad_whole), PLANE)
    grad_both = ffn_gate_back(dot(grad_whole, own_first_down, 1, 1), first_both)
    grad_normed = scatter_plane(parts_of(dot(grad_both, own_first, 1, 1)))
    first_columns = reduce_squares(by_square(dot(first_normed, grad_both, 0, 0).astype(BF)))
    first_rows = dot(first_hidden, grad_whole, 0, 0).astype(BF)
    grad_stream, first_gain_grad = norm_back(first_stream, gains[1], grad_normed)
    grad = grad + grad_stream
    grad, qkv_columns, attention_out_grad = settle(grad, qkv_columns, attention_out_grad)
    first_down_grad = reduce_squares(first_rows.reshape(planes, units, wide)).astype(F32)

    grad_whole = gather_plane(grad.astype(BF)).reshape(-1, wide)
    grad_whole, back_keys = settle(grad_whole, back_keys)
    back_keys = cache_back(back_keys)
    grad_gated = dot(grad_whole, own_out, 1, 1).reshape(mixed.shape)
    grad_core = grad_gated * jax.nn.silu(gate)
    back_contents = trade(tie(back_contents, grad_core), PLANE)
    grad_gate = (grad_gated * mixed_out * silu_slope(gate)).astype(BF).reshape(-1, width)
    skip_grad = jnp.sum(grad_core * mixed, axis=(0, 1, 2))
    grad_mixed, grad_step, grad_b, grad_c, grad_decay, grad_start = scan_back(
        order, mixed, step, wide_b, wide_c, grad_core, past, decay, end
    )
    new_state, grad_state = swap_planes(jnp.stack([end, grad_start]))
    grad_out = dot(gated, grad_whole, 0, 0).astype(BF).reshape(planes, channels, wide)
    out_rows = reduce_squares(grad_out)
    gate_columns = reduce_squares(by_square(dot(normed, grad_gate, 0, 0).astype(BF)))
    grad_step, back_contents, first_columns, first_down_grad = settle(
        grad_step, back_contents, first_columns, first_down_grad
    )
    back_contents = cache_back(back_contents)
    second_gate_up_grad = hidden_back(trade(tie(second_columns, grad_step), PLANE))
    got = trade(tie(qkv_columns, grad_step), PLANE)
    grad_pre = grad_step * valid * jax.nn.sigmoid(pre)
    step_bias_grad = jnp.sum(grad_pre, axis=(0, 1, 2))
    grad_pre = grad_pre.astype(BF).reshape(-1, width)
    step_proj_grad = dot(grad_pre, step_low, 0, 0)
    grad_low = dot(grad_pre, own_step_proj, 1, 0).reshape(members, rows, group, rank)
    grad_select = sum_plane(jnp.concatenate(
            [grad_low] + [jnp.sum(part.astype(F32), axis=-1) for part in (grad_b, grad_c)], axis=-1
        ))
    grad_select = grad_select.astype(BF).reshape(-1, rank + 2 * states)
    grad_select, got, gate_columns, out_rows, back_keys = settle(
        grad_select, got, gate_columns, out_rows, back_keys
    )
    got = jnp.sum(got.reshape(planes, inner, shard, -1).astype(F32), axis=1)
    moves = []
    for owner in range(planes):
        for part in range(3):
            source = (0, owner, part * head_width, head_width)
            moves.append(((0, part * wide + owner * head_width), shard, source))
    attention_qkv_grad = assemble([got], moves, (shard, 3 * wide))
    selection_grad = dot(flat_low, grad_select, 0, 0)
    grad_mixed = (
        grad_mixed
        + grad_core * skip
        + dot(grad_select, own_selection, 1, 1).reshape(mixed.shape)
    )
    grad_inner, tap_sums = conv_back(order, grad_mixed, total, inner_part, taps)
    grad_inner = grad_inner.reshape(-1, width)
    first_got = trade(tie(first_columns, grad_inner), PLANE)
    first_gate_up_grad = hidden_back(first_got)
    inner_columns = by_square(dot(normed, grad_inner, 0, 0).astype(BF))
    grad_inner = tie(grad_inner, inner_columns)
    inner_columns = reduce_squares(inner_columns)
    parts = dot(grad_inner, own_inner, 1, 1) + dot(grad_gate, own_gate, 1, 1)
    gate_columns = trade(tie(gate_columns, grad_inner), PLANE)
    moved = relocate(jnp.concatenate([out_rows, attention_out_grad], axis=0), True).astype(F32)
    mamba_out_grad, attention_out_grad = moved[:channels], moved[channels:]
    grad_normed = scatter_plane(parts_of(parts))
    grad_normed, inner_columns = settle(grad_normed, inner_columns)
    inner_columns = trade(inner_columns, PLANE)
    grad_stream, mamba_gain_grad = norm_back(stream, gains[0], grad_normed)
    grad_input = swap_planes(grad + grad_stream)
    moves = []
    for which in range(2):
        for owner in range(members):
            column = (which * members + owner) * width
            moves.append(((0, column), shard, (which, owner, 0, width)))
    mamba_in_grad = assemble([inner_columns, gate_columns], moves, mamba_in.shape)
    packed = jnp.concatenate(
        [
            selection_grad,
            step_proj_grad,
            tap_sums[: CONV + 1].T,
            step_bias_grad[:, None],
            (grad_decay * decay).T,
            skip_grad[:, None],
        ],
        axis=1,
    )
    packed = jnp.pad(packed, ((0, 0), (0, -packed.shape[1] % 128)))
    packed = pair_sum(pair_sum(packed.reshape(2, 2, channels, -1), "u"), "v")
    packed = relocate(packed, True)
    pieces = [packed[:, starts[index] : starts[index + 1]] for index in range(len(cuts))]

    gain_grads = jnp.stack([mamba_gain_grad, first_gain_grad, attention_gain_grad, second_gain_grad])
    index = (u * 2 + c) * members + place
    gain_grads = lax.dynamic_slice_in_dim(total_small(gain_grads), index * shard, shard, 1)
    return (
        output,
        new_state,
        segment_kv,
        grad_input,
        grad_state,
        jnp.concatenate([back_keys, back_contents], axis=2).astype(F32),
        gain_grads[0],
        mamba_in_grad,
        pieces[2].T,
        pieces[3][:, 0],
        pieces[0],
        pieces[1].T,
        pieces[4][:, 0],
        pieces[5].T,
        pieces[6][:, 0],
        mamba_out_grad,
        gain_grads[1],
        first_gate_up_grad,
        first_down_grad,
        gain_grads[2],
        attention_qkv_grad,
        attention_out_grad,
        gain_grads[3],
        second_gate_up_grad,
        second_down_grad,
    )


def placements(dp, seq):
    every = dp + seq
    places = (
        P(dp, seq, None),
        P(dp, seq, None),
        P(dp, None, None),
        P(dp, seq, None),
        P(dp),
        P(every),
        P(every, None),
        P(None, every),
        P(every),
        P(every, None),
        P(None, every),
        P(every),
        P(None, every),
        P(every),
        P(every, None),
        P(every),
        P(every, None),
        P(every, None),
        P(every),
        P(every, None),
        P(every, None),
        P(every),
        P(every, None),
        P(every, None),

    )
    results = (
        P(dp, seq, None),
        P(dp, None, seq),
        P(dp, seq, None),
        P(dp, seq, None),
        P(dp, None, seq),
        P(dp, seq, None),
        P(every),
        P(every, None),
        P(None, every),
        P(every),
        P(every, None),
        P(None, every),
        P(every),
        P(None, every),
        P(every),
        P(every, None),
        P(every),
        P(every, None),
        P(every, None),
        P(every),
        P(every, None),
        P(every, None),
        P(every),
        P(every, None),
        P(every, None),

    )
    return places, results


def plane_fits(mesh):
    dp, seq = mesh.shape["dp"], mesh.shape["seq"]
    return dp == 4 and seq == 2 * dp


def solution(mesh):
    if not plane_fits(mesh):
        places, results = placements(("dp",), ("seq",))
        return jax.shard_map(
            local, mesh=mesh, in_specs=places, out_specs=results, check_vma=False
        )
    dp, seq = mesh.shape["dp"], mesh.shape["seq"]
    devices = mesh.devices.reshape(dp // 2, 2, seq // 4, 2, 2)
    places, results = placements(("u", "c"), ("y", "x", "v"))
    return jax.shard_map(
        plane_local,
        mesh=Mesh(devices, EVERY),
        in_specs=places,
        out_specs=results,
        check_vma=False,
    )
```
